32 devices in a mesh: ctx: 8 (over z, x), head: 4 (over y, core).
Axes of the slice: x: 2, y: 2, z: 4, core: 2. Of those that a mesh axis runs over, the one named last changes fastest.
Arguments:
- queries: bfloat16 [1, 2048, 2048], P(None, 'ctx', 'head'), may hold values from -128 to 128
- key_rows: bfloat16 [1, 2048, 128], P(None, ('ctx', 'head')), may hold values from -4.5 to 4.5
- value_rows: bfloat16 [1, 2048, 128], P(None, ('ctx', 'head')), may hold values from -5 to 5
- document_lengths: int32 [1, 4], replicated, may hold values from 1 to 1536, 2048 in all within a row
Outputs:
- attended: bfloat16 [1, 2048, 2048], P(None, 'ctx', 'head')
The draws below stay inside these ranges and needn't reach their ends.
All inputs are finite; a program needn't handle non-finite values.
Results may differ from the reference program's by a relative error of at most 0.0045.
Values may be sent and summed in bfloat16 or wider, within the bound.
No kernel may reach another device: no remote copies, remote signals or barrier semaphores. Data moves between devices by JAX's collectives and lax.ppermute only.
A program may use at most 64 MiB of HBM per device.

```python
import math
import jax
import jax.numpy as jnp
import numpy as np
from jax import lax

HD = 128
HEADS = 16
SEQS = 1
NDOC = 4
LEN = 2048
MOST = 1536


def shared_base(key):
    base = jax.random.normal(key, (SEQS, LEN, HD), jnp.float32)
    return jnp.clip(base, -4.5, 4.5)


def draw_key_rows(key, part):
    base = shared_base(key)
    return base.astype(jnp.bfloat16)


def draw_queries(key, part):
    key = jax.random.fold_in(key, 3)
    noise = 3.0 * jnp.clip(jax.random.normal(key, (SEQS, LEN, HEADS, HD), jnp.float32), -4.5, 4.5)
    return noise.reshape(SEQS, LEN, HEADS * HD).astype(jnp.bfloat16)


def levels(stream_key, extent, cuts, least, top_value):
    factor_of, own = 1.0, jax.random.fold_in(stream_key, 6)
    for position, blocks in cuts:
        heights = jnp.exp(jax.random.uniform(jax.random.fold_in(own, position), (blocks,), jnp.float32, least / len(cuts), top_value / len(cuts)))
        factor_of = factor_of * jnp.repeat(heights, extent[position] // blocks).reshape([-1 if axis == position else 1 for axis in range(len(extent))])
    return factor_of


def split_up(count, total, reach, slope):
    portions = [(1 << 20) // math.isqrt(grade ** slope) + 1 for grade in range(2, count + 1)]
    spare, holding = total - reach - (count - 1), [1] * (count - 1)
    while spare > 0:
        movable = [i for i in range(count - 1) if holding[i] < reach]
        pool, remaining = sum([portions[i] for i in movable]), spare
        for i in movable:
            extra = min(reach - holding[i], max(1, remaining * portions[i] // pool), spare)
            holding[i] = holding[i] + extra
            spare = spare - extra
    return np.array([reach] + holding)


def uneven_parts(rng, count, total, bound, lean):
    if count == 2:
        one = jax.random.randint(rng, (), max(1, total - bound), min(bound, total - 1) + 1)
        return jnp.stack([one, total - one])
    tallies = jnp.asarray(split_up(count, total, bound, lean), jnp.int32)
    couples = (count - 1) // 2
    donor, taker = tallies[1:1 + 2 * couples:2], tallies[2:2 + 2 * couples:2]
    room = jnp.minimum(donor - 1, bound - taker)
    passed = jax.random.randint(jax.random.fold_in(rng, 1), (couples,), 0, 1 << 20) % (room + 1)
    tallies = tallies.at[1:1 + 2 * couples:2].set(donor - passed).at[2:2 + 2 * couples:2].set(taker + passed)
    return tallies[jax.random.permutation(jax.random.fold_in(rng, 2), count)]


def scatter_about(key, shape, spread, most, shards=(), held_as=jnp.bfloat16):
    loudness = levels(key, shape, shards, -0.22, 0.18) if shards else 1.0
    result = jax.random.normal(key, shape, jnp.float32) * spread * loudness
    return jnp.minimum(jnp.maximum(result, -most), most).astype(held_as)


def setup_inputs(seed: int = 0) -> dict:
    key_of = jax.random.split(jax.random.key(seed), 5)
    queries = draw_queries(jax.random.fold_in(key_of[4], 71), 0)
    key_rows = draw_key_rows(jax.random.fold_in(key_of[4], 71), 0)
    value_rows = scatter_about(key_of[2], (SEQS, LEN, HD), 1.0, 5.0, ((1, 32),))
    document_lengths = jax.vmap(lambda own: uneven_parts(own, NDOC, LEN, MOST, 2))(jax.random.split(key_of[3], SEQS)).reshape((SEQS, NDOC)).astype(jnp.int32)
    return {"queries": queries, "key_rows": key_rows, "value_rows": value_rows, "document_lengths": document_lengths}


NEG = -1e+30

def document_ids(positions, ends):
    return lax.optimization_barrier(jnp.sum((positions[:, None] >= ends[None, :]).astype(jnp.int32), axis=1))

def reference(queries, key_rows, value_rows, document_lengths):
    scale = 1.0 / math.sqrt(HD)
    block_rows = math.gcd(LEN, 512)
    blocks = LEN // block_rows
    results = []
    for seq_index in range(SEQS):
        ends = jnp.cumsum(document_lengths[seq_index]).astype(jnp.int32)
        positions = jnp.arange(LEN, dtype=jnp.int32)
        key_docs = document_ids(positions, ends)
        keys_here = key_rows[seq_index]
        values_here = value_rows[seq_index]
        query_blocks = queries[seq_index].reshape(blocks, block_rows, HEADS, HD)
        query_blocks = query_blocks.transpose(0, 2, 1, 3).reshape(blocks * HEADS, block_rows, HD)
        starts = jnp.arange(blocks * HEADS, dtype=jnp.int32) // HEADS * block_rows

        def attend(item):
            query_block, start = item
            query_pos = start + jnp.arange(block_rows, dtype=jnp.int32)
            query_docs = document_ids(query_pos, ends)
            scores = jnp.dot(query_block, keys_here.T, preferred_element_type=jnp.float32) * scale
            valid = (positions[None, :] <= query_pos[:, None]) & (key_docs[None, :] == query_docs[:, None])
            scores = jnp.where(valid, scores, NEG)
            top = lax.optimization_barrier(jnp.max(scores, axis=1, keepdims=True))
            weights = jnp.where(valid, jnp.exp(scores - top), 0.0)
            total = lax.optimization_barrier(jnp.sum(weights, axis=1, keepdims=True))
            mixed = jnp.dot(weights.astype(jnp.bfloat16), values_here, preferred_element_type=jnp.float32)
            return (mixed / total).astype(jnp.bfloat16)
        output = lax.map(attend, (query_blocks, starts))
        output = output.reshape(blocks, HEADS, block_rows, HD).transpose(0, 2, 1, 3)
        results.append(output.reshape(LEN, HEADS * HD))
    return jnp.stack(results)
```

```python
import functools
import math

import jax
import jax.numpy as jnp
from jax import lax
from jax.experimental import pallas as pl
from jax.experimental.pallas import tpu as pltpu
from jax.sharding import PartitionSpec as P

NEG = -1e30


def attention_kernel(head_size, lengths_ref, queries_ref, kv_ref, out_ref, accum_ref):
    own = lax.axis_index("ctx")
    rows, width = queries_ref.shape
    heads = width // head_size
    pieces, _, piece_rows, _ = kv_ref.shape
    block_rows = pieces * piece_rows
    slope = math.log2(math.e) / math.sqrt(head_size)

    query_pos = own * rows + lax.broadcasted_iota(jnp.int32, (1, rows), 1)
    starts = jnp.zeros((1, rows), jnp.int32)
    first = jnp.int32(0)
    end = jnp.int32(0)
    for document in range(lengths_ref.shape[1]):
        end = end + lengths_ref[0, document]
        starts = jnp.where(query_pos >= end, end, starts)
        first = jnp.where(own * rows >= end, end, first)

    def block_step(block, state, fresh):
        kv = kv_ref[:, pl.ds(block, 1)].reshape(block_rows, 2 * head_size)
        keys, values = kv[:, :head_size], kv[:, head_size:]
        key_pos = block * block_rows + lax.broadcasted_iota(jnp.int32, (block_rows, rows), 0)
        valid = (key_pos >= starts) & (key_pos <= query_pos)
        new_state = []
        for head in range(heads):
            query = queries_ref[:, head * head_size : (head + 1) * head_size]
            scores = lax.dot_general(keys, query, (((1,), (1,)), ((), ())), preferred_element_type=jnp.float32)
            scores = jnp.where(valid, scores, NEG)
            block_top = jnp.max(scores, axis=0, keepdims=True)
            if fresh:
                top = block_top
            else:
                top = jnp.maximum(state[2 * head], block_top)
            weights = jnp.exp2((scores - top) * slope)
            total = jnp.sum(weights, axis=0, keepdims=True)
            mixed = lax.dot_general(
                values, weights.astype(jnp.bfloat16), (((0,), (0,)), ((), ())), preferred_element_type=jnp.float32
            )
            if fresh:
                accum_ref[head] = mixed
            else:
                factor = jnp.exp2((state[2 * head] - top) * slope)
                total = state[2 * head + 1] * factor + total
                accum_ref[head] = accum_ref[head] * factor + mixed
            new_state += [top, total]
        return tuple(new_state)

    state = block_step(own, None, True)
    state = lax.fori_loop(
        first // block_rows, own, lambda block, inner: block_step(block, inner, False), state
    )
    for head in range(heads):
        mixed = accum_ref[head] / state[2 * head + 1]
        out_ref[:, head * head_size : (head + 1) * head_size] = mixed.T.astype(out_ref.dtype)


def attend(queries, kv, lengths, head_size):
    rows, width = queries.shape
    heads = width // head_size
    keys = kv.shape[0] * kv.shape[1] * kv.shape[2]
    whole = pl.BlockSpec(memory_space=pltpu.VMEM)
    return pl.pallas_call(
        functools.partial(attention_kernel, head_size),
        out_shape=jax.ShapeDtypeStruct((rows, width), queries.dtype),
        in_specs=[pl.BlockSpec(memory_space=pltpu.SMEM), whole, whole],
        out_specs=whole,
        scratch_shapes=[pltpu.VMEM((heads, head_size, rows), jnp.float32)],
        compiler_params=pltpu.CompilerParams(vmem_limit_bytes=48 * 1024 * 1024),
        cost_estimate=pl.CostEstimate(
            flops=4 * rows * width * keys, bytes_accessed=4 * rows * width + 4 * keys * head_size,
            transcendentals=rows * heads * keys,
        ),
    )(lengths, queries, kv)


def body(queries, key_rows, value_rows, document_lengths):
    seqs, rows, width = queries.shape
    piece_rows, head_size = key_rows.shape[1:]
    results = []
    for seq in range(seqs):
        kv = jnp.concatenate([key_rows[seq], value_rows[seq]], axis=1)
        kv = lax.all_gather(kv, "ctx", axis=0)
        kv = lax.all_gather(kv, "head", axis=0)
        lengths = document_lengths[seq : seq + 1]
        results.append(attend(queries[seq], kv, lengths, head_size))
    return jnp.stack(results)


def solution(mesh):
    in_specs = (
        P(None, "ctx", "head"),
        P(None, ("ctx", "head"), None),
        P(None, ("ctx", "head"), None),
        P(),
    )
    out_specs = P(None, "ctx", "head")
    return jax.shard_map(body, mesh=mesh, in_specs=in_specs, out_specs=out_specs, check_vma=False)
```

```python
import functools
import math

import jax
import jax.numpy as jnp
from jax import lax
from jax.experimental import pallas as pl
from jax.experimental.pallas import tpu as pltpu
from jax.sharding import PartitionSpec as P

NEG = -1e30


def attention_kernel(head_size, lengths_ref, queries_ref, *refs):
    *kv_refs, out_ref, accum_ref = refs
    own, piece = lax.axis_index("ctx"), lax.axis_index("head")
    rows, width = queries_ref.shape
    heads = width // head_size
    pieces = len(kv_refs)
    piece_rows = kv_refs[0].shape[1]
    block_rows = pieces * piece_rows
    slope = math.log2(math.e) / math.sqrt(head_size)

    query_pos = own * rows + lax.broadcasted_iota(jnp.int32, (1, rows), 1)
    starts = jnp.zeros((1, rows), jnp.int32)
    first = jnp.int32(0)
    end = jnp.int32(0)
    for document in range(lengths_ref.shape[1]):
        end = end + lengths_ref[0, document]
        starts = jnp.where(query_pos >= end, end, starts)
        first = jnp.where(own * rows >= end, end, first)
    in_piece = lax.broadcasted_iota(jnp.int32, (piece_rows, rows), 0)
    in_block = jnp.concatenate([in_piece + lax.rem(piece + pieces - i, pieces) * piece_rows for i in range(pieces)], axis=0)

    def block_step(back, state, fresh):
        kv = jnp.concatenate([kv_ref[back] for kv_ref in kv_refs], axis=0)
        keys, values = kv[:, :head_size], kv[:, head_size:]
        key_pos = (own - back) * block_rows + in_block
        valid = (key_pos >= starts) & (key_pos <= query_pos)
        new_state = []
        for head in range(heads):
            query = queries_ref[:, head * head_size : (head + 1) * head_size]
            scores = lax.dot_general(keys, query, (((1,), (1,)), ((), ())), preferred_element_type=jnp.float32)
            scores = jnp.where(valid, scores, NEG)
            block_top = jnp.max(scores, axis=0, keepdims=True)
            if fresh:
                top = block_top
            else:
                top = jnp.maximum(state[2 * head], block_top)
            weights = jnp.exp2((scores - top) * slope)
            total = jnp.sum(weights, axis=0, keepdims=True)
            mixed = lax.dot_general(
                values, weights.astype(jnp.bfloat16), (((0,), (0,)), ((), ())), preferred_element_type=jnp.float32
            )
            if fresh:
                accum_ref[head] = mixed
            else:
                factor = jnp.exp2((state[2 * head] - top) * slope)
                total = state[2 * head + 1] * factor + total
                accum_ref[head] = accum_ref[head] * factor + mixed
            new_state += [top, total]
        return tuple(new_state)

    state = block_step(0, None, True)
    state = lax.fori_loop(
        1, own - first // block_rows + 1, lambda back, inner: block_step(back, inner, False), state
    )
    for head in range(heads):
        mixed = accum_ref[head] / state[2 * head + 1]
        out_ref[:, head * head_size : (head + 1) * head_size] = mixed.T.astype(out_ref.dtype)


def attend(queries, kvs, lengths, head_size):
    rows, width = queries.shape
    heads = width // head_size
    keys = sum(kv.shape[0] * kv.shape[1] for kv in kvs)
    whole = pl.BlockSpec(memory_space=pltpu.VMEM)
    return pl.pallas_call(
        functools.partial(attention_kernel, head_size),
        out_shape=jax.ShapeDtypeStruct((rows, width), queries.dtype),
        in_specs=[pl.BlockSpec(memory_space=pltpu.SMEM)] + [whole] * (1 + len(kvs)),
        out_specs=whole,
        scratch_shapes=[pltpu.VMEM((heads, head_size, rows), jnp.float32)],
        compiler_params=pltpu.CompilerParams(vmem_limit_bytes=48 * 1024 * 1024),
        cost_estimate=pl.CostEstimate(
            flops=4 * rows * width * keys, bytes_accessed=4 * rows * width + 4 * keys * head_size,
            transcendentals=rows * heads * keys,
        ),
    )(lengths, queries, *kvs)


RADIX = 8


def earlier_blocks(block, axis):
    size = lax.axis_size(axis)
    held = block[None]
    while held.shape[0] < size:
        count = held.shape[0]
        moved = [held]
        for step in range(1, RADIX):
            shift = step * count
            if shift < size:
                moved.append(lax.ppermute(held, axis, [(i, i + shift) for i in range(size - shift)]))
        held = jnp.concatenate(moved, axis=0)
    return held[:size]


def body(queries, key_rows, value_rows, document_lengths):
    seqs, rows, width = queries.shape
    piece_rows, head_size = key_rows.shape[1:]
    pieces = lax.axis_size("head")
    results = []
    for seq in range(seqs):
        kv = jnp.concatenate([key_rows[seq], value_rows[seq]], axis=1)
        kv = earlier_blocks(kv, "ctx")
        kvs = [kv]
        for shift in range(1, pieces):
            kvs.append(lax.ppermute(kv, "head", [(i, (i + shift) % pieces) for i in range(pieces)]))
        lengths = document_lengths[seq : seq + 1]
        results.append(attend(queries[seq], kvs, lengths, head_size))
    return jnp.stack(results)


def solution(mesh):
    in_specs = (
        P(None, "ctx", "head"),
        P(None, ("ctx", "head"), None),
        P(None, ("ctx", "head"), None),
        P(),
    )
    out_specs = P(None, "ctx", "head")
    return jax.shard_map(body, mesh=mesh, in_specs=in_specs, out_specs=out_specs, check_vma=False)
```

```python
import functools
import math

import jax
import jax.numpy as jnp
from jax import lax
from jax.experimental import pallas as pl
from jax.experimental.pallas import tpu as pltpu
from jax.sharding import PartitionSpec as P

NEG = -1e30


def attention_kernel(head_size, order, lengths_ref, queries_ref, *refs):
    *kv_refs, out_ref, accum_ref = refs
    own, piece = lax.axis_index("ctx"), lax.axis_index("head")
    rows, width = queries_ref.shape
    heads = width // head_size
    piece_rows = kv_refs[0].shape[2]
    block_rows = len(order) * piece_rows
    slope = math.log2(math.e) / math.sqrt(head_size)

    query_pos = own * rows + lax.broadcasted_iota(jnp.int32, (1, rows), 1)
    starts = jnp.zeros((1, rows), jnp.int32)
    first = jnp.int32(0)
    end = jnp.int32(0)
    for document in range(lengths_ref.shape[1]):
        end = end + lengths_ref[0, document]
        starts = jnp.where(query_pos >= end, end, starts)
        first = jnp.where(own * rows >= end, end, first)
    in_piece = lax.broadcasted_iota(jnp.int32, (piece_rows, rows), 0)
    in_block = jnp.concatenate([in_piece + (piece ^ i) * piece_rows for i in order], axis=0)

    def block_step(block, state, fresh):
        kv = jnp.concatenate([kv_ref[i, block] for kv_ref in kv_refs for i in range(kv_ref.shape[0])], axis=0)
        keys, values = kv[:, :head_size], kv[:, head_size:]
        key_pos = block * block_rows + in_block
        valid = (key_pos >= starts) & (key_pos <= query_pos)
        new_state = []
        for head in range(heads):
            query = queries_ref[:, head * head_size : (head + 1) * head_size]
            scores = lax.dot_general(keys, query, (((1,), (1,)), ((), ())), preferred_element_type=jnp.float32)
            scores = jnp.where(valid, scores, NEG)
            block_top = jnp.max(scores, axis=0, keepdims=True)
            if fresh:
                top = block_top
            else:
                top = jnp.maximum(state[2 * head], block_top)
            weights = jnp.exp2((scores - top) * slope)
            total = jnp.sum(weights, axis=0, keepdims=True)
            mixed = lax.dot_general(
                values, weights.astype(jnp.bfloat16), (((0,), (0,)), ((), ())), preferred_element_type=jnp.float32
            )
            if fresh:
                accum_ref[head] = mixed
            else:
                factor = jnp.exp2((state[2 * head] - top) * slope)
                total = state[2 * head + 1] * factor + total
                accum_ref[head] = accum_ref[head] * factor + mixed
            new_state += [top, total]
        return tuple(new_state)

    state = block_step(own, None, True)
    state = lax.fori_loop(
        first // block_rows, own, lambda block, inner: block_step(block, inner, False), state
    )
    for head in range(heads):
        mixed = accum_ref[head] / state[2 * head + 1]
        out_ref[:, head * head_size : (head + 1) * head_size] = mixed.T.astype(out_ref.dtype)


def attend(queries, kvs, order, lengths, head_size):
    rows, width = queries.shape
    heads = width // head_size
    keys = sum(math.prod(kv.shape[:3]) for kv in kvs)
    whole = pl.BlockSpec(memory_space=pltpu.VMEM)
    return pl.pallas_call(
        functools.partial(attention_kernel, head_size, order),
        out_shape=jax.ShapeDtypeStruct((rows, width), queries.dtype),
        in_specs=[pl.BlockSpec(memory_space=pltpu.SMEM)] + [whole] * (1 + len(kvs)),
        out_specs=whole,
        scratch_shapes=[pltpu.VMEM((heads, head_size, rows), jnp.float32)],
        compiler_params=pltpu.CompilerParams(vmem_limit_bytes=48 * 1024 * 1024),
        cost_estimate=pl.CostEstimate(
            flops=4 * rows * width * keys, bytes_accessed=4 * rows * width + 4 * keys * head_size,
            transcendentals=rows * heads * keys,
        ),
    )(lengths, queries, *kvs)


def all_blocks(block, axis):
    size = lax.axis_size(axis)
    return lax.all_to_all(jnp.broadcast_to(block, (size,) + block.shape), axis, 0, 0)


def exchanged(piece, axis):
    size = lax.axis_size(axis)
    held, order = [piece[None]], [0]
    bit = size // 2
    while bit:
        held.append(lax.ppermute(jnp.concatenate(held), axis, [(i, i ^ bit) for i in range(size)]))
        order = order + [i ^ bit for i in order]
        bit //= 2
    return held, order


def body(queries, key_rows, value_rows, document_lengths):
    seqs, rows, width = queries.shape
    piece_rows, head_size = key_rows.shape[1:]
    results = []
    for seq in range(seqs):
        kv = jnp.concatenate([key_rows[seq], value_rows[seq]], axis=1)
        kvs, order = exchanged(all_blocks(kv, "ctx"), "head")
        lengths = document_lengths[seq : seq + 1]
        results.append(attend(queries[seq], kvs, order, lengths, head_size))
    return jnp.stack(results)


def solution(mesh):
    in_specs = (
        P(None, "ctx", "head"),
        P(None, ("ctx", "head"), None),
        P(None, ("ctx", "head"), None),
        P(),
    )
    out_specs = P(None, "ctx", "head")
    return jax.shard_map(body, mesh=mesh, in_specs=in_specs, out_specs=out_specs, check_vma=False)
```

```python
import functools
import math

import jax
import jax.numpy as jnp
from jax import lax
from jax.experimental import pallas as pl
from jax.experimental.pallas import tpu as pltpu
from jax.sharding import PartitionSpec as P

NEG = -1e30


def attention_kernel(head_size, order, lengths_ref, queries_ref, *refs):
    *kv_refs, out_ref, accum_ref = refs
    own, piece = lax.axis_index("ctx"), lax.axis_index("head")
    rows, width = queries_ref.shape
    heads = width // head_size
    blocks, piece_rows, _ = kv_refs[0].shape
    block_rows = len(order) * piece_rows
    slope = math.log2(math.e) / math.sqrt(head_size)

    query_pos = own * rows + lax.broadcasted_iota(jnp.int32, (1, rows), 1)
    starts = jnp.zeros((1, rows), jnp.int32)
    first = jnp.int32(0)
    end = jnp.int32(0)
    for document in range(lengths_ref.shape[1]):
        end = end + lengths_ref[0, document]
        starts = jnp.where(query_pos >= end, end, starts)
        first = jnp.where(own * rows >= end, end, first)
    in_piece = lax.broadcasted_iota(jnp.int32, (piece_rows, rows), 0)
    in_block = jnp.concatenate([in_piece + (piece ^ i) * piece_rows for i in order], axis=0)

    def block_step(block, state, fresh):
        entry = reversed_bits(own ^ block, blocks)
        kv = jnp.concatenate([kv_ref[entry] for kv_ref in kv_refs], axis=0)
        keys, values = kv[:, :head_size], kv[:, head_size:]
        key_pos = block * block_rows + in_block
        valid = (key_pos >= starts) & (key_pos <= query_pos)
        new_state = []
        for head in range(heads):
            query = queries_ref[:, head * head_size : (head + 1) * head_size]
            scores = lax.dot_general(keys, query, (((1,), (1,)), ((), ())), preferred_element_type=jnp.float32)
            scores = jnp.where(valid, scores, NEG)
            block_top = jnp.max(scores, axis=0, keepdims=True)
            if fresh:
                top = block_top
            else:
                top = jnp.maximum(state[2 * head], block_top)
            weights = jnp.exp2((scores - top) * slope)
            total = jnp.sum(weights, axis=0, keepdims=True)
            mixed = lax.dot_general(
                values, weights.astype(jnp.bfloat16), (((0,), (0,)), ((), ())), preferred_element_type=jnp.float32
            )
            if fresh:
                accum_ref[head] = mixed
            else:
                factor = jnp.exp2((state[2 * head] - top) * slope)
                total = state[2 * head + 1] * factor + total
                accum_ref[head] = accum_ref[head] * factor + mixed
            new_state += [top, total]
        return tuple(new_state)

    state = block_step(own, None, True)
    state = lax.fori_loop(
        first // block_rows, own, lambda block, inner: block_step(block, inner, False), state
    )
    for head in range(heads):
        mixed = accum_ref[head] / state[2 * head + 1]
        out_ref[:, head * head_size : (head + 1) * head_size] = mixed.T.astype(out_ref.dtype)


def attend(queries, kvs, order, lengths, head_size):
    rows, width = queries.shape
    heads = width // head_size
    keys = sum(math.prod(kv.shape[:2]) for kv in kvs)
    whole = pl.BlockSpec(memory_space=pltpu.VMEM)
    return pl.pallas_call(
        functools.partial(attention_kernel, head_size, order),
        out_shape=jax.ShapeDtypeStruct((rows, width), queries.dtype),
        in_specs=[pl.BlockSpec(memory_space=pltpu.SMEM)] + [whole] * (1 + len(kvs)),
        out_specs=whole,
        scratch_shapes=[pltpu.VMEM((heads, head_size, rows), jnp.float32)],
        compiler_params=pltpu.CompilerParams(vmem_limit_bytes=48 * 1024 * 1024),
        cost_estimate=pl.CostEstimate(
            flops=4 * rows * width * keys, bytes_accessed=4 * rows * width + 4 * keys * head_size,
            transcendentals=rows * heads * keys,
        ),
    )(lengths, queries, *kvs)


def exchange(held, axis, bit):
    return lax.ppermute(held, axis, [(i, i ^ bit) for i in range(lax.axis_size(axis))])


def all_blocks(block, axis):
    held = block[None]
    bit = lax.axis_size(axis) // 2
    while bit:
        held = jnp.concatenate([held, exchange(held, axis, bit)])
        bit //= 2
    return held


def all_pieces(piece, axis):
    held = {0: piece}
    bit = lax.axis_size(axis) // 2
    while bit:
        held |= {i ^ bit: exchange(held[i], axis, bit) for i in held}
        bit //= 2
    return held


def reversed_bits(index, size):
    result, bit = 0, 1
    while bit < size:
        result = result * 2 + (index // bit) % 2
        bit *= 2
    return result


def body(queries, key_rows, value_rows, document_lengths):
    seqs, rows, width = queries.shape
    piece_rows, head_size = key_rows.shape[1:]
    results = []
    for seq in range(seqs):
        kv = jnp.concatenate([key_rows[seq], value_rows[seq]], axis=1)
        kvs = all_pieces(all_blocks(kv, "ctx"), "head")
        lengths = document_lengths[seq : seq + 1]
        results.append(attend(queries[seq], list(kvs.values()), list(kvs), lengths, head_size))
    return jnp.stack(results)


def solution(mesh):
    in_specs = (
        P(None, "ctx", "head"),
        P(None, ("ctx", "head"), None),
        P(None, ("ctx", "head"), None),
        P(),
    )
    out_specs = P(None, "ctx", "head")
    return jax.shard_map(body, mesh=mesh, in_specs=in_specs, out_specs=out_specs, check_vma=False)
```

```python
import functools
import math

import jax
import jax.numpy as jnp
from jax import lax
from jax.experimental import pallas as pl
from jax.experimental.pallas import tpu as pltpu
from jax.sharding import PartitionSpec as P

NEG = -1e30
STEP_BLOCKS = 8


def attention_kernel(head_size, place, first, last, lengths_ref, queries_ref, kv_ref, *refs):
    if first:
        old_stats_ref = old_sums_ref = None
    else:
        old_stats_ref, old_sums_ref, *refs = refs
    if last:
        out_ref, stats_ref, sums_ref = refs
    elif first:
        stats_ref, sums_ref, turned_ref = refs
    else:
        stats_ref, sums_ref = refs
    own, piece = lax.axis_index("ctx"), lax.axis_index("head") ^ place
    heads, _, rows = sums_ref.shape
    blocks, piece_rows, _ = kv_ref.shape
    slope = math.log2(math.e) / math.sqrt(head_size)
    step_blocks = math.gcd(blocks, STEP_BLOCKS)
    keys_a_step = step_blocks * piece_rows

    query_pos = own * rows + lax.broadcasted_iota(jnp.int32, (1, rows), 1)
    starts = jnp.zeros((1, rows), jnp.int32)
    first_key = jnp.int32(0)
    end = jnp.int32(0)
    for document in range(lengths_ref.shape[1]):
        end = end + lengths_ref[0, document]
        starts = jnp.where(query_pos >= end, end, starts)
        first_key = jnp.where(own * rows >= end, end, first_key)

    if first:
        for head in range(heads):
            turned_ref[head] = queries_ref[:, head * head_size : (head + 1) * head_size].T
        queries_ref = turned_ref
    in_block = piece * piece_rows + lax.broadcasted_iota(jnp.int32, (piece_rows, rows), 0)

    def step(start, old):
        kv = kv_ref[pl.ds(start, step_blocks)].reshape(keys_a_step, 2 * head_size)
        keys, values = kv[:, :head_size], kv[:, head_size:].T
        key_pos = jnp.concatenate([(start + i) * rows + in_block for i in range(step_blocks)], axis=0)
        valid = (key_pos >= starts) & (key_pos <= query_pos)
        scores = [
            jnp.where(valid, jnp.dot(keys, queries_ref[head], preferred_element_type=jnp.float32), NEG)
            for head in range(heads)
        ]
        tops, totals, sums = [], [], []
        for head in range(heads):
            top = jnp.max(scores[head], axis=0, keepdims=True)
            if old is not None:
                top = jnp.maximum(old[0][head], top)
            weights = jnp.exp2((scores[head] - top) * slope)
            total = jnp.sum(weights, axis=0, keepdims=True)
            mixed = jnp.dot(values, weights.astype(jnp.bfloat16), preferred_element_type=jnp.float32)
            if old is not None:
                factor = jnp.exp2((old[0][head] - top) * slope)
                total = old[1][head] * factor + total
                mixed = old[2][head] * factor + mixed
            tops.append(top)
            totals.append(total)
            sums.append(mixed)
        return tops, totals, sums

    def load(stats, sums):
        return (
            [stats[head : head + 1] for head in range(heads)],
            [stats[heads + head : heads + head + 1] for head in range(heads)],
            [sums[head] for head in range(heads)],
        )

    def store(state):
        tops, totals, sums = state
        stats_ref[...] = jnp.concatenate(tops + totals, axis=0)
        for head in range(heads):
            sums_ref[head] = sums[head]

    if blocks == step_blocks:
        state = step(0, None if first else load(old_stats_ref[...], old_sums_ref))
        if not last:
            store(state)
    else:
        if first:
            stats_ref[...] = jnp.concatenate([jnp.full((heads, rows), NEG), jnp.zeros((heads, rows))], axis=0)
            sums_ref[...] = jnp.zeros_like(sums_ref)
        else:
            stats_ref[...] = old_stats_ref[...]
            sums_ref[...] = old_sums_ref[...]

        @pl.loop(first_key // rows // step_blocks, own // step_blocks + 1)
        def _(index):
            store(step(index * step_blocks, load(stats_ref[...], sums_ref)))

        state = load(stats_ref[...], sums_ref)
    if last:
        _, totals, sums = state
        for head in range(heads):
            out_ref[:, head * head_size : (head + 1) * head_size] = (sums[head] / totals[head]).T.astype(out_ref.dtype)


def attend(place, first, last, lengths, queries, kv, state, heads):
    head_size = kv.shape[2] // 2
    rows = queries.shape[0] if first else queries.shape[2]
    keys = kv.shape[0] * kv.shape[1]
    stats = jax.ShapeDtypeStruct((2 * heads, rows), jnp.float32)
    sums = jax.ShapeDtypeStruct((heads, head_size, rows), jnp.float32)
    turned = jax.ShapeDtypeStruct((heads, head_size, rows), queries.dtype)
    whole = pl.BlockSpec(memory_space=pltpu.VMEM)
    scratch = []
    if last:
        out_shape = jax.ShapeDtypeStruct((rows, heads * head_size), queries.dtype)
        scratch = [pltpu.VMEM(stats.shape, stats.dtype), pltpu.VMEM(sums.shape, sums.dtype)]
    elif first:
        out_shape = (stats, sums, turned)
    else:
        out_shape = (stats, sums)
    return pl.pallas_call(
        functools.partial(attention_kernel, head_size, place, first, last),
        out_shape=out_shape,
        in_specs=[pl.BlockSpec(memory_space=pltpu.SMEM)] + [whole] * (2 + len(state)),
        out_specs=jax.tree.map(lambda _: whole, out_shape),
        scratch_shapes=scratch,
        compiler_params=pltpu.CompilerParams(vmem_limit_bytes=32 * 1024 * 1024),
        cost_estimate=pl.CostEstimate(
            flops=4 * rows * heads * head_size * keys,
            bytes_accessed=4 * keys * head_size + 16 * rows * heads * head_size,
            transcendentals=rows * heads * keys,
        ),
    )(lengths, queries, kv, *state)


def all_blocks(block, axis):
    size = lax.axis_size(axis)
    return lax.all_to_all(jnp.broadcast_to(block, (size,) + block.shape), axis, 0, 0)


def exchange(piece, axis, bit):
    return lax.ppermute(piece, axis, [(i, i ^ bit) for i in range(lax.axis_size(axis))])


def body(queries, key_rows, value_rows, document_lengths):
    seqs, rows, width = queries.shape
    heads = width // key_rows.shape[2]
    places = lax.axis_size("head")
    assert places in (1, 2, 4)
    results = []
    for seq in range(seqs):
        kv = jnp.concatenate([key_rows[seq], value_rows[seq]], axis=1)
        lengths = document_lengths[seq : seq + 1]
        state, turned = (), queries[seq]
        near = {0: all_blocks(kv, "ctx")}
        bit, left = 2, places
        while near:
            far = {place ^ bit: exchange(piece, "head", bit) for place, piece in near.items() if bit < places}
            near |= {place ^ 1: exchange(piece, "head", 1) for place, piece in near.items() if places > 1}
            for place, piece in near.items():
                first, last = left == places, left == 1
                result = attend(place, first, last, lengths, turned, piece, state, heads)
                left -= 1
                if last:
                    results.append(result)
                elif first:
                    *state, turned = result
                else:
                    state = result
            if far:
                far, state = lax.optimization_barrier((far, state))
            near = far
            bit *= 2
    return jnp.stack(results)


def solution(mesh):
    in_specs = (
        P(None, "ctx", "head"),
        P(None, ("ctx", "head"), None),
        P(None, ("ctx", "head"), None),
        P(),
    )
    out_specs = P(None, "ctx", "head")
    return jax.shard_map(body, mesh=mesh, in_specs=in_specs, out_specs=out_specs, check_vma=False)
```

```python
import functools
import math

import jax
import jax.numpy as jnp
from jax import lax
from jax.experimental import pallas as pl
from jax.experimental.pallas import tpu as pltpu
from jax.sharding import PartitionSpec as P

NEG = -1e30
DIGIT = 8


def attention_kernel(head_size, parts, step_blocks, first, last, lengths_ref, queries_ref, *refs):
    kv_refs, refs = refs[: len(parts)], refs[len(parts) :]
    if first:
        stats_ref, sums_ref, turned_ref = refs
        old_stats_ref, old_sums_ref = stats_ref, sums_ref
    elif last:
        old_stats_ref, old_sums_ref, out_ref = refs
    else:
        old_stats_ref, old_sums_ref, stats_ref, sums_ref = refs
    own = lax.axis_index("ctx")
    heads, _, rows = old_sums_ref.shape
    entries, piece_rows, _ = kv_refs[0].shape
    slope = math.log2(math.e) / math.sqrt(head_size)

    query_pos = own * rows + lax.broadcasted_iota(jnp.int32, (1, rows), 1)
    starts = jnp.zeros((1, rows), jnp.int32)
    first_key = jnp.int32(0)
    end = jnp.int32(0)
    for document in range(lengths_ref.shape[1]):
        end = end + lengths_ref[0, document]
        starts = jnp.where(query_pos >= end, end, starts)
        first_key = jnp.where(own * rows >= end, end, first_key)

    if first:
        for head in range(heads):
            turned_ref[head] = queries_ref[:, head * head_size : (head + 1) * head_size].T
        queries_ref = turned_ref
    in_piece = lax.broadcasted_iota(jnp.int32, (piece_rows, rows), 0)

    def step(index, old):
        kv, key_pos = [], []
        for kv_ref, (place, start) in zip(kv_refs, parts):
            in_block = (lax.axis_index("head") ^ place) * piece_rows + in_piece
            kv.append(kv_ref[pl.ds(index * step_blocks, step_blocks)].reshape(step_blocks * piece_rows, 2 * head_size))
            key_pos += [(own ^ (start + index * step_blocks + i)) * rows + in_block for i in range(step_blocks)]
        kv = jnp.concatenate(kv, axis=0)
        key_pos = jnp.concatenate(key_pos, axis=0)
        keys, values = kv[:, :head_size], kv[:, head_size:].T
        valid = (key_pos >= starts) & (key_pos <= query_pos)
        scores = [
            jnp.where(valid, jnp.dot(keys, queries_ref[head], preferred_element_type=jnp.float32), NEG)
            for head in range(heads)
        ]
        tops, totals, sums = [], [], []
        for head in range(heads):
            top = jnp.max(scores[head], axis=0, keepdims=True)
            if old is not None:
                top = jnp.maximum(old[0][head], top)
            weights = jnp.exp2((scores[head] - top) * slope)
            total = jnp.sum(weights, axis=0, keepdims=True)
            mixed = jnp.dot(values, weights.astype(jnp.bfloat16), preferred_element_type=jnp.float32)
            if old is not None:
                factor = jnp.exp2((old[0][head] - top) * slope)
                total = old[1][head] * factor + total
                mixed = old[2][head] * factor + mixed
            tops.append(top)
            totals.append(total)
            sums.append(mixed)
        return tops, totals, sums

    def load(stats, sums):
        return (
            [stats[head : head + 1] for head in range(heads)],
            [stats[heads + head : heads + head + 1] for head in range(heads)],
            [sums[head] for head in range(heads)],
        )

    def store(state):
        tops, totals, sums = state
        if last:
            for head in range(heads):
                result = (sums[head] * (1.0 / totals[head])).astype(out_ref.dtype)
                out_ref[:, head * head_size : (head + 1) * head_size] = result.T
        else:
            stats_ref[...] = jnp.concatenate(tops + totals, axis=0)
            for head in range(heads):
                sums_ref[head] = sums[head]

    def needed(index):
        group = (own ^ (parts[0][1] + index * step_blocks)) // step_blocks
        return (group <= own // step_blocks) & (group >= first_key // rows // step_blocks)

    def step_or_skip(index, state):
        return lax.cond(needed(index), lambda: step(index, state), lambda: state)

    steps = entries // step_blocks
    if first:
        state = step(0, None)
    else:
        state = load(old_stats_ref[...], old_sums_ref)
        state = step_or_skip(0, state)
    if steps == 2:
        state = step_or_skip(1, state)
    elif steps > 2:
        state = lax.fori_loop(1, steps, step_or_skip, state)
    store(state)


def attend(parts, step_blocks, first, last, lengths, queries, kvs, state, heads):
    head_size = kvs[0].shape[2] // 2
    rows = queries.shape[0] if first else queries.shape[2]
    keys = sum(kv.shape[0] * kv.shape[1] for kv in kvs)
    stats = jax.ShapeDtypeStruct((2 * heads, rows), jnp.float32)
    sums = jax.ShapeDtypeStruct((heads, head_size, rows), jnp.float32)
    turned = jax.ShapeDtypeStruct((heads, head_size, rows), queries.dtype)
    whole = pl.BlockSpec(memory_space=pltpu.VMEM)
    if last:
        out_shape = jax.ShapeDtypeStruct((rows, heads * head_size), queries.dtype)
    elif first:
        out_shape = (stats, sums, turned)
    else:
        out_shape = (stats, sums)
    return pl.pallas_call(
        functools.partial(attention_kernel, head_size, parts, step_blocks, first, last),
        out_shape=out_shape,
        in_specs=[pl.BlockSpec(memory_space=pltpu.SMEM)] + [whole] * (1 + len(kvs) + len(state)),
        out_specs=jax.tree.map(lambda _: whole, out_shape),
        compiler_params=pltpu.CompilerParams(vmem_limit_bytes=32 * 1024 * 1024),
        cost_estimate=pl.CostEstimate(
            flops=4 * rows * heads * head_size * keys,
            bytes_accessed=4 * keys * head_size + 16 * rows * heads * head_size,
            transcendentals=rows * heads * keys,
        ),
    )(lengths, queries, *kvs, *state)


def exchange(piece, axis, bits):
    return lax.ppermute(piece, axis, [(i, i ^ bits) for i in range(lax.axis_size(axis))])


def all_blocks(block, axis):
    held = block[None]
    while (count := held.shape[0]) < lax.axis_size(axis):
        held = jnp.concatenate([held] + [exchange(held, axis, digit * count) for digit in range(1, DIGIT)])
    return held


def body(queries, key_rows, value_rows, document_lengths):
    seqs, rows, width = queries.shape
    heads = width // key_rows.shape[2]
    assert lax.axis_size("head") == 4
    results = []
    for seq in range(seqs):
        lengths = document_lengths[seq : seq + 1]
        piece_0 = all_blocks(jnp.concatenate([key_rows[seq], value_rows[seq]], axis=1), "ctx")
        whole, half = DIGIT, DIGIT // 2
        piece_2 = exchange(piece_0, "head", 2)
        piece_1 = exchange(piece_0, "head", 1)
        *state, turned = attend([(0, 0)], whole, True, False, lengths, queries[seq], [piece_0], (), heads)
        state = attend([(1, 0)], whole, False, False, lengths, turned, [piece_1], state, heads)
        piece_2, state = lax.optimization_barrier((piece_2, state))
        piece_3 = exchange(piece_2, "head", 1)
        state = attend([(2, 0)], whole, False, False, lengths, turned, [piece_2], state, heads)
        results.append(attend([(3, 0)], half, False, True, lengths, turned, [piece_3], state, heads))
    return jnp.stack(results)


def solution(mesh):
    in_specs = (
        P(None, "ctx", "head"),
        P(None, ("ctx", "head"), None),
        P(None, ("ctx", "head"), None),
        P(),
    )
    out_specs = P(None, "ctx", "head")
    return jax.shard_map(body, mesh=mesh, in_specs=in_specs, out_specs=out_specs, check_vma=False)
```

```python
import functools
import math

import jax
import jax.numpy as jnp
from jax import lax
from jax.experimental import pallas as pl
from jax.experimental.pallas import tpu as pltpu
from jax.sharding import PartitionSpec as P

NEG = -1e30
STEP_BLOCKS = 8


def attention_kernel(head_size, parts, step_blocks, first, last, lengths_ref, queries_ref, *refs):
    kv_refs, refs = refs[: len(parts)], refs[len(parts) :]
    if first:
        stats_ref, sums_ref, turned_ref = refs
        old_stats_ref, old_sums_ref = stats_ref, sums_ref
    elif last:
        old_stats_ref, old_sums_ref, out_ref = refs
    else:
        old_stats_ref, old_sums_ref, stats_ref, sums_ref = refs
    own = lax.axis_index("ctx")
    heads, _, rows = old_sums_ref.shape
    entries, piece_rows, _ = kv_refs[0].shape
    slope = math.log2(math.e) / math.sqrt(head_size)

    query_pos = own * rows + lax.broadcasted_iota(jnp.int32, (1, rows), 1)
    starts = jnp.zeros((1, rows), jnp.int32)
    first_key = jnp.int32(0)
    end = jnp.int32(0)
    for document in range(lengths_ref.shape[1]):
        end = end + lengths_ref[0, document]
        starts = jnp.where(query_pos >= end, end, starts)
        first_key = jnp.where(own * rows >= end, end, first_key)

    if first:
        for head in range(heads):
            turned_ref[head] = queries_ref[:, head * head_size : (head + 1) * head_size].T
        queries_ref = turned_ref
    in_piece = lax.broadcasted_iota(jnp.int32, (piece_rows, rows), 0)

    def step(index, old):
        kv, key_pos = [], []
        for kv_ref, (place, start) in zip(kv_refs, parts):
            in_block = (lax.axis_index("head") ^ place) * piece_rows + in_piece
            kv.append(kv_ref[pl.ds(index * step_blocks, step_blocks)].reshape(step_blocks * piece_rows, 2 * head_size))
            key_pos += [(start + index * step_blocks + i) * rows + in_block for i in range(step_blocks)]
        kv = jnp.concatenate(kv, axis=0)
        key_pos = jnp.concatenate(key_pos, axis=0)
        keys, values = kv[:, :head_size], kv[:, head_size:].T
        bias = jnp.where((key_pos >= starts) & (key_pos <= query_pos), 0.0, NEG)

        def scores_of(head):
            return jnp.dot(keys, queries_ref[head], preferred_element_type=jnp.float32) + bias

        tops, totals, sums = [], [], []
        ahead = scores_of(0)
        for head in range(heads):
            scores = ahead
            if head + 1 < heads:
                ahead = scores_of(head + 1)
            top = jnp.max(scores, axis=0, keepdims=True)
            if old is not None:
                top = jnp.maximum(old[0][head], top)
            weights = jnp.exp2((scores - top) * slope)
            total = jnp.sum(weights, axis=0, keepdims=True)
            mixed = jnp.dot(values, weights.astype(jnp.bfloat16), preferred_element_type=jnp.float32)
            if old is not None:
                factor = jnp.exp2((old[0][head] - top) * slope)
                total = old[1][head] * factor + total
                mixed = old[2][head] * factor + mixed
            tops.append(top)
            totals.append(total)
            sums.append(mixed)
        return tops, totals, sums

    def load(stats, sums):
        return (
            [stats[head : head + 1] for head in range(heads)],
            [stats[heads + head : heads + head + 1] for head in range(heads)],
            [sums[head] for head in range(heads)],
        )

    def store(state):
        tops, totals, sums = state
        if last:
            for head in range(heads):
                result = (sums[head] * (1.0 / totals[head])).astype(out_ref.dtype)
                out_ref[:, head * head_size : (head + 1) * head_size] = result.T
        else:
            stats_ref[...] = jnp.concatenate(tops + totals, axis=0)
            for head in range(heads):
                sums_ref[head] = sums[head]

    start = parts[0][1]
    steps = entries // step_blocks
    low = jnp.maximum(first_key // rows - start, 0) // step_blocks
    high = jnp.minimum(own + step_blocks - start, entries) // step_blocks

    def old_state():
        return load(old_stats_ref[...], old_sums_ref)

    if first:
        state = step(0, None)
        if steps > 1:
            state = lax.fori_loop(jnp.maximum(low, 1), high, step, state)
        store(state)
    elif steps > 1:
        store(lax.fori_loop(low, high, step, old_state()))
    else:
        needed = (low < 1) & (high > 0)
        pl.when(needed)(lambda: store(step(0, old_state())))
        pl.when(jnp.logical_not(needed))(lambda: store(old_state()))


def attend(parts, first, last, lengths, queries, kvs, state, heads):
    head_size = kvs[0].shape[2] // 2
    step_blocks = math.gcd(kvs[0].shape[0], STEP_BLOCKS)
    rows = queries.shape[0] if first else queries.shape[2]
    keys = sum(kv.shape[0] * kv.shape[1] for kv in kvs)
    stats = jax.ShapeDtypeStruct((2 * heads, rows), jnp.float32)
    sums = jax.ShapeDtypeStruct((heads, head_size, rows), jnp.float32)
    turned = jax.ShapeDtypeStruct((heads, head_size, rows), queries.dtype)
    whole = pl.BlockSpec(memory_space=pltpu.VMEM)
    if last:
        out_shape = jax.ShapeDtypeStruct((rows, heads * head_size), queries.dtype)
    elif first:
        out_shape = (stats, sums, turned)
    else:
        out_shape = (stats, sums)
    return pl.pallas_call(
        functools.partial(attention_kernel, head_size, parts, step_blocks, first, last),
        out_shape=out_shape,
        in_specs=[pl.BlockSpec(memory_space=pltpu.SMEM)] + [whole] * (1 + len(kvs) + len(state)),
        out_specs=jax.tree.map(lambda _: whole, out_shape),
        compiler_params=pltpu.CompilerParams(vmem_limit_bytes=32 * 1024 * 1024),
        cost_estimate=pl.CostEstimate(
            flops=4 * rows * heads * head_size * keys,
            bytes_accessed=4 * keys * head_size + 16 * rows * heads * head_size,
            transcendentals=rows * heads * keys,
        ),
    )(lengths, queries, *kvs, *state)


def exchange(piece, axis, bits):
    return lax.ppermute(piece, axis, [(i, i ^ bits) for i in range(lax.axis_size(axis))])


def all_blocks(block, axis):
    size = lax.axis_size(axis)
    return lax.all_to_all(jnp.broadcast_to(block, (size,) + block.shape), axis, 0, 0)


def exchange(piece, axis, bits):
    return lax.ppermute(piece, axis, [(i, i ^ bits) for i in range(lax.axis_size(axis))])


def body(queries, key_rows, value_rows, document_lengths):
    seqs, rows, width = queries.shape
    heads = width // key_rows.shape[2]
    assert lax.axis_size("head") == 4
    results = []
    for seq in range(seqs):
        lengths = document_lengths[seq : seq + 1]
        piece_0 = all_blocks(jnp.concatenate([key_rows[seq], value_rows[seq]], axis=1), "ctx")
        half = piece_0.shape[0] // 2
        piece_2a = exchange(piece_0[:half], "head", 2)
        piece_2b = exchange(piece_0[half:], "head", 2)
        piece_1 = exchange(piece_0, "head", 1)
        *state, turned = attend([(0, 0)], True, False, lengths, queries[seq], [piece_0], (), heads)
        state = attend([(1, 0)], False, False, lengths, turned, [piece_1], state, heads)
        piece_2a, state = lax.optimization_barrier((piece_2a, state))
        piece_3a = exchange(piece_2a, "head", 1)
        state = attend([(2, 0), (3, 0)], False, False, lengths, turned, [piece_2a, piece_3a], state, heads)
        piece_2b, state = lax.optimization_barrier((piece_2b, state))
        piece_3b = exchange(piece_2b, "head", 1)
        state = attend([(2, half)], False, False, lengths, turned, [piece_2b], state, heads)
        results.append(attend([(3, half)], False, True, lengths, turned, [piece_3b], state, heads))
    return jnp.stack(results)


def solution(mesh):
    in_specs = (
        P(None, "ctx", "head"),
        P(None, ("ctx", "head"), None),
        P(None, ("ctx", "head"), None),
        P(),
    )
    out_specs = P(None, "ctx", "head")
    return jax.shard_map(body, mesh=mesh, in_specs=in_specs, out_specs=out_specs, check_vma=False)
```

```python
import functools
import math

import jax
import jax.numpy as jnp
from jax import lax
from jax.experimental import pallas as pl
from jax.experimental.pallas import tpu as pltpu
from jax.sharding import PartitionSpec as P

NEG = -1e30
STEP_BLOCKS = 8


def attention_kernel(head_size, place, first, tail, last, lengths_ref, queries_ref, kv_ref, *refs):
    if first:
        stats_ref, sums_ref, turned_ref = refs
        old_stats_ref, old_sums_ref = stats_ref, sums_ref
    elif last:
        old_stats_ref, old_sums_ref, out_ref, result_ref, sent = refs
    else:
        old_stats_ref, old_sums_ref, stats_ref, sums_ref = refs
    own, piece = lax.axis_index("ctx"), lax.axis_index("head") ^ place
    heads, _, rows = old_sums_ref.shape
    blocks, _, piece_rows, _ = kv_ref.shape
    slope = math.log2(math.e) / math.sqrt(head_size)
    step_blocks = math.gcd(blocks, STEP_BLOCKS)

    query_pos = own * rows + lax.broadcasted_iota(jnp.int32, (1, rows), 1)
    starts = jnp.zeros((1, rows), jnp.int32)
    first_key = jnp.int32(0)
    end = jnp.int32(0)
    for document in range(lengths_ref.shape[1]):
        end = end + lengths_ref[0, document]
        starts = jnp.where(query_pos >= end, end, starts)
        first_key = jnp.where(own * rows >= end, end, first_key)

    if first:
        for head in range(heads):
            turned_ref[head] = queries_ref[:, head * head_size : (head + 1) * head_size].T
        queries_ref = turned_ref
    in_block = piece * piece_rows + lax.broadcasted_iota(jnp.int32, (piece_rows, rows), 0)

    def step(index, count, old, emit):
        start = index * step_blocks
        keys = kv_ref[pl.ds(start, count), 0].reshape(count * piece_rows, head_size)
        values = kv_ref[pl.ds(start, count), 1].reshape(count * piece_rows, head_size).T
        key_pos = jnp.concatenate([(start + i) * rows + in_block for i in range(count)], axis=0)
        valid = (key_pos >= starts) & (key_pos <= query_pos)
        scores = [
            jnp.where(valid, jnp.dot(keys, queries_ref[head], preferred_element_type=jnp.float32), NEG)
            for head in range(heads)
        ]
        for head in range(heads):
            top = jnp.max(scores[head], axis=0, keepdims=True)
            if old is not None:
                old_top, old_total, old_sums = old(head)
                top = jnp.maximum(old_top, top)
            weights = jnp.exp2((scores[head] - top) * slope)
            total = jnp.sum(weights, axis=0, keepdims=True)
            sums = jnp.dot(values, weights.astype(jnp.bfloat16), preferred_element_type=jnp.float32)
            if old is not None:
                factor = jnp.exp2((old_top - top) * slope)
                total = old_total * factor + total
                sums = old_sums * factor + sums
            emit(head, top, total, sums)

    def old_state(head):
        return old_stats_ref[head : head + 1], old_stats_ref[heads + head : heads + head + 1], old_sums_ref[head]

    def keep(head, top, total, sums):
        stats_ref[head : head + 1] = top
        stats_ref[heads + head : heads + head + 1] = total
        sums_ref[head] = sums

    def send(head):
        columns = pl.ds(head * head_size, head_size)
        return pltpu.make_async_copy(result_ref.at[:, columns], out_ref.at[:, columns], sent.at[head])

    def finish(head, top, total, sums):
        del top
        result_ref[:, head * head_size : (head + 1) * head_size] = (sums * (1.0 / total)).astype(result_ref.dtype).T
        send(head).start()

    if blocks == step_blocks:
        if first or not tail:
            step(0, blocks, None if first else old_state, keep)
        else:
            emit = finish if last else keep
            reach = 0
            for count in sorted({max(blocks // 4, 1), max(blocks // 2, 1), blocks}):
                pl.when((own >= reach) & (own < count))(functools.partial(step, 0, count, old_state, emit))
                reach = count
    else:
        if first:
            stats_ref[...] = jnp.concatenate([jnp.full((heads, rows), NEG), jnp.zeros((heads, rows))], axis=0)
            sums_ref[...] = jnp.zeros_like(sums_ref)

        def keep_old(head, top, total, sums):
            old_stats_ref[head : head + 1] = top
            old_stats_ref[heads + head : heads + head + 1] = total
            old_sums_ref[head] = sums

        @pl.loop(first_key // rows // step_blocks, own // step_blocks + 1)
        def _(index):
            step(index, step_blocks, old_state, keep_old)

        for head in range(heads):
            if not first:
                (finish if last else keep)(head, *old_state(head))
    if last:
        for head in range(heads):
            send(head).wait()


def attend(place, first, tail, last, lengths, queries, kv, state, heads):
    blocks, _, piece_rows, head_size = kv.shape
    rows = queries.shape[0] if first else queries.shape[2]
    keys = blocks * piece_rows
    stats = jax.ShapeDtypeStruct((2 * heads, rows), jnp.float32)
    sums = jax.ShapeDtypeStruct((heads, head_size, rows), jnp.float32)
    turned = jax.ShapeDtypeStruct((heads, head_size, rows), queries.dtype)
    whole = pl.BlockSpec(memory_space=pltpu.VMEM)
    scratch = []
    if last:
        out_shape = jax.ShapeDtypeStruct((rows, heads * head_size), queries.dtype)
        out_specs = pl.BlockSpec(memory_space=pl.ANY)
        scratch = [pltpu.VMEM(out_shape.shape, out_shape.dtype), pltpu.SemaphoreType.DMA((heads,))]
    else:
        out_shape = (stats, sums, turned) if first else (stats, sums)
        out_specs = (whole,) * len(out_shape)
    return pl.pallas_call(
        functools.partial(attention_kernel, head_size, place, first, tail, last),
        out_shape=out_shape,
        in_specs=[pl.BlockSpec(memory_space=pltpu.SMEM)] + [whole] * (2 + len(state)),
        out_specs=out_specs,
        scratch_shapes=scratch,
        compiler_params=pltpu.CompilerParams(vmem_limit_bytes=32 * 1024 * 1024),
        cost_estimate=pl.CostEstimate(
            flops=4 * rows * heads * head_size * keys,
            bytes_accessed=4 * keys * head_size + 16 * rows * heads * head_size,
            transcendentals=rows * heads * keys,
        ),
    )(lengths, queries, kv, *state)


def all_blocks(block, axis):
    size = lax.axis_size(axis)
    return lax.all_to_all(jnp.broadcast_to(block, (size,) + block.shape), axis, 0, 0)


def exchange(piece, axis, bits):
    return lax.ppermute(piece, axis, [(i, i ^ bits) for i in range(lax.axis_size(axis))])


def body(queries, key_rows, value_rows, document_lengths):
    seqs, rows, width = queries.shape
    heads = width // key_rows.shape[2]
    assert lax.axis_size("head") == 4
    results = []
    for seq in range(seqs):
        lengths = document_lengths[seq : seq + 1]
        piece_0 = all_blocks(jnp.stack([key_rows[seq], value_rows[seq]]), "ctx")
        piece_2 = exchange(piece_0, "head", 2)
        piece_1 = exchange(piece_0, "head", 1)
        *state, turned = attend(0, True, False, False, lengths, queries[seq], piece_0, (), heads)
        state = attend(1, False, False, False, lengths, turned, piece_1, state, heads)
        piece_2, state = lax.optimization_barrier((piece_2, state))
        piece_3 = exchange(piece_2, "head", 1)
        state = attend(2, False, True, False, lengths, turned, piece_2, state, heads)
        results.append(attend(3, False, True, True, lengths, turned, piece_3, state, heads))
    return jnp.stack(results)


def solution(mesh):
    in_specs = (
        P(None, "ctx", "head"),
        P(None, ("ctx", "head"), None),
        P(None, ("ctx", "head"), None),
        P(),
    )
    out_specs = P(None, "ctx", "head")
    return jax.shard_map(body, mesh=mesh, in_specs=in_specs, out_specs=out_specs, check_vma=False)
```

```python
import functools
import math

import jax
import jax.numpy as jnp
from jax import lax
from jax.experimental import pallas as pl
from jax.experimental.pallas import tpu as pltpu
from jax.sharding import PartitionSpec as P

NEG = -1e30
STEP_BLOCKS = 8


def attention_kernel(head_size, place, first, tail, last, pieces, *refs):
    queries_ref, *refs = refs
    kv_refs, refs = refs[:pieces], refs[pieces:]
    blocks, _, piece_rows, _ = kv_refs[0].shape
    step_blocks = math.gcd(blocks, STEP_BLOCKS)
    lengths_ref = None
    if first or blocks > step_blocks:
        lengths_ref, *refs = refs
    if first:
        stats_ref, sums_ref, starts_ref, turned_ref = refs
        old_stats_ref, old_sums_ref = stats_ref, sums_ref
    elif last:
        old_stats_ref, old_sums_ref, starts_ref, out_ref, result_ref, sent = refs[:6]
    else:
        old_stats_ref, old_sums_ref, starts_ref, stats_ref, sums_ref = refs
    own, piece = lax.axis_index("ctx"), lax.axis_index("head") ^ place
    heads, _, rows = old_sums_ref.shape
    slope = math.log2(math.e) / math.sqrt(head_size)

    query_pos = own * rows + lax.broadcasted_iota(jnp.int32, (1, rows), 1)
    first_key = jnp.int32(0)
    if lengths_ref is not None:
        starts = jnp.zeros((1, rows), jnp.int32)
        end = jnp.int32(0)
        for document in range(lengths_ref.shape[1]):
            end = end + lengths_ref[0, document]
            starts = jnp.where(query_pos >= end, end, starts)
            first_key = jnp.where(own * rows >= end, end, first_key)
    else:
        starts = starts_ref[...]
    if first:
        starts_ref[...] = starts
        for head in range(heads):
            turned_ref[head] = queries_ref[:, head * head_size : (head + 1) * head_size].T
        queries_ref = turned_ref
    in_block = piece * piece_rows + lax.broadcasted_iota(jnp.int32, (piece_rows, rows), 0)

    def step(index, count, old, emit):
        start = index * step_blocks
        keys, values = (
            jnp.concatenate(
                [kv_ref[pl.ds(start, count), i].reshape(count * piece_rows, head_size) for kv_ref in kv_refs], axis=0
            )
            for i in range(2)
        )
        values = values.T
        key_pos = jnp.concatenate(
            [(i * blocks + start + j) * rows + in_block for i in range(pieces) for j in range(count)], axis=0
        )
        valid = (key_pos >= starts) & (key_pos <= query_pos)
        scores = [
            jnp.where(valid, jnp.dot(keys, queries_ref[head], preferred_element_type=jnp.float32), NEG)
            for head in range(heads)
        ]
        for head in range(heads):
            top = jnp.max(scores[head], axis=0, keepdims=True)
            if old is not None:
                old_top, old_total, old_sums = old(head)
                top = jnp.maximum(old_top, top)
            weights = jnp.exp2((scores[head] - top) * slope)
            total = jnp.sum(weights, axis=0, keepdims=True)
            sums = jnp.dot(values, weights.astype(jnp.bfloat16), preferred_element_type=jnp.float32)
            if old is not None:
                factor = jnp.exp2((old_top - top) * slope)
                total = old_total * factor + total
                sums = old_sums * factor + sums
            emit(head, top, total, sums)

    def old_state(head):
        return old_stats_ref[head : head + 1], old_stats_ref[heads + head : heads + head + 1], old_sums_ref[head]

    def keep(head, top, total, sums):
        stats_ref[head : head + 1] = top
        stats_ref[heads + head : heads + head + 1] = total
        sums_ref[head] = sums

    def send(head):
        columns = pl.ds(head * head_size, head_size)
        return pltpu.make_async_copy(result_ref.at[:, columns], out_ref.at[:, columns], sent.at[head])

    def finish(head, top, total, sums):
        del top
        result_ref[:, head * head_size : (head + 1) * head_size] = (sums * (1.0 / total)).astype(result_ref.dtype).T
        send(head).start()

    if blocks == step_blocks:
        if first or not tail:
            step(0, blocks, None if first else old_state, keep)
        else:
            emit = finish if last else keep
            reach = 0
            for count in sorted({max(blocks // 4, 1), max(blocks // 2, 1), blocks}):
                pl.when((own >= reach) & (own < count))(functools.partial(step, 0, count, old_state, emit))
                reach = count
    else:
        if last:
            stats_ref, sums_ref = refs[-2:]
        if first:
            stats_ref[...] = jnp.concatenate([jnp.full((heads, rows), NEG), jnp.zeros((heads, rows))], axis=0)
            sums_ref[...] = jnp.zeros_like(sums_ref)
        else:
            stats_ref[...] = old_stats_ref[...]
            sums_ref[...] = old_sums_ref[...]

        def new_state(head):
            return stats_ref[head : head + 1], stats_ref[heads + head : heads + head + 1], sums_ref[head]

        low = first_key // rows // step_blocks if pieces == 1 else 0
        high = jnp.minimum(own // step_blocks + 1, blocks // step_blocks)

        @pl.loop(low, high)
        def _(index):
            step(index, step_blocks, new_state, keep)

        if last:
            for head in range(heads):
                finish(head, *new_state(head))
    if last:
        for head in range(heads):
            send(head).wait()


def attend(place, first, tail, last, lengths, queries, kvs, state, heads):
    blocks, _, piece_rows, head_size = kvs[0].shape
    rows = queries.shape[0] if first else queries.shape[2]
    stats = jax.ShapeDtypeStruct((2 * heads, rows), jnp.float32)
    sums = jax.ShapeDtypeStruct((heads, head_size, rows), jnp.float32)
    starts = jax.ShapeDtypeStruct((1, rows), jnp.int32)
    turned = jax.ShapeDtypeStruct((heads, head_size, rows), queries.dtype)
    whole = pl.BlockSpec(memory_space=pltpu.VMEM)
    operands, in_specs = [queries, *kvs], [whole] * (1 + len(kvs))
    if first or blocks > math.gcd(blocks, STEP_BLOCKS):
        operands.append(lengths)
        in_specs.append(pl.BlockSpec(memory_space=pltpu.SMEM))
    scratch = []
    if last:
        out_shape = jax.ShapeDtypeStruct((rows, heads * head_size), queries.dtype)
        out_specs = pl.BlockSpec(memory_space=pl.ANY)
        scratch = [pltpu.VMEM(out_shape.shape, out_shape.dtype), pltpu.SemaphoreType.DMA((heads,))]
        if blocks > math.gcd(blocks, STEP_BLOCKS):
            scratch += [pltpu.VMEM(stats.shape, stats.dtype), pltpu.VMEM(sums.shape, sums.dtype)]
    else:
        out_shape = (stats, sums, starts, turned) if first else (stats, sums)
        out_specs = (whole,) * len(out_shape)
    return pl.pallas_call(
        functools.partial(attention_kernel, head_size, place, first, tail, last, len(kvs)),
        out_shape=out_shape,
        in_specs=in_specs + [whole] * len(state),
        out_specs=out_specs,
        scratch_shapes=scratch,
        compiler_params=pltpu.CompilerParams(vmem_limit_bytes=32 * 1024 * 1024),
        cost_estimate=pl.CostEstimate(flops=1, bytes_accessed=1, transcendentals=0),
    )(*operands, *state)


def all_blocks(block, axis):
    size = lax.axis_size(axis)
    return lax.all_to_all(jnp.broadcast_to(block, (size,) + block.shape), axis, 0, 0)


def exchange(piece, axis, bits):
    return lax.ppermute(piece, axis, [(i, i ^ bits) for i in range(lax.axis_size(axis))])


def body(queries, key_rows, value_rows, document_lengths):
    seqs, rows, width = queries.shape
    heads = width // key_rows.shape[2]
    assert lax.axis_size("head") == 4
    results = []
    for seq in range(seqs):
        lengths = document_lengths[seq : seq + 1]
        piece_0 = all_blocks(jnp.stack([key_rows[seq], value_rows[seq]]), "ctx")
        half = piece_0.shape[0] // 2
        piece_2 = exchange(piece_0, "head", 2)
        piece_1 = [exchange(piece_0[:half], "head", 1), exchange(piece_0[half:], "head", 1)]
        *state, starts, turned = attend(0, True, False, False, lengths, queries[seq], [piece_0], (), heads)
        state = attend(1, False, False, False, lengths, turned, piece_1, (*state, starts), heads)
        piece_2, state = lax.optimization_barrier((piece_2, state))
        piece_3 = exchange(piece_2, "head", 1)
        state = attend(2, False, True, False, lengths, turned, [piece_2], (*state, starts), heads)
        results.append(attend(3, False, True, True, lengths, turned, [piece_3], (*state, starts), heads))
    return jnp.stack(results)


def solution(mesh):
    in_specs = (
        P(None, "ctx", "head"),
        P(None, ("ctx", "head"), None),
        P(None, ("ctx", "head"), None),
        P(),
    )
    out_specs = P(None, "ctx", "head")
    return jax.shard_map(body, mesh=mesh, in_specs=in_specs, out_specs=out_specs, check_vma=False)
```

```python
import functools
import math

import jax
import jax.numpy as jnp
from jax import lax
from jax.experimental import pallas as pl
from jax.experimental.pallas import tpu as pltpu
from jax.sharding import PartitionSpec as P

NEG = -1e30
STEP_BLOCKS = 8


def attention_kernel(head_size, parts, kind, *refs):
    first, last = kind == "first", kind == "last"
    queries_ref, *refs = refs
    kv_refs, refs = refs[: len(parts)], refs[len(parts) :]
    blocks = kv_refs[0].shape[0]
    step_blocks = math.gcd(blocks, STEP_BLOCKS)
    lengths_ref = None
    if first or blocks > step_blocks:
        lengths_ref, *refs = refs
    if first:
        stats_ref, sums_ref, starts_ref, turned_ref = refs
        old_stats_ref, old_sums_ref = stats_ref, sums_ref
    elif last:
        old_stats_ref, old_sums_ref, starts_ref, out_ref, result_ref, sent = refs[:6]
    else:
        old_stats_ref, old_sums_ref, starts_ref, stats_ref, sums_ref = refs
    own, head_place = lax.axis_index("ctx"), lax.axis_index("head")
    heads, _, rows = old_sums_ref.shape
    piece_rows = rows // lax.axis_size("head")
    slope = math.log2(math.e) / math.sqrt(head_size)

    query_pos = own * rows + lax.broadcasted_iota(jnp.int32, (1, rows), 1)
    first_key = jnp.int32(0)
    if lengths_ref is not None:
        starts = jnp.zeros((1, rows), jnp.int32)
        end = jnp.int32(0)
        for document in range(lengths_ref.shape[1]):
            end = end + lengths_ref[0, document]
            starts = jnp.where(query_pos >= end, end, starts)
            first_key = jnp.where(own * rows >= end, end, first_key)
    else:
        starts = starts_ref[...]
    if first:
        starts_ref[...] = starts
        for head in range(heads):
            turned_ref[head] = queries_ref[:, head * head_size : (head + 1) * head_size].T
        queries_ref = turned_ref
    in_piece = lax.broadcasted_iota(jnp.int32, (piece_rows, rows), 0)

    def step(index, count, old, emit):
        here = pl.ds(index * step_blocks, count)
        keys, values = (
            jnp.concatenate([kv_ref[here, i].reshape(-1, head_size) for kv_ref in kv_refs], axis=0) for i in range(2)
        )
        values = values.T
        key_pos = []
        for kv_ref, (flip, place, skip) in zip(kv_refs, parts):
            for i in range(count):
                block = 2 * (index * step_blocks + i) + (own ^ flip) % 2
                start = block * rows + (head_place ^ place) * piece_rows + skip
                key_pos.append(start + in_piece[: kv_ref.shape[2]])
        key_pos = jnp.concatenate(key_pos, axis=0)
        valid = (key_pos >= starts) & (key_pos <= query_pos)
        scores = [
            jnp.where(valid, jnp.dot(keys, queries_ref[head], preferred_element_type=jnp.float32), NEG)
            for head in range(heads)
        ]
        for head in range(heads):
            top = jnp.max(scores[head], axis=0, keepdims=True)
            if old is not None:
                old_top, old_total, old_sums = old(head)
                top = jnp.maximum(old_top, top)
            weights = jnp.exp2((scores[head] - top) * slope)
            total = jnp.sum(weights, axis=0, keepdims=True)
            sums = jnp.dot(values, weights.astype(jnp.bfloat16), preferred_element_type=jnp.float32)
            if old is not None:
                factor = jnp.exp2((old_top - top) * slope)
                total = old_total * factor + total
                sums = old_sums * factor + sums
            emit(head, top, total, sums)

    def old_state(head):
        return old_stats_ref[head : head + 1], old_stats_ref[heads + head : heads + head + 1], old_sums_ref[head]

    def keep(head, top, total, sums):
        stats_ref[head : head + 1] = top
        stats_ref[heads + head : heads + head + 1] = total
        sums_ref[head] = sums

    def send(head):
        columns = pl.ds(head * head_size, head_size)
        return pltpu.make_async_copy(result_ref.at[:, columns], out_ref.at[:, columns], sent.at[head])

    def finish(head, top, total, sums):
        del top
        result_ref[:, head * head_size : (head + 1) * head_size] = (sums * (1.0 / total)).astype(result_ref.dtype).T
        send(head).start()

    if blocks == step_blocks:
        if first:
            step(0, blocks, None, keep)
        else:
            emit = finish if last else keep
            reach = 0
            for count in sorted({max(blocks // 4, 1), max(blocks // 2, 1), blocks}):
                pl.when((own // 2 >= reach) & (own // 2 < count))(functools.partial(step, 0, count, old_state, emit))
                reach = count
    else:
        if last:
            stats_ref, sums_ref = refs[-2:]
        if first:
            stats_ref[...] = jnp.concatenate([jnp.full((heads, rows), NEG), jnp.zeros((heads, rows))], axis=0)
            sums_ref[...] = jnp.zeros_like(sums_ref)
        else:
            stats_ref[...] = old_stats_ref[...]
            sums_ref[...] = old_sums_ref[...]

        def new_state(head):
            return stats_ref[head : head + 1], stats_ref[heads + head : heads + head + 1], sums_ref[head]

        @pl.loop(first_key // rows // 2 // step_blocks, own // 2 // step_blocks + 1)
        def _(index):
            step(index, step_blocks, new_state, keep)

        if last:
            for head in range(heads):
                finish(head, *new_state(head))
    if last:
        for head in range(heads):
            send(head).wait()


def attend(parts, kind, lengths, queries, kvs, state, heads):
    first, last = kind == "first", kind == "last"
    blocks, head_size = kvs[0].shape[0], kvs[0].shape[3]
    rows = queries.shape[0] if first else queries.shape[2]
    stats = jax.ShapeDtypeStruct((2 * heads, rows), jnp.float32)
    sums = jax.ShapeDtypeStruct((heads, head_size, rows), jnp.float32)
    starts = jax.ShapeDtypeStruct((1, rows), jnp.int32)
    turned = jax.ShapeDtypeStruct((heads, head_size, rows), queries.dtype)
    whole = pl.BlockSpec(memory_space=pltpu.VMEM)
    operands, in_specs = [queries, *kvs], [whole] * (1 + len(kvs))
    if first or blocks > math.gcd(blocks, STEP_BLOCKS):
        operands.append(lengths)
        in_specs.append(pl.BlockSpec(memory_space=pltpu.SMEM))
    scratch = []
    if last:
        out_shape = jax.ShapeDtypeStruct((rows, heads * head_size), queries.dtype)
        out_specs = pl.BlockSpec(memory_space=pl.ANY)
        scratch = [pltpu.VMEM(out_shape.shape, out_shape.dtype), pltpu.SemaphoreType.DMA((heads,))]
        if blocks > math.gcd(blocks, STEP_BLOCKS):
            scratch += [pltpu.VMEM(stats.shape, stats.dtype), pltpu.VMEM(sums.shape, sums.dtype)]
    else:
        out_shape = (stats, sums, starts, turned) if first else (stats, sums)
        out_specs = (whole,) * len(out_shape)
    return pl.pallas_call(
        functools.partial(attention_kernel, head_size, parts, kind),
        out_shape=out_shape,
        in_specs=in_specs + [whole] * len(state),
        out_specs=out_specs,
        scratch_shapes=scratch,
        compiler_params=pltpu.CompilerParams(vmem_limit_bytes=32 * 1024 * 1024),
        cost_estimate=pl.CostEstimate(flops=1, bytes_accessed=1, transcendentals=0),
    )(*operands, *state)


def same_parity_blocks(block, axis):
    size = lax.axis_size(axis)
    groups = [list(range(parity, size, 2)) for parity in range(2)]
    spread = jnp.broadcast_to(block, (size // 2,) + block.shape)
    return lax.all_to_all(spread, axis, 0, 0, axis_index_groups=groups)


def exchange(piece, axis, bits):
    return lax.ppermute(piece, axis, [(i, i ^ bits) for i in range(lax.axis_size(axis))])


def body(queries, key_rows, value_rows, document_lengths):
    seqs, rows, width = queries.shape
    heads = width // key_rows.shape[2]
    assert lax.axis_size("head") == 4 and lax.axis_size("ctx") % 2 == 0
    results = []
    for seq in range(seqs):
        run = functools.partial(attend, lengths=document_lengths[seq : seq + 1], heads=heads)
        own = same_parity_blocks(jnp.stack([key_rows[seq], value_rows[seq]]), "ctx")
        half = own.shape[2] // 2

        across = exchange(own, "ctx", 1)
        far = exchange(own, "head", 2)
        near = [exchange(own[:, :, :half], "head", 1), exchange(own[:, :, half:], "head", 1)]
        stats, sums, starts, turned = run([(0, 0, 0)], "first", queries=queries[seq], kvs=[own], state=())
        run = functools.partial(run, queries=turned)
        stats, sums = run([(0, 1, 0), (0, 1, half)], "middle", kvs=near, state=(stats, sums, starts))
        across, far, stats, sums = lax.optimization_barrier((across, far, stats, sums))

        corner = [exchange(across[:, :, :half], "head", 2), exchange(far[:, :, half:], "ctx", 1)]
        near = [exchange(across, "head", 1), exchange(far, "head", 1)]
        stats, sums = run([(1, 0, 0), (0, 2, 0)], "middle", kvs=[across, far], state=(stats, sums, starts))
        stats, sums = run([(1, 1, 0), (0, 3, 0)], "middle", kvs=near, state=(stats, sums, starts))
        *corner, stats, sums = lax.optimization_barrier((*corner, stats, sums))

        near = [exchange(part, "head", 1) for part in corner]
        stats, sums = run([(1, 2, 0), (1, 2, half)], "middle", kvs=corner, state=(stats, sums, starts))
        results.append(run([(1, 3, 0), (1, 3, half)], "last", kvs=near, state=(stats, sums, starts)))
    return jnp.stack(results)


def solution(mesh):
    in_specs = (
        P(None, "ctx", "head"),
        P(None, ("ctx", "head"), None),
        P(None, ("ctx", "head"), None),
        P(),
    )
    out_specs = P(None, "ctx", "head")
    return jax.shard_map(body, mesh=mesh, in_specs=in_specs, out_specs=out_specs, check_vma=False)
```

```python
import functools
import math

import jax
import jax.numpy as jnp
from jax import lax
from jax.experimental import pallas as pl
from jax.experimental.pallas import tpu as pltpu
from jax.sharding import PartitionSpec as P

NEG = -1e30
STEP_BLOCKS = 8


def attention_kernel(head_size, place, first, tail, last, pieces, window, *refs):
    queries_ref, *refs = refs
    kv_refs, refs = refs[:pieces], refs[pieces:]
    counts = [kv_ref.shape[0] for kv_ref in kv_refs]
    piece_rows = kv_refs[0].shape[2]
    lengths_ref = None
    if first or window > STEP_BLOCKS:
        lengths_ref, *refs = refs
    if first:
        stats_ref, sums_ref, starts_ref, turned_ref = refs
        old_stats_ref, old_sums_ref = stats_ref, sums_ref
    elif last:
        old_stats_ref, old_sums_ref, starts_ref, out_ref, result_ref, sent = refs[:6]
    else:
        old_stats_ref, old_sums_ref, starts_ref, stats_ref, sums_ref = refs
    own, piece = lax.axis_index("ctx"), lax.axis_index("head") ^ place
    base = jnp.maximum(own - (window - 1), 0)
    heads, _, rows = old_sums_ref.shape
    slope = math.log2(math.e) / math.sqrt(head_size)

    query_pos = own * rows + lax.broadcasted_iota(jnp.int32, (1, rows), 1)
    first_key = jnp.int32(0)
    if lengths_ref is not None:
        starts = jnp.zeros((1, rows), jnp.int32)
        end = jnp.int32(0)
        for document in range(lengths_ref.shape[1]):
            end = end + lengths_ref[0, document]
            starts = jnp.where(query_pos >= end, end, starts)
            first_key = jnp.where(own * rows >= end, end, first_key)
    else:
        starts = starts_ref[...]
    if first:
        starts_ref[...] = starts
        for head in range(heads):
            turned_ref[head] = queries_ref[:, head * head_size : (head + 1) * head_size].T
        queries_ref = turned_ref
    in_block = piece * piece_rows + lax.broadcasted_iota(jnp.int32, (piece_rows, rows), 0)

    def step(start, taken, old, emit):
        keys, values = (
            jnp.concatenate(
                [
                    kv_ref[pl.ds(start, count), i].reshape(count * piece_rows, head_size)
                    for kv_ref, count in zip(kv_refs, taken)
                ],
                axis=0,
            )
            for i in range(2)
        )
        values = values.T
        key_pos = jnp.concatenate(
            [
                (base + sum(counts[:i]) + start + j) * rows + in_block
                for i, count in enumerate(taken)
                for j in range(count)
            ],
            axis=0,
        )
        valid = (key_pos >= starts) & (key_pos <= query_pos)
        scores = [
            jnp.where(valid, jnp.dot(keys, queries_ref[head], preferred_element_type=jnp.float32), NEG)
            for head in range(heads)
        ]
        for head in range(heads):
            top = jnp.max(scores[head], axis=0, keepdims=True)
            if old is not None:
                old_top, old_total, old_sums = old(head)
                top = jnp.maximum(old_top, top)
            weights = jnp.exp2((scores[head] - top) * slope)
            total = jnp.sum(weights, axis=0, keepdims=True)
            sums = jnp.dot(values, weights.astype(jnp.bfloat16), preferred_element_type=jnp.float32)
            if old is not None:
                factor = jnp.exp2((old_top - top) * slope)
                total = old_total * factor + total
                sums = old_sums * factor + sums
            emit(head, top, total, sums)

    def old_state(head):
        return old_stats_ref[head : head + 1], old_stats_ref[heads + head : heads + head + 1], old_sums_ref[head]

    def keep(head, top, total, sums):
        stats_ref[head : head + 1] = top
        stats_ref[heads + head : heads + head + 1] = total
        sums_ref[head] = sums

    def send(head):
        columns = pl.ds(head * head_size, head_size)
        return pltpu.make_async_copy(result_ref.at[:, columns], out_ref.at[:, columns], sent.at[head])

    def finish(head, top, total, sums):
        del top
        result_ref[:, head * head_size : (head + 1) * head_size] = (sums * (1.0 / total)).astype(result_ref.dtype).T
        send(head).start()

    if window <= STEP_BLOCKS:
        if first or not tail:
            step(0, counts, None if first else old_state, keep)
        else:
            emit = finish if last else keep
            reach = 0
            for count in sorted({min(max(STEP_BLOCKS // 4, 1), window), min(max(STEP_BLOCKS // 2, 1), window), window}):
                here = (own >= reach) & (own < count) if count < window else own >= reach
                pl.when(here)(functools.partial(step, 0, [count], old_state, emit))
                reach = count
    else:
        if last:
            stats_ref, sums_ref = refs[-2:]
        if first:
            stats_ref[...] = jnp.concatenate([jnp.full((heads, rows), NEG), jnp.zeros((heads, rows))], axis=0)
            sums_ref[...] = jnp.zeros_like(sums_ref)
        else:
            stats_ref[...] = old_stats_ref[...]
            sums_ref[...] = old_sums_ref[...]

        def new_state(head):
            return stats_ref[head : head + 1], stats_ref[heads + head : heads + head + 1], sums_ref[head]

        step_blocks = math.gcd(counts[0], STEP_BLOCKS)
        low = jnp.maximum(first_key // rows - base, 0) // step_blocks if pieces == 1 else 0
        high = jnp.minimum((own - base) // step_blocks + 1, counts[0] // step_blocks)

        @pl.loop(low, high)
        def _(index):
            step(index * step_blocks, [step_blocks] * pieces, new_state, keep)

        if last:
            for head in range(heads):
                finish(head, *new_state(head))
    if last:
        for head in range(heads):
            send(head).wait()


def attend(place, first, tail, last, lengths, queries, kvs, state, heads):
    window, head_size = sum(kv.shape[0] for kv in kvs), kvs[0].shape[3]
    rows = queries.shape[0] if first else queries.shape[2]
    stats = jax.ShapeDtypeStruct((2 * heads, rows), jnp.float32)
    sums = jax.ShapeDtypeStruct((heads, head_size, rows), jnp.float32)
    starts = jax.ShapeDtypeStruct((1, rows), jnp.int32)
    turned = jax.ShapeDtypeStruct((heads, head_size, rows), queries.dtype)
    whole = pl.BlockSpec(memory_space=pltpu.VMEM)
    operands, in_specs = [queries, *kvs], [whole] * (1 + len(kvs))
    if first or window > STEP_BLOCKS:
        operands.append(lengths)
        in_specs.append(pl.BlockSpec(memory_space=pltpu.SMEM))
    scratch = []
    if last:
        out_shape = jax.ShapeDtypeStruct((rows, heads * head_size), queries.dtype)
        out_specs = pl.BlockSpec(memory_space=pl.ANY)
        scratch = [pltpu.VMEM(out_shape.shape, out_shape.dtype), pltpu.SemaphoreType.DMA((heads,))]
        if window > STEP_BLOCKS:
            scratch += [pltpu.VMEM(stats.shape, stats.dtype), pltpu.VMEM(sums.shape, sums.dtype)]
    else:
        out_shape = (stats, sums, starts, turned) if first else (stats, sums)
        out_specs = (whole,) * len(out_shape)
    return pl.pallas_call(
        functools.partial(attention_kernel, head_size, place, first, tail, last, len(kvs), window),
        out_shape=out_shape,
        in_specs=in_specs + [whole] * len(state),
        out_specs=out_specs,
        scratch_shapes=scratch,
        compiler_params=pltpu.CompilerParams(vmem_limit_bytes=32 * 1024 * 1024),
        cost_estimate=pl.CostEstimate(flops=1, bytes_accessed=1, transcendentals=0),
    )(*operands, *state)


def all_blocks(block, axis):
    size = lax.axis_size(axis)
    return lax.all_to_all(jnp.broadcast_to(block, (size,) + block.shape), axis, 0, 0)


def window_blocks(rows, blocks):
    longest = 3 * rows * blocks // 4
    window = -(-(longest - 1) // rows) + 1
    if window > STEP_BLOCKS:
        window = -(-window // STEP_BLOCKS) * STEP_BLOCKS
    return min(window, blocks)


def exchange(piece, axis, bits):
    return lax.ppermute(piece, axis, [(i, i ^ bits) for i in range(lax.axis_size(axis))])


def body(queries, key_rows, value_rows, document_lengths):
    seqs, rows, width = queries.shape
    heads = width // key_rows.shape[2]
    assert lax.axis_size("head") == 4
    results = []
    for seq in range(seqs):
        lengths = document_lengths[seq : seq + 1]
        piece_0 = all_blocks(jnp.stack([key_rows[seq], value_rows[seq]]), "ctx")
        window = window_blocks(rows, piece_0.shape[0])
        base = jnp.maximum(lax.axis_index("ctx") - (window - 1), 0)
        piece_0 = lax.dynamic_slice_in_dim(piece_0, base, window, 0)
        half = (window + 1) // 2
        piece_2 = exchange(piece_0, "head", 2)
        piece_1 = [exchange(piece_0[:half], "head", 1), exchange(piece_0[half:], "head", 1)]
        *state, starts, turned = attend(0, True, False, False, lengths, queries[seq], [piece_0], (), heads)
        state = attend(1, False, False, False, lengths, turned, piece_1, (*state, starts), heads)
        piece_2, state = lax.optimization_barrier((piece_2, state))
        piece_3 = exchange(piece_2, "head", 1)
        state = attend(2, False, True, False, lengths, turned, [piece_2], (*state, starts), heads)
        results.append(attend(3, False, True, True, lengths, turned, [piece_3], (*state, starts), heads))
    return jnp.stack(results)


def solution(mesh):
    in_specs = (
        P(None, "ctx", "head"),
        P(None, ("ctx", "head"), None),
        P(None, ("ctx", "head"), None),
        P(),
    )
    out_specs = P(None, "ctx", "head")
    return jax.shard_map(body, mesh=mesh, in_specs=in_specs, out_specs=out_specs, check_vma=False)
```

```python
import functools
import math

import jax
import jax.numpy as jnp
from jax import lax
from jax.experimental import pallas as pl
from jax.experimental.pallas import tpu as pltpu
from jax.sharding import PartitionSpec as P

NEG = -1e30
STEP_BLOCKS = 8


def attention_kernel(head_size, parts, kind, *refs):
    first, last = kind == "first", kind == "last"
    queries_ref, *refs = refs
    kv_refs, refs = refs[: len(parts)], refs[len(parts) :]
    blocks = kv_refs[0].shape[0]
    step_blocks = math.gcd(blocks, STEP_BLOCKS)
    lengths_ref = None
    if first or blocks > step_blocks:
        lengths_ref, *refs = refs
    if first:
        stats_ref, sums_ref, starts_ref, turned_ref = refs
        old_stats_ref, old_sums_ref = stats_ref, sums_ref
    elif last:
        old_stats_ref, old_sums_ref, starts_ref, out_ref, result_ref, sent = refs[:6]
    else:
        old_stats_ref, old_sums_ref, starts_ref, stats_ref, sums_ref = refs
    own, head_place = lax.axis_index("ctx"), lax.axis_index("head")
    heads, _, rows = old_sums_ref.shape
    piece_rows = rows // lax.axis_size("head")
    slope = math.log2(math.e) / math.sqrt(head_size)

    query_pos = own * rows + lax.broadcasted_iota(jnp.int32, (1, rows), 1)
    first_key = jnp.int32(0)
    if lengths_ref is not None:
        starts = jnp.zeros((1, rows), jnp.int32)
        end = jnp.int32(0)
        for document in range(lengths_ref.shape[1]):
            end = end + lengths_ref[0, document]
            starts = jnp.where(query_pos >= end, end, starts)
            first_key = jnp.where(own * rows >= end, end, first_key)
    else:
        starts = starts_ref[...]
    if first:
        starts_ref[...] = starts
        for head in range(heads):
            turned_ref[head] = queries_ref[:, head * head_size : (head + 1) * head_size].T
        queries_ref = turned_ref
    in_piece = lax.broadcasted_iota(jnp.int32, (piece_rows, rows), 0)

    def step(index, count, old, emit):
        here = pl.ds(index * step_blocks, count)
        keys, values = (
            jnp.concatenate([kv_ref[here, i].reshape(-1, head_size) for kv_ref in kv_refs], axis=0) for i in range(2)
        )
        values = values.T
        key_pos = []
        for kv_ref, (flip, place, skip) in zip(kv_refs, parts):
            for i in range(count):
                block = 2 * (index * step_blocks + i) + (own ^ flip) % 2
                start = block * rows + (head_place ^ place) * piece_rows + skip
                key_pos.append(start + in_piece[: kv_ref.shape[2]])
        key_pos = jnp.concatenate(key_pos, axis=0)
        valid = (key_pos >= starts) & (key_pos <= query_pos)
        scores = [
            jnp.where(valid, jnp.dot(keys, queries_ref[head], preferred_element_type=jnp.float32), NEG)
            for head in range(heads)
        ]
        for head in range(heads):
            top = jnp.max(scores[head], axis=0, keepdims=True)
            if old is not None:
                old_top, old_total, old_sums = old(head)
                top = jnp.maximum(old_top, top)
            weights = jnp.exp2((scores[head] - top) * slope)
            total = jnp.sum(weights, axis=0, keepdims=True)
            sums = jnp.dot(values, weights.astype(jnp.bfloat16), preferred_element_type=jnp.float32)
            if old is not None:
                factor = jnp.exp2((old_top - top) * slope)
                total = old_total * factor + total
                sums = old_sums * factor + sums
            emit(head, top, total, sums)

    def old_state(head):
        return old_stats_ref[head : head + 1], old_stats_ref[heads + head : heads + head + 1], old_sums_ref[head]

    def keep(head, top, total, sums):
        stats_ref[head : head + 1] = top
        stats_ref[heads + head : heads + head + 1] = total
        sums_ref[head] = sums

    def send(head):
        columns = pl.ds(head * head_size, head_size)
        return pltpu.make_async_copy(result_ref.at[:, columns], out_ref.at[:, columns], sent.at[head])

    def finish(head, top, total, sums):
        del top
        result_ref[:, head * head_size : (head + 1) * head_size] = (sums * (1.0 / total)).astype(result_ref.dtype).T
        send(head).start()

    if blocks == step_blocks:
        if first:
            step(0, blocks, None, keep)
        else:
            emit = finish if last else keep
            reach = 0
            for count in sorted({max(blocks // 4, 1), max(blocks // 2, 1), blocks}):
                pl.when((own // 2 >= reach) & (own // 2 < count))(functools.partial(step, 0, count, old_state, emit))
                reach = count
    else:
        if last:
            stats_ref, sums_ref = refs[-2:]
        if first:
            stats_ref[...] = jnp.concatenate([jnp.full((heads, rows), NEG), jnp.zeros((heads, rows))], axis=0)
            sums_ref[...] = jnp.zeros_like(sums_ref)
        else:
            stats_ref[...] = old_stats_ref[...]
            sums_ref[...] = old_sums_ref[...]

        def new_state(head):
            return stats_ref[head : head + 1], stats_ref[heads + head : heads + head + 1], sums_ref[head]

        @pl.loop(first_key // rows // 2 // step_blocks, own // 2 // step_blocks + 1)
        def _(index):
            step(index, step_blocks, new_state, keep)

        if last:
            for head in range(heads):
                finish(head, *new_state(head))
    if last:
        for head in range(heads):
            send(head).wait()


def attend(parts, kind, lengths, queries, kvs, state, heads):
    first, last = kind == "first", kind == "last"
    blocks, head_size = kvs[0].shape[0], kvs[0].shape[3]
    rows = queries.shape[0] if first else queries.shape[2]
    stats = jax.ShapeDtypeStruct((2 * heads, rows), jnp.float32)
    sums = jax.ShapeDtypeStruct((heads, head_size, rows), jnp.float32)
    starts = jax.ShapeDtypeStruct((1, rows), jnp.int32)
    turned = jax.ShapeDtypeStruct((heads, head_size, rows), queries.dtype)
    whole = pl.BlockSpec(memory_space=pltpu.VMEM)
    operands, in_specs = [queries, *kvs], [whole] * (1 + len(kvs))
    if first or blocks > math.gcd(blocks, STEP_BLOCKS):
        operands.append(lengths)
        in_specs.append(pl.BlockSpec(memory_space=pltpu.SMEM))
    scratch = []
    if last:
        out_shape = jax.ShapeDtypeStruct((rows, heads * head_size), queries.dtype)
        out_specs = pl.BlockSpec(memory_space=pl.ANY)
        scratch = [pltpu.VMEM(out_shape.shape, out_shape.dtype), pltpu.SemaphoreType.DMA((heads,))]
        if blocks > math.gcd(blocks, STEP_BLOCKS):
            scratch += [pltpu.VMEM(stats.shape, stats.dtype), pltpu.VMEM(sums.shape, sums.dtype)]
    else:
        out_shape = (stats, sums, starts, turned) if first else (stats, sums)
        out_specs = (whole,) * len(out_shape)
    return pl.pallas_call(
        functools.partial(attention_kernel, head_size, parts, kind),
        out_shape=out_shape,
        in_specs=in_specs + [whole] * len(state),
        out_specs=out_specs,
        scratch_shapes=scratch,
        compiler_params=pltpu.CompilerParams(vmem_limit_bytes=32 * 1024 * 1024),
        cost_estimate=pl.CostEstimate(flops=1, bytes_accessed=1, transcendentals=0),
    )(*operands, *state)


def same_parity_blocks(block, axis):
    size = lax.axis_size(axis)
    groups = [list(range(parity, size, 2)) for parity in range(2)]
    spread = jnp.broadcast_to(block, (size // 2,) + block.shape)
    return lax.all_to_all(spread, axis, 0, 0, axis_index_groups=groups)


def exchange(piece, axis, bits):
    return lax.ppermute(piece, axis, [(i, i ^ bits) for i in range(lax.axis_size(axis))])


def halves_exchanged(piece):
    half = piece.shape[2] // 2
    return [exchange(piece[:, :, :half], "head", 1), exchange(piece[:, :, half:], "head", 1)]


def body(queries, key_rows, value_rows, document_lengths):
    seqs, rows, width = queries.shape
    heads = width // key_rows.shape[2]
    assert lax.axis_size("head") == 4 and lax.axis_size("ctx") % 2 == 0
    results = []
    for seq in range(seqs):
        run = functools.partial(attend, lengths=document_lengths[seq : seq + 1], heads=heads)
        own = same_parity_blocks(jnp.stack([key_rows[seq], value_rows[seq]]), "ctx")
        half = own.shape[2] // 2

        across = exchange(own, "ctx", 1)
        far = exchange(own, "head", 2)
        corner = exchange(own, ("ctx", "head"), lax.axis_size("head") + 2)
        near = halves_exchanged(own)
        stats, sums, starts, turned = run([(0, 0, 0)], "first", queries=queries[seq], kvs=[own], state=())
        run = functools.partial(run, queries=turned)
        stats, sums = run([(0, 1, 0), (0, 1, half)], "middle", kvs=near, state=(stats, sums, starts))

        across, far, stats, sums = lax.optimization_barrier((across, far, stats, sums))
        near = halves_exchanged(across) + halves_exchanged(far)
        stats, sums = run([(1, 0, 0), (0, 2, 0)], "middle", kvs=[across, far], state=(stats, sums, starts))
        parts = [(1, 1, 0), (1, 1, half), (0, 3, 0), (0, 3, half)]
        stats, sums = run(parts, "middle", kvs=near, state=(stats, sums, starts))
        corner, stats, sums = lax.optimization_barrier((corner, stats, sums))
        near = exchange(corner, "head", 1)
        stats, sums = run([(1, 2, 0)], "middle", kvs=[corner], state=(stats, sums, starts))
        results.append(run([(1, 3, 0)], "last", kvs=[near], state=(stats, sums, starts)))
    return jnp.stack(results)


def solution(mesh):
    in_specs = (
        P(None, "ctx", "head"),
        P(None, ("ctx", "head"), None),
        P(None, ("ctx", "head"), None),
        P(),
    )
    out_specs = P(None, "ctx", "head")
    return jax.shard_map(body, mesh=mesh, in_specs=in_specs, out_specs=out_specs, check_vma=False)
```

```python
import functools
import math

import jax
import jax.numpy as jnp
from jax import lax
from jax.experimental import pallas as pl
from jax.experimental.pallas import tpu as pltpu
from jax.sharding import PartitionSpec as P

NEG = -1e30
STEP_BLOCKS = 8


def attention_kernel(head_size, parts, kind, *refs):
    first, last = kind == "first", kind == "last"
    queries_ref, *refs = refs
    kv_refs, refs = refs[: len(parts)], refs[len(parts) :]
    blocks = kv_refs[0].shape[0]
    step_blocks = math.gcd(blocks, STEP_BLOCKS)
    lengths_ref = None
    if first or blocks > step_blocks:
        lengths_ref, *refs = refs
    if first:
        stats_ref, sums_ref, starts_ref, turned_ref = refs
        old_stats_ref, old_sums_ref = stats_ref, sums_ref
    elif last:
        old_stats_ref, old_sums_ref, starts_ref, out_ref, result_ref, sent = refs[:6]
    else:
        old_stats_ref, old_sums_ref, starts_ref, stats_ref, sums_ref = refs
    own, head_place = lax.axis_index("ctx"), lax.axis_index("head")
    heads, _, rows = old_sums_ref.shape
    piece_rows = rows // lax.axis_size("head")
    slope = math.log2(math.e) / math.sqrt(head_size)

    query_pos = own * rows + lax.broadcasted_iota(jnp.int32, (1, rows), 1)
    first_key = jnp.int32(0)
    if lengths_ref is not None:
        starts = jnp.zeros((1, rows), jnp.int32)
        end = jnp.int32(0)
        for document in range(lengths_ref.shape[1]):
            end = end + lengths_ref[0, document]
            starts = jnp.where(query_pos >= end, end, starts)
            first_key = jnp.where(own * rows >= end, end, first_key)
    else:
        starts = starts_ref[...]
    if first:
        starts_ref[...] = starts
        for head in range(heads):
            turned_ref[head] = queries_ref[:, head * head_size : (head + 1) * head_size].T
        queries_ref = turned_ref
    in_piece = lax.broadcasted_iota(jnp.int32, (piece_rows, rows), 0)

    def step(index, count, old, emit):
        here = pl.ds(index * step_blocks, count)
        keys, values = (
            jnp.concatenate([kv_ref[here, i].reshape(-1, head_size) for kv_ref in kv_refs], axis=0) for i in range(2)
        )
        values = values.T
        key_pos = []
        for kv_ref, (flip, place, skip) in zip(kv_refs, parts):
            for i in range(count):
                block = 2 * (index * step_blocks + i) + (own ^ flip) % 2
                start = block * rows + (head_place ^ place) * piece_rows + skip
                key_pos.append(start + in_piece[: kv_ref.shape[2]])
        key_pos = jnp.concatenate(key_pos, axis=0)
        valid = (key_pos >= starts) & (key_pos <= query_pos)
        scores = [
            jnp.where(valid, jnp.dot(keys, queries_ref[head], preferred_element_type=jnp.float32), NEG)
            for head in range(heads)
        ]
        for head in range(heads):
            top = jnp.max(scores[head], axis=0, keepdims=True)
            if old is not None:
                old_top, old_total, old_sums = old(head)
                top = jnp.maximum(old_top, top)
            weights = jnp.exp2((scores[head] - top) * slope)
            total = jnp.sum(weights, axis=0, keepdims=True)
            sums = jnp.dot(values, weights.astype(jnp.bfloat16), preferred_element_type=jnp.float32)
            if old is not None:
                factor = jnp.exp2((old_top - top) * slope)
                total = old_total * factor + total
                sums = old_sums * factor + sums
            emit(head, top, total, sums)

    def old_state(head):
        return old_stats_ref[head : head + 1], old_stats_ref[heads + head : heads + head + 1], old_sums_ref[head]

    def keep(head, top, total, sums):
        stats_ref[head : head + 1] = top
        stats_ref[heads + head : heads + head + 1] = total
        sums_ref[head] = sums

    def send(head):
        columns = pl.ds(head * head_size, head_size)
        return pltpu.make_async_copy(result_ref.at[:, columns], out_ref.at[:, columns], sent.at[head])

    def finish(head, top, total, sums):
        del top
        result_ref[:, head * head_size : (head + 1) * head_size] = (sums * (1.0 / total)).astype(result_ref.dtype).T
        send(head).start()

    if blocks == step_blocks:
        if first:
            step(0, blocks, None, keep)
        else:
            emit = finish if last else keep
            reach = 0
            for count in sorted({max(blocks // 4, 1), max(blocks // 2, 1), blocks}):
                pl.when((own // 2 >= reach) & (own // 2 < count))(functools.partial(step, 0, count, old_state, emit))
                reach = count
    else:
        if last:
            stats_ref, sums_ref = refs[-2:]
        if first:
            stats_ref[...] = jnp.concatenate([jnp.full((heads, rows), NEG), jnp.zeros((heads, rows))], axis=0)
            sums_ref[...] = jnp.zeros_like(sums_ref)
        else:
            stats_ref[...] = old_stats_ref[...]
            sums_ref[...] = old_sums_ref[...]

        def new_state(head):
            return stats_ref[head : head + 1], stats_ref[heads + head : heads + head + 1], sums_ref[head]

        @pl.loop(first_key // rows // 2 // step_blocks, own // 2 // step_blocks + 1)
        def _(index):
            step(index, step_blocks, new_state, keep)

        if last:
            for head in range(heads):
                finish(head, *new_state(head))
    if last:
        for head in range(heads):
            send(head).wait()


def attend(parts, kind, lengths, queries, kvs, state, heads):
    first, last = kind == "first", kind == "last"
    blocks, head_size = kvs[0].shape[0], kvs[0].shape[3]
    rows = queries.shape[0] if first else queries.shape[2]
    stats = jax.ShapeDtypeStruct((2 * heads, rows), jnp.float32)
    sums = jax.ShapeDtypeStruct((heads, head_size, rows), jnp.float32)
    starts = jax.ShapeDtypeStruct((1, rows), jnp.int32)
    turned = jax.ShapeDtypeStruct((heads, head_size, rows), queries.dtype)
    whole = pl.BlockSpec(memory_space=pltpu.VMEM)
    operands, in_specs = [queries, *kvs], [whole] * (1 + len(kvs))
    if first or blocks > math.gcd(blocks, STEP_BLOCKS):
        operands.append(lengths)
        in_specs.append(pl.BlockSpec(memory_space=pltpu.SMEM))
    scratch = []
    if last:
        out_shape = jax.ShapeDtypeStruct((rows, heads * head_size), queries.dtype)
        out_specs = pl.BlockSpec(memory_space=pl.ANY)
        scratch = [pltpu.VMEM(out_shape.shape, out_shape.dtype), pltpu.SemaphoreType.DMA((heads,))]
        if blocks > math.gcd(blocks, STEP_BLOCKS):
            scratch += [pltpu.VMEM(stats.shape, stats.dtype), pltpu.VMEM(sums.shape, sums.dtype)]
    else:
        out_shape = (stats, sums, starts, turned) if first else (stats, sums)
        out_specs = (whole,) * len(out_shape)
    return pl.pallas_call(
        functools.partial(attention_kernel, head_size, parts, kind),
        out_shape=out_shape,
        in_specs=in_specs + [whole] * len(state),
        out_specs=out_specs,
        scratch_shapes=scratch,
        compiler_params=pltpu.CompilerParams(vmem_limit_bytes=32 * 1024 * 1024),
        cost_estimate=pl.CostEstimate(flops=1, bytes_accessed=1, transcendentals=0),
    )(*operands, *state)


def same_parity_blocks(block, axis):
    size = lax.axis_size(axis)
    groups = [list(range(parity, size, 2)) for parity in range(2)]
    spread = jnp.broadcast_to(block, (size // 2,) + block.shape)
    return lax.all_to_all(spread, axis, 0, 0, axis_index_groups=groups)


def exchange(piece, axis, bits):
    return lax.ppermute(piece, axis, [(i, i ^ bits) for i in range(lax.axis_size(axis))])


def body(queries, key_rows, value_rows, document_lengths):
    seqs, rows, width = queries.shape
    heads = width // key_rows.shape[2]
    assert lax.axis_size("head") == 4 and lax.axis_size("ctx") % 2 == 0
    results = []
    for seq in range(seqs):
        run = functools.partial(attend, lengths=document_lengths[seq : seq + 1], heads=heads)
        own = same_parity_blocks(jnp.stack([key_rows[seq], value_rows[seq]]), "ctx")
        half = own.shape[2] // 2

        across = exchange(own, "ctx", 1)
        far = exchange(own, "head", 2)
        corner = exchange(own, ("ctx", "head"), lax.axis_size("head") + 2)
        near = [exchange(own[:, :, :half], "head", 1), exchange(own[:, :, half:], "head", 1)]
        stats, sums, starts, turned = run([(0, 0, 0)], "first", queries=queries[seq], kvs=[own], state=())
        run = functools.partial(run, queries=turned)
        stats, sums = run([(0, 1, 0), (0, 1, half)], "middle", kvs=near, state=(stats, sums, starts))

        across, far, stats, sums = lax.optimization_barrier((across, far, stats, sums))
        near = [exchange(across, "head", 1), exchange(far, "head", 1)]
        stats, sums = run([(1, 0, 0), (0, 2, 0)], "middle", kvs=[across, far], state=(stats, sums, starts))
        corner, stats, sums = lax.optimization_barrier((corner, stats, sums))
        near_corner = exchange(corner, "head", 1)
        parts = [(1, 1, 0), (0, 3, 0), (1, 2, 0)]
        stats, sums = run(parts, "middle", kvs=[*near, corner], state=(stats, sums, starts))
        results.append(run([(1, 3, 0)], "last", kvs=[near_corner], state=(stats, sums, starts)))
    return jnp.stack(results)


def solution(mesh):
    in_specs = (
        P(None, "ctx", "head"),
        P(None, ("ctx", "head"), None),
        P(None, ("ctx", "head"), None),
        P(),
    )
    out_specs = P(None, "ctx", "head")
    return jax.shard_map(body, mesh=mesh, in_specs=in_specs, out_specs=out_specs, check_vma=False)
```

```python
import functools
import math

import jax
import jax.numpy as jnp
from jax import lax
from jax.experimental import pallas as pl
from jax.experimental.pallas import tpu as pltpu
from jax.sharding import PartitionSpec as P

NEG = -1e30
STEP_BLOCKS = 8
DIGIT = 4


def attention_kernel(head_size, parts, kind, *refs):
    first, last = kind == "first", kind == "last"
    queries_ref, *refs = refs
    kv_refs, refs = refs[: len(parts)], refs[len(parts) :]
    blocks = kv_refs[0].shape[0]
    step_blocks = math.gcd(blocks, STEP_BLOCKS)
    lengths_ref = None
    if first or blocks > step_blocks:
        lengths_ref, *refs = refs
    if first:
        stats_ref, sums_ref, starts_ref, turned_ref = refs
        old_stats_ref, old_sums_ref = stats_ref, sums_ref
    elif last:
        old_stats_ref, old_sums_ref, starts_ref, out_ref, result_ref, sent = refs[:6]
    else:
        old_stats_ref, old_sums_ref, starts_ref, stats_ref, sums_ref = refs
    own, head_place = lax.axis_index("ctx"), lax.axis_index("head")
    heads, _, rows = old_sums_ref.shape
    piece_rows = rows // lax.axis_size("head")
    slope = math.log2(math.e) / math.sqrt(head_size)

    query_pos = own * rows + lax.broadcasted_iota(jnp.int32, (1, rows), 1)
    first_key = jnp.int32(0)
    if lengths_ref is not None:
        starts = jnp.zeros((1, rows), jnp.int32)
        end = jnp.int32(0)
        for document in range(lengths_ref.shape[1]):
            end = end + lengths_ref[0, document]
            starts = jnp.where(query_pos >= end, end, starts)
            first_key = jnp.where(own * rows >= end, end, first_key)
    else:
        starts = starts_ref[...]
    if first:
        starts_ref[...] = starts
        for head in range(heads):
            turned_ref[head] = queries_ref[:, head * head_size : (head + 1) * head_size].T
        queries_ref = turned_ref
    in_piece = lax.broadcasted_iota(jnp.int32, (piece_rows, rows), 0)

    def step(index, count, old, emit):
        here = pl.ds(index * step_blocks, count)
        keys, values = (
            jnp.concatenate([kv_ref[here, i].reshape(-1, head_size) for kv_ref in kv_refs], axis=0) for i in range(2)
        )
        values = values.T
        key_pos = []
        for kv_ref, (flip, place, skip) in zip(kv_refs, parts):
            for i in range(count):
                block = 2 * ((own // 2) ^ (index * step_blocks + i)) + (own ^ flip) % 2
                start = block * rows + (head_place ^ place) * piece_rows + skip
                key_pos.append(start + in_piece[: kv_ref.shape[2]])
        key_pos = jnp.concatenate(key_pos, axis=0)
        valid = (key_pos >= starts) & (key_pos <= query_pos)
        scores = [
            jnp.where(valid, jnp.dot(keys, queries_ref[head], preferred_element_type=jnp.float32), NEG)
            for head in range(heads)
        ]
        for head in range(heads):
            top = jnp.max(scores[head], axis=0, keepdims=True)
            if old is not None:
                old_top, old_total, old_sums = old(head)
                top = jnp.maximum(old_top, top)
            weights = jnp.exp2((scores[head] - top) * slope)
            total = jnp.sum(weights, axis=0, keepdims=True)
            sums = jnp.dot(values, weights.astype(jnp.bfloat16), preferred_element_type=jnp.float32)
            if old is not None:
                factor = jnp.exp2((old_top - top) * slope)
                total = old_total * factor + total
                sums = old_sums * factor + sums
            emit(head, top, total, sums)

    def old_state(head):
        return old_stats_ref[head : head + 1], old_stats_ref[heads + head : heads + head + 1], old_sums_ref[head]

    def keep(head, top, total, sums):
        stats_ref[head : head + 1] = top
        stats_ref[heads + head : heads + head + 1] = total
        sums_ref[head] = sums

    def send(head):
        columns = pl.ds(head * head_size, head_size)
        return pltpu.make_async_copy(result_ref.at[:, columns], out_ref.at[:, columns], sent.at[head])

    def finish(head, top, total, sums):
        del top
        result_ref[:, head * head_size : (head + 1) * head_size] = (sums * (1.0 / total)).astype(result_ref.dtype).T
        send(head).start()

    if blocks == step_blocks:
        if first:
            step(0, blocks, None, keep)
        else:
            emit = finish if last else keep
            reach = 0
            for count in sorted({max(blocks // 4, 1), max(blocks // 2, 1), blocks}):
                pl.when((own // 2 >= reach) & (own // 2 < count))(functools.partial(step, 0, count, old_state, emit))
                reach = count
    else:
        if last:
            stats_ref, sums_ref = refs[-2:]
        if first:
            stats_ref[...] = jnp.concatenate([jnp.full((heads, rows), NEG), jnp.zeros((heads, rows))], axis=0)
            sums_ref[...] = jnp.zeros_like(sums_ref)
        else:
            stats_ref[...] = old_stats_ref[...]
            sums_ref[...] = old_sums_ref[...]

        def new_state(head):
            return stats_ref[head : head + 1], stats_ref[heads + head : heads + head + 1], sums_ref[head]

        @pl.loop(0, blocks // step_blocks)
        def _(index):
            group = (own // 2 // step_blocks) ^ index
            needed = (group <= own // 2 // step_blocks) & (group >= first_key // rows // 2 // step_blocks)
            pl.when(needed)(lambda: step(index, step_blocks, new_state, keep))

        if last:
            for head in range(heads):
                finish(head, *new_state(head))
    if last:
        for head in range(heads):
            send(head).wait()


def attend(parts, kind, lengths, queries, kvs, state, heads):
    first, last = kind == "first", kind == "last"
    blocks, head_size = kvs[0].shape[0], kvs[0].shape[3]
    rows = queries.shape[0] if first else queries.shape[2]
    stats = jax.ShapeDtypeStruct((2 * heads, rows), jnp.float32)
    sums = jax.ShapeDtypeStruct((heads, head_size, rows), jnp.float32)
    starts = jax.ShapeDtypeStruct((1, rows), jnp.int32)
    turned = jax.ShapeDtypeStruct((heads, head_size, rows), queries.dtype)
    whole = pl.BlockSpec(memory_space=pltpu.VMEM)
    operands, in_specs = [queries, *kvs], [whole] * (1 + len(kvs))
    if first or blocks > math.gcd(blocks, STEP_BLOCKS):
        operands.append(lengths)
        in_specs.append(pl.BlockSpec(memory_space=pltpu.SMEM))
    scratch = []
    if last:
        out_shape = jax.ShapeDtypeStruct((rows, heads * head_size), queries.dtype)
        out_specs = pl.BlockSpec(memory_space=pl.ANY)
        scratch = [pltpu.VMEM(out_shape.shape, out_shape.dtype), pltpu.SemaphoreType.DMA((heads,))]
        if blocks > math.gcd(blocks, STEP_BLOCKS):
            scratch += [pltpu.VMEM(stats.shape, stats.dtype), pltpu.VMEM(sums.shape, sums.dtype)]
    else:
        out_shape = (stats, sums, starts, turned) if first else (stats, sums)
        out_specs = (whole,) * len(out_shape)
    return pl.pallas_call(
        functools.partial(attention_kernel, head_size, parts, kind),
        out_shape=out_shape,
        in_specs=in_specs + [whole] * len(state),
        out_specs=out_specs,
        scratch_shapes=scratch,
        compiler_params=pltpu.CompilerParams(vmem_limit_bytes=32 * 1024 * 1024),
        cost_estimate=pl.CostEstimate(flops=1, bytes_accessed=1, transcendentals=0),
    )(*operands, *state)


def exchange(piece, axis, bits):
    return lax.ppermute(piece, axis, [(i, i ^ bits) for i in range(lax.axis_size(axis))])


def same_parity_blocks(block, axis):
    pairs = lax.axis_size(axis) // 2
    held = block[None]
    while (count := held.shape[0]) < pairs:
        digits = range(1, min(DIGIT, pairs // count))
        held = jnp.concatenate([held] + [exchange(held, axis, 2 * digit * count) for digit in digits])
    return held


def body(queries, key_rows, value_rows, document_lengths):
    seqs, rows, width = queries.shape
    heads = width // key_rows.shape[2]
    assert lax.axis_size("head") == 4 and lax.axis_size("ctx") % 2 == 0
    results = []
    for seq in range(seqs):
        run = functools.partial(attend, lengths=document_lengths[seq : seq + 1], heads=heads)
        own = same_parity_blocks(jnp.stack([key_rows[seq], value_rows[seq]]), "ctx")
        half = own.shape[2] // 2

        across = exchange(own, "ctx", 1)
        far = exchange(own, "head", 2)
        corner = exchange(own, ("ctx", "head"), lax.axis_size("head") + 2)
        near = [exchange(own[:, :, :half], "head", 1), exchange(own[:, :, half:], "head", 1)]
        stats, sums, starts, turned = run([(0, 0, 0)], "first", queries=queries[seq], kvs=[own], state=())
        run = functools.partial(run, queries=turned)
        stats, sums = run([(0, 1, 0), (0, 1, half)], "middle", kvs=near, state=(stats, sums, starts))

        across, far, stats, sums = lax.optimization_barrier((across, far, stats, sums))
        near = [exchange(across, "head", 1), exchange(far, "head", 1)]
        stats, sums = run([(1, 0, 0), (0, 2, 0)], "middle", kvs=[across, far], state=(stats, sums, starts))
        corner, stats, sums = lax.optimization_barrier((corner, stats, sums))
        near_corner = exchange(corner, "head", 1)
        parts = [(1, 1, 0), (0, 3, 0), (1, 2, 0)]
        stats, sums = run(parts, "middle", kvs=[*near, corner], state=(stats, sums, starts))
        results.append(run([(1, 3, 0)], "last", kvs=[near_corner], state=(stats, sums, starts)))
    return jnp.stack(results)


def solution(mesh):
    in_specs = (
        P(None, "ctx", "head"),
        P(None, ("ctx", "head"), None),
        P(None, ("ctx", "head"), None),
        P(),
    )
    out_specs = P(None, "ctx", "head")
    return jax.shard_map(body, mesh=mesh, in_specs=in_specs, out_specs=out_specs, check_vma=False)
```

```python
import functools
import math

import jax
import jax.numpy as jnp
from jax import lax
from jax.experimental import pallas as pl
from jax.experimental.pallas import tpu as pltpu
from jax.sharding import PartitionSpec as P

NEG = -1e30
STEP_BLOCKS = 8
DIGIT = 4
ORDER = (2, 3, 1)


def attention_kernel(head_size, parts, kind, *refs):
    first, last = kind == "first", kind == "last"
    queries_ref, *refs = refs
    kv_refs, refs = refs[: len(parts)], refs[len(parts) :]
    blocks = kv_refs[0].shape[0]
    step_blocks = math.gcd(blocks, STEP_BLOCKS)
    lengths_ref = None
    if first or blocks > step_blocks:
        lengths_ref, *refs = refs
    if first:
        stats_ref, sums_ref, starts_ref, turned_ref = refs
        old_stats_ref, old_sums_ref = stats_ref, sums_ref
    elif last:
        old_stats_ref, old_sums_ref, starts_ref, out_ref, result_ref, sent = refs[:6]
    else:
        old_stats_ref, old_sums_ref, starts_ref, stats_ref, sums_ref = refs
    own, head_place = lax.axis_index("ctx"), lax.axis_index("head")
    heads, _, rows = old_sums_ref.shape
    piece_rows = rows // lax.axis_size("head")
    slope = math.log2(math.e) / math.sqrt(head_size)

    query_pos = own * rows + lax.broadcasted_iota(jnp.int32, (1, rows), 1)
    first_key = jnp.int32(0)
    if lengths_ref is not None:
        starts = jnp.zeros((1, rows), jnp.int32)
        end = jnp.int32(0)
        for document in range(lengths_ref.shape[1]):
            end = end + lengths_ref[0, document]
            starts = jnp.where(query_pos >= end, end, starts)
            first_key = jnp.where(own * rows >= end, end, first_key)
    else:
        starts = starts_ref[...]
    if first:
        starts_ref[...] = starts
        for head in range(heads):
            turned_ref[head] = queries_ref[:, head * head_size : (head + 1) * head_size].T
        queries_ref = turned_ref
    in_piece = lax.broadcasted_iota(jnp.int32, (piece_rows, rows), 0)

    def step(index, count, old, emit):
        here = pl.ds(index * step_blocks, count)
        keys, values = (
            jnp.concatenate([kv_ref[here, i].reshape(-1, head_size) for kv_ref in kv_refs], axis=0) for i in range(2)
        )
        values = values.T
        key_pos = []
        for kv_ref, (flip, place, skip) in zip(kv_refs, parts):
            for i in range(count):
                block = 2 * ((own // 2) ^ (index * step_blocks + i)) + (own ^ flip) % 2
                start = block * rows + (head_place ^ place) * piece_rows + skip
                key_pos.append(start + in_piece[: kv_ref.shape[2]])
        key_pos = jnp.concatenate(key_pos, axis=0)
        valid = (key_pos >= starts) & (key_pos <= query_pos)
        scores = [
            jnp.where(valid, jnp.dot(keys, queries_ref[head], preferred_element_type=jnp.float32), NEG)
            for head in range(heads)
        ]
        for head in range(heads):
            top = jnp.max(scores[head], axis=0, keepdims=True)
            if old is not None:
                old_top, old_total, old_sums = old(head)
                top = jnp.maximum(old_top, top)
            weights = jnp.exp2((scores[head] - top) * slope)
            total = jnp.sum(weights, axis=0, keepdims=True)
            sums = jnp.dot(values, weights.astype(jnp.bfloat16), preferred_element_type=jnp.float32)
            if old is not None:
                factor = jnp.exp2((old_top - top) * slope)
                total = old_total * factor + total
                sums = old_sums * factor + sums
            emit(head, top, total, sums)

    def old_state(head):
        return old_stats_ref[head : head + 1], old_stats_ref[heads + head : heads + head + 1], old_sums_ref[head]

    def keep(head, top, total, sums):
        stats_ref[head : head + 1] = top
        stats_ref[heads + head : heads + head + 1] = total
        sums_ref[head] = sums

    def send(head):
        columns = pl.ds(head * head_size, head_size)
        return pltpu.make_async_copy(result_ref.at[:, columns], out_ref.at[:, columns], sent.at[head])

    def finish(head, top, total, sums):
        del top
        result_ref[:, head * head_size : (head + 1) * head_size] = (sums * (1.0 / total)).astype(result_ref.dtype).T
        send(head).start()

    if blocks == step_blocks:
        if first:
            step(0, blocks, None, keep)
        else:
            emit = finish if last else keep
            reach = 0
            for count in sorted({max(blocks // 4, 1), max(blocks // 2, 1), blocks}):
                pl.when((own // 2 >= reach) & (own // 2 < count))(functools.partial(step, 0, count, old_state, emit))
                reach = count
    else:
        if last:
            stats_ref, sums_ref = refs[-2:]
        if first:
            stats_ref[...] = jnp.concatenate([jnp.full((heads, rows), NEG), jnp.zeros((heads, rows))], axis=0)
            sums_ref[...] = jnp.zeros_like(sums_ref)
        else:
            stats_ref[...] = old_stats_ref[...]
            sums_ref[...] = old_sums_ref[...]

        def new_state(head):
            return stats_ref[head : head + 1], stats_ref[heads + head : heads + head + 1], sums_ref[head]

        @pl.loop(0, blocks // step_blocks)
        def _(index):
            group = (own // 2 // step_blocks) ^ index
            needed = (group <= own // 2 // step_blocks) & (group >= first_key // rows // 2 // step_blocks)
            pl.when(needed)(lambda: step(index, step_blocks, new_state, keep))

        if last:
            for head in range(heads):
                finish(head, *new_state(head))
    if last:
        for head in range(heads):
            send(head).wait()


def attend(parts, kind, lengths, queries, kvs, state, heads):
    first, last = kind == "first", kind == "last"
    blocks, head_size = kvs[0].shape[0], kvs[0].shape[3]
    rows = queries.shape[0] if first else queries.shape[2]
    stats = jax.ShapeDtypeStruct((2 * heads, rows), jnp.float32)
    sums = jax.ShapeDtypeStruct((heads, head_size, rows), jnp.float32)
    starts = jax.ShapeDtypeStruct((1, rows), jnp.int32)
    turned = jax.ShapeDtypeStruct((heads, head_size, rows), queries.dtype)
    whole = pl.BlockSpec(memory_space=pltpu.VMEM)
    operands, in_specs = [queries, *kvs], [whole] * (1 + len(kvs))
    if first or blocks > math.gcd(blocks, STEP_BLOCKS):
        operands.append(lengths)
        in_specs.append(pl.BlockSpec(memory_space=pltpu.SMEM))
    scratch = []
    if last:
        out_shape = jax.ShapeDtypeStruct((rows, heads * head_size), queries.dtype)
        out_specs = pl.BlockSpec(memory_space=pl.ANY)
        scratch = [pltpu.VMEM(out_shape.shape, out_shape.dtype), pltpu.SemaphoreType.DMA((heads,))]
        if blocks > math.gcd(blocks, STEP_BLOCKS):
            scratch += [pltpu.VMEM(stats.shape, stats.dtype), pltpu.VMEM(sums.shape, sums.dtype)]
    else:
        out_shape = (stats, sums, starts, turned) if first else (stats, sums)
        out_specs = (whole,) * len(out_shape)
    return pl.pallas_call(
        functools.partial(attention_kernel, head_size, parts, kind),
        out_shape=out_shape,
        in_specs=in_specs + [whole] * len(state),
        out_specs=out_specs,
        scratch_shapes=scratch,
        compiler_params=pltpu.CompilerParams(vmem_limit_bytes=32 * 1024 * 1024),
        cost_estimate=pl.CostEstimate(flops=1, bytes_accessed=1, transcendentals=0),
    )(*operands, *state)


def exchange(piece, axis, bits):
    return lax.ppermute(piece, axis, [(i, i ^ bits) for i in range(lax.axis_size(axis))])


def same_parity_blocks(block, axis):
    pairs = lax.axis_size(axis) // 2
    held = block[None]
    while (count := held.shape[0]) < pairs:
        digits = sorted(range(1, min(DIGIT, pairs // count)), key=lambda digit: ORDER.index(digit))
        moved = lax.optimization_barrier([exchange(held, axis, 2 * digit * count) for digit in digits])
        moved = dict(zip(digits, moved))
        held = jnp.concatenate([held] + [moved[digit] for digit in sorted(digits)])
    return held


def body(queries, key_rows, value_rows, document_lengths):
    seqs, rows, width = queries.shape
    heads = width // key_rows.shape[2]
    assert lax.axis_size("head") == 4 and lax.axis_size("ctx") % 2 == 0
    results = []
    for seq in range(seqs):
        run = functools.partial(attend, lengths=document_lengths[seq : seq + 1], heads=heads)
        own = same_parity_blocks(jnp.stack([key_rows[seq], value_rows[seq]]), "ctx")
        half = own.shape[2] // 2

        across = exchange(own, "ctx", 1)
        far = exchange(own, "head", 2)
        corner = exchange(own, ("ctx", "head"), lax.axis_size("head") + 2)
        near = [exchange(own[:, :, :half], "head", 1), exchange(own[:, :, half:], "head", 1)]
        stats, sums, starts, turned = run([(0, 0, 0)], "first", queries=queries[seq], kvs=[own], state=())
        run = functools.partial(run, queries=turned)
        stats, sums = run([(0, 1, 0), (0, 1, half)], "middle", kvs=near, state=(stats, sums, starts))

        across, far, stats, sums = lax.optimization_barrier((across, far, stats, sums))
        near = [exchange(across, "head", 1), exchange(far, "head", 1)]
        stats, sums = run([(1, 0, 0), (0, 2, 0)], "middle", kvs=[across, far], state=(stats, sums, starts))
        corner, stats, sums = lax.optimization_barrier((corner, stats, sums))
        near_corner = exchange(corner, "head", 1)
        parts = [(1, 1, 0), (0, 3, 0), (1, 2, 0)]
        stats, sums = run(parts, "middle", kvs=[*near, corner], state=(stats, sums, starts))
        results.append(run([(1, 3, 0)], "last", kvs=[near_corner], state=(stats, sums, starts)))
    return jnp.stack(results)


def solution(mesh):
    in_specs = (
        P(None, "ctx", "head"),
        P(None, ("ctx", "head"), None),
        P(None, ("ctx", "head"), None),
        P(),
    )
    out_specs = P(None, "ctx", "head")
    return jax.shard_map(body, mesh=mesh, in_specs=in_specs, out_specs=out_specs, check_vma=False)
```

```python
import functools
import math

import jax
import jax.numpy as jnp
from jax import lax
from jax.experimental import pallas as pl
from jax.experimental.pallas import tpu as pltpu
from jax.sharding import PartitionSpec as P

NEG = -1e30
STEP_BLOCKS = 8
DIGIT = 4
ORDER = (2, 3, 1)


def attention_kernel(head_size, parts, kind, *refs):
    first, last = kind == "first", kind == "last"
    queries_ref, *refs = refs
    kv_refs, refs = refs[: len(parts)], refs[len(parts) :]
    blocks = kv_refs[0].shape[0]
    step_blocks = math.gcd(blocks, STEP_BLOCKS)
    lengths_ref = None
    if first or blocks > step_blocks:
        lengths_ref, *refs = refs
    if first:
        stats_ref, sums_ref, starts_ref, turned_ref = refs
        old_stats_ref, old_sums_ref = stats_ref, sums_ref
    elif last:
        old_stats_ref, old_sums_ref, starts_ref, out_ref, result_ref, sent = refs[:6]
    else:
        old_stats_ref, old_sums_ref, starts_ref, stats_ref, sums_ref = refs
    own, head_place = lax.axis_index("ctx"), lax.axis_index("head")
    heads, _, rows = old_sums_ref.shape
    piece_rows = rows // lax.axis_size("head")
    slope = math.log2(math.e) / math.sqrt(head_size)

    query_pos = own * rows + lax.broadcasted_iota(jnp.int32, (1, rows), 1)
    first_key = jnp.int32(0)
    if lengths_ref is not None:
        starts = jnp.zeros((1, rows), jnp.int32)
        end = jnp.int32(0)
        for document in range(lengths_ref.shape[1]):
            end = end + lengths_ref[0, document]
            starts = jnp.where(query_pos >= end, end, starts)
            first_key = jnp.where(own * rows >= end, end, first_key)
    else:
        starts = starts_ref[...]
    if first:
        starts_ref[...] = starts
        for head in range(heads):
            turned_ref[head] = queries_ref[:, head * head_size : (head + 1) * head_size].T
        queries_ref = turned_ref
    in_piece = lax.broadcasted_iota(jnp.int32, (piece_rows, rows), 0)

    def step(index, count, old, emit):
        here = pl.ds(index * step_blocks, count)
        keys, values = (
            jnp.concatenate([kv_ref[here, i].reshape(-1, head_size) for kv_ref in kv_refs], axis=0) for i in range(2)
        )
        values = values.T
        key_pos = []
        for kv_ref, (flip, place, skip) in zip(kv_refs, parts):
            for i in range(count):
                block = 2 * ((own // 2) ^ (index * step_blocks + i)) + (own ^ flip) % 2
                start = block * rows + (head_place ^ place) * piece_rows + skip
                key_pos.append(start + in_piece[: kv_ref.shape[2]])
        key_pos = jnp.concatenate(key_pos, axis=0)
        valid = (key_pos >= starts) & (key_pos <= query_pos)
        scores = [
            jnp.where(valid, jnp.dot(keys, queries_ref[head], preferred_element_type=jnp.float32), NEG)
            for head in range(heads)
        ]
        for head in range(heads):
            top = jnp.max(scores[head], axis=0, keepdims=True)
            if old is not None:
                old_top, old_total, old_sums = old(head)
                top = jnp.maximum(old_top, top)
            weights = jnp.exp2((scores[head] - top) * slope)
            total = jnp.sum(weights, axis=0, keepdims=True)
            sums = jnp.dot(values, weights.astype(jnp.bfloat16), preferred_element_type=jnp.float32)
            if old is not None:
                factor = jnp.exp2((old_top - top) * slope)
                total = old_total * factor + total
                sums = old_sums * factor + sums
            emit(head, top, total, sums)

    def old_state(head):
        return old_stats_ref[head : head + 1], old_stats_ref[heads + head : heads + head + 1], old_sums_ref[head]

    def keep(head, top, total, sums):
        stats_ref[head : head + 1] = top
        stats_ref[heads + head : heads + head + 1] = total
        sums_ref[head] = sums

    def send(head):
        columns = pl.ds(head * head_size, head_size)
        return pltpu.make_async_copy(result_ref.at[:, columns], out_ref.at[:, columns], sent.at[head])

    def finish(head, top, total, sums):
        del top
        result_ref[:, head * head_size : (head + 1) * head_size] = (sums * (1.0 / total)).astype(result_ref.dtype).T
        send(head).start()

    if blocks == step_blocks:
        if first:
            step(0, blocks, None, keep)
        else:
            emit = finish if last else keep
            reach = 0
            for count in sorted({max(blocks // 4, 1), max(blocks // 2, 1), blocks}):
                pl.when((own // 2 >= reach) & (own // 2 < count))(functools.partial(step, 0, count, old_state, emit))
                reach = count
    else:
        if last:
            stats_ref, sums_ref = refs[-2:]
        if first:
            stats_ref[...] = jnp.concatenate([jnp.full((heads, rows), NEG), jnp.zeros((heads, rows))], axis=0)
            sums_ref[...] = jnp.zeros_like(sums_ref)
        else:
            stats_ref[...] = old_stats_ref[...]
            sums_ref[...] = old_sums_ref[...]

        def new_state(head):
            return stats_ref[head : head + 1], stats_ref[heads + head : heads + head + 1], sums_ref[head]

        @pl.loop(0, blocks // step_blocks)
        def _(index):
            group = (own // 2 // step_blocks) ^ index
            needed = (group <= own // 2 // step_blocks) & (group >= first_key // rows // 2 // step_blocks)
            pl.when(needed)(lambda: step(index, step_blocks, new_state, keep))

        if last:
            for head in range(heads):
                finish(head, *new_state(head))
    if last:
        for head in range(heads):
            send(head).wait()


def attend(parts, kind, lengths, queries, kvs, state, heads):
    first, last = kind == "first", kind == "last"
    blocks, head_size = kvs[0].shape[0], kvs[0].shape[3]
    rows = queries.shape[0] if first else queries.shape[2]
    stats = jax.ShapeDtypeStruct((2 * heads, rows), jnp.float32)
    sums = jax.ShapeDtypeStruct((heads, head_size, rows), jnp.float32)
    starts = jax.ShapeDtypeStruct((1, rows), jnp.int32)
    turned = jax.ShapeDtypeStruct((heads, head_size, rows), queries.dtype)
    whole = pl.BlockSpec(memory_space=pltpu.VMEM)
    operands, in_specs = [queries, *kvs], [whole] * (1 + len(kvs))
    if first or blocks > math.gcd(blocks, STEP_BLOCKS):
        operands.append(lengths)
        in_specs.append(pl.BlockSpec(memory_space=pltpu.SMEM))
    scratch = []
    if last:
        out_shape = jax.ShapeDtypeStruct((rows, heads * head_size), queries.dtype)
        out_specs = pl.BlockSpec(memory_space=pl.ANY)
        scratch = [pltpu.VMEM(out_shape.shape, out_shape.dtype), pltpu.SemaphoreType.DMA((heads,))]
        if blocks > math.gcd(blocks, STEP_BLOCKS):
            scratch += [pltpu.VMEM(stats.shape, stats.dtype), pltpu.VMEM(sums.shape, sums.dtype)]
    else:
        out_shape = (stats, sums, starts, turned) if first else (stats, sums)
        out_specs = (whole,) * len(out_shape)
    return pl.pallas_call(
        functools.partial(attention_kernel, head_size, parts, kind),
        out_shape=out_shape,
        in_specs=in_specs + [whole] * len(state),
        out_specs=out_specs,
        scratch_shapes=scratch,
        compiler_params=pltpu.CompilerParams(vmem_limit_bytes=32 * 1024 * 1024),
        cost_estimate=pl.CostEstimate(flops=1, bytes_accessed=1, transcendentals=0),
    )(*operands, *state)


def exchange(piece, axis, bits):
    return lax.ppermute(piece, axis, [(i, i ^ bits) for i in range(lax.axis_size(axis))])


def same_parity_blocks(block, axis):
    pairs = lax.axis_size(axis) // 2
    held = block[None]
    while (count := held.shape[0]) < pairs:
        digits = sorted(range(1, min(DIGIT, pairs // count)), key=lambda digit: ORDER.index(digit))
        moved = []
        for digit in digits:
            targets = [(i, i ^ (2 * digit * count)) for i in range(lax.axis_size(axis))]
            targets = [(i, j) for i, j in targets if j // (2 * count) % DIGIT]
            moved.append(lax.ppermute(held, axis, targets))
        moved = dict(zip(digits, lax.optimization_barrier(moved)))
        held = jnp.concatenate([held] + [moved[digit] for digit in sorted(digits)])
    return held


def body(queries, key_rows, value_rows, document_lengths):
    seqs, rows, width = queries.shape
    heads = width // key_rows.shape[2]
    assert lax.axis_size("head") == 4 and lax.axis_size("ctx") % 2 == 0
    results = []
    for seq in range(seqs):
        run = functools.partial(attend, lengths=document_lengths[seq : seq + 1], heads=heads)
        own = same_parity_blocks(jnp.stack([key_rows[seq], value_rows[seq]]), "ctx")
        half = own.shape[2] // 2

        across = exchange(own, "ctx", 1)
        far = exchange(own, "head", 2)
        corner = exchange(own, ("ctx", "head"), lax.axis_size("head") + 2)
        near = [exchange(own[:, :, :half], "head", 1), exchange(own[:, :, half:], "head", 1)]
        stats, sums, starts, turned = run([(0, 0, 0)], "first", queries=queries[seq], kvs=[own], state=())
        run = functools.partial(run, queries=turned)
        stats, sums = run([(0, 1, 0), (0, 1, half)], "middle", kvs=near, state=(stats, sums, starts))

        across, far, stats, sums = lax.optimization_barrier((across, far, stats, sums))
        near = [exchange(across, "head", 1), exchange(far, "head", 1)]
        stats, sums = run([(1, 0, 0), (0, 2, 0)], "middle", kvs=[across, far], state=(stats, sums, starts))
        corner, stats, sums = lax.optimization_barrier((corner, stats, sums))
        near_corner = exchange(corner, "head", 1)
        parts = [(1, 1, 0), (0, 3, 0), (1, 2, 0)]
        stats, sums = run(parts, "middle", kvs=[*near, corner], state=(stats, sums, starts))
        results.append(run([(1, 3, 0)], "last", kvs=[near_corner], state=(stats, sums, starts)))
    return jnp.stack(results)


def solution(mesh):
    in_specs = (
        P(None, "ctx", "head"),
        P(None, ("ctx", "head"), None),
        P(None, ("ctx", "head"), None),
        P(),
    )
    out_specs = P(None, "ctx", "head")
    return jax.shard_map(body, mesh=mesh, in_specs=in_specs, out_specs=out_specs, check_vma=False)
```

```python
import functools
import math

import jax
import jax.numpy as jnp
from jax import lax
from jax.experimental import pallas as pl
from jax.experimental.pallas import tpu as pltpu
from jax.sharding import PartitionSpec as P

NEG = -1e30
STEP_BLOCKS = 8
DIGIT = 4
ORDER = (2, 3, 1)


def attention_kernel(head_size, parts, kind, *refs):
    first, last = kind == "first", kind == "last"
    queries_ref, *refs = refs
    kv_refs, refs = refs[: len(parts)], refs[len(parts) :]
    blocks = kv_refs[0].shape[0]
    step_blocks = math.gcd(blocks, STEP_BLOCKS)
    lengths_ref = None
    if first or blocks > step_blocks:
        lengths_ref, *refs = refs
    if first:
        stats_ref, sums_ref, starts_ref, turned_ref = refs
        old_stats_ref, old_sums_ref = stats_ref, sums_ref
    elif last:
        old_stats_ref, old_sums_ref, starts_ref, out_ref, result_ref, sent = refs[:6]
    else:
        old_stats_ref, old_sums_ref, starts_ref, stats_ref, sums_ref = refs
    own, head_place = lax.axis_index("ctx"), lax.axis_index("head")
    heads, _, rows = old_sums_ref.shape
    piece_rows = rows // lax.axis_size("head")
    slope = math.log2(math.e) / math.sqrt(head_size)

    query_pos = own * rows + lax.broadcasted_iota(jnp.int32, (1, rows), 1)
    first_key = jnp.int32(0)
    if lengths_ref is not None:
        starts = jnp.zeros((1, rows), jnp.int32)
        end = jnp.int32(0)
        for document in range(lengths_ref.shape[1]):
            end = end + lengths_ref[0, document]
            starts = jnp.where(query_pos >= end, end, starts)
            first_key = jnp.where(own * rows >= end, end, first_key)
    else:
        starts = starts_ref[...]
    if first:
        starts_ref[...] = starts
        for head in range(heads):
            turned_ref[head] = queries_ref[:, head * head_size : (head + 1) * head_size].T
        queries_ref = turned_ref
    in_piece = lax.broadcasted_iota(jnp.int32, (piece_rows, rows), 0)

    def step(index, count, old, emit):
        here = pl.ds(index * step_blocks, count)
        keys, values = (
            jnp.concatenate([kv_ref[here, i].reshape(-1, head_size) for kv_ref in kv_refs], axis=0) for i in range(2)
        )
        values = values.T
        key_pos = []
        for kv_ref, (flip, place, skip) in zip(kv_refs, parts):
            for i in range(count):
                block = 2 * ((own // 2) ^ (index * step_blocks + i)) + (own ^ flip) % 2
                start = block * rows + (head_place ^ place) * piece_rows + skip
                key_pos.append(start + in_piece[: kv_ref.shape[2]])
        key_pos = jnp.concatenate(key_pos, axis=0)
        valid = (key_pos >= starts) & (key_pos <= query_pos)
        scores = [
            jnp.where(valid, jnp.dot(keys, queries_ref[head], preferred_element_type=jnp.float32), NEG)
            for head in range(heads)
        ]
        for head in range(heads):
            top = jnp.max(scores[head], axis=0, keepdims=True)
            if old is not None:
                old_top, old_total, old_sums = old(head)
                top = jnp.maximum(old_top, top)
            weights = jnp.exp2((scores[head] - top) * slope)
            total = jnp.sum(weights, axis=0, keepdims=True)
            sums = jnp.dot(values, weights.astype(jnp.bfloat16), preferred_element_type=jnp.float32)
            if old is not None:
                factor = jnp.exp2((old_top - top) * slope)
                total = old_total * factor + total
                sums = old_sums * factor + sums
            emit(head, top, total, sums)

    def old_state(head):
        return old_stats_ref[head : head + 1], old_stats_ref[heads + head : heads + head + 1], old_sums_ref[head]

    def keep(head, top, total, sums):
        stats_ref[head : head + 1] = top
        stats_ref[heads + head : heads + head + 1] = total
        sums_ref[head] = sums

    def send(head):
        columns = pl.ds(head * head_size, head_size)
        return pltpu.make_async_copy(result_ref.at[:, columns], out_ref.at[:, columns], sent.at[head])

    def finish(head, top, total, sums):
        del top
        result_ref[:, head * head_size : (head + 1) * head_size] = (sums * (1.0 / total)).astype(result_ref.dtype).T
        send(head).start()

    if blocks == step_blocks:
        if first:
            step(0, blocks, None, keep)
        else:
            emit = finish if last else keep
            reach = 0
            for count in sorted({max(blocks // 4, 1), max(blocks // 2, 1), blocks}):
                pl.when((own // 2 >= reach) & (own // 2 < count))(functools.partial(step, 0, count, old_state, emit))
                reach = count
    else:
        if last:
            stats_ref, sums_ref = refs[-2:]
        if first:
            stats_ref[...] = jnp.concatenate([jnp.full((heads, rows), NEG), jnp.zeros((heads, rows))], axis=0)
            sums_ref[...] = jnp.zeros_like(sums_ref)
        else:
            stats_ref[...] = old_stats_ref[...]
            sums_ref[...] = old_sums_ref[...]

        def new_state(head):
            return stats_ref[head : head + 1], stats_ref[heads + head : heads + head + 1], sums_ref[head]

        @pl.loop(0, blocks // step_blocks)
        def _(index):
            group = (own // 2 // step_blocks) ^ index
            needed = (group <= own // 2 // step_blocks) & (group >= first_key // rows // 2 // step_blocks)
            pl.when(needed)(lambda: step(index, step_blocks, new_state, keep))

        if last:
            for head in range(heads):
                finish(head, *new_state(head))
    if last:
        for head in range(heads):
            send(head).wait()


def attend(parts, kind, lengths, queries, kvs, state, heads):
    first, last = kind == "first", kind == "last"
    blocks, head_size = kvs[0].shape[0], kvs[0].shape[3]
    rows = queries.shape[0] if first else queries.shape[2]
    stats = jax.ShapeDtypeStruct((2 * heads, rows), jnp.float32)
    sums = jax.ShapeDtypeStruct((heads, head_size, rows), jnp.float32)
    starts = jax.ShapeDtypeStruct((1, rows), jnp.int32)
    turned = jax.ShapeDtypeStruct((heads, head_size, rows), queries.dtype)
    whole = pl.BlockSpec(memory_space=pltpu.VMEM)
    operands, in_specs = [queries, *kvs], [whole] * (1 + len(kvs))
    if first or blocks > math.gcd(blocks, STEP_BLOCKS):
        operands.append(lengths)
        in_specs.append(pl.BlockSpec(memory_space=pltpu.SMEM))
    scratch = []
    if last:
        out_shape = jax.ShapeDtypeStruct((rows, heads * head_size), queries.dtype)
        out_specs = pl.BlockSpec(memory_space=pl.ANY)
        scratch = [pltpu.VMEM(out_shape.shape, out_shape.dtype), pltpu.SemaphoreType.DMA((heads,))]
        if blocks > math.gcd(blocks, STEP_BLOCKS):
            scratch += [pltpu.VMEM(stats.shape, stats.dtype), pltpu.VMEM(sums.shape, sums.dtype)]
    else:
        out_shape = (stats, sums, starts, turned) if first else (stats, sums)
        out_specs = (whole,) * len(out_shape)
    return pl.pallas_call(
        functools.partial(attention_kernel, head_size, parts, kind),
        out_shape=out_shape,
        in_specs=in_specs + [whole] * len(state),
        out_specs=out_specs,
        scratch_shapes=scratch,
        compiler_params=pltpu.CompilerParams(vmem_limit_bytes=32 * 1024 * 1024),
        cost_estimate=pl.CostEstimate(flops=1, bytes_accessed=1, transcendentals=0),
    )(*operands, *state)


def exchange(piece, axis, bits):
    return lax.ppermute(piece, axis, [(i, i ^ bits) for i in range(lax.axis_size(axis))])


def same_parity_blocks(block, axis):
    pairs = lax.axis_size(axis) // 2
    held = block[None]
    while (count := held.shape[0]) < pairs:
        digits = sorted(range(1, min(DIGIT, pairs // count)), key=lambda digit: ORDER.index(digit))
        moved = lax.optimization_barrier([exchange(held, axis, 2 * digit * count) for digit in digits])
        moved = dict(zip(digits, moved))
        held = jnp.concatenate([held] + [moved[digit] for digit in sorted(digits)])
    return held


def body(queries, key_rows, value_rows, document_lengths):
    seqs, rows, width = queries.shape
    heads = width // key_rows.shape[2]
    assert lax.axis_size("head") == 4 and lax.axis_size("ctx") % 2 == 0
    results = []
    for seq in range(seqs):
        run = functools.partial(attend, lengths=document_lengths[seq : seq + 1], heads=heads)
        own = same_parity_blocks(jnp.stack([key_rows[seq], value_rows[seq]]), "ctx")
        half = own.shape[2] // 2

        across = exchange(own, "ctx", 1)
        corner = exchange(own, ("ctx", "head"), lax.axis_size("head") + 2)
        far = exchange(own, "head", 2)
        near = [exchange(own[:, :, :half], "head", 1), exchange(own[:, :, half:], "head", 1)]
        stats, sums, starts, turned = run([(0, 0, 0)], "first", queries=queries[seq], kvs=[own], state=())
        run = functools.partial(run, queries=turned)
        stats, sums = run([(0, 1, 0), (0, 1, half)], "middle", kvs=near, state=(stats, sums, starts))

        across, corner, stats, sums = lax.optimization_barrier((across, corner, stats, sums))
        near = [exchange(across, "head", 1), exchange(corner, "head", 1)]
        stats, sums = run([(1, 0, 0), (1, 2, 0)], "middle", kvs=[across, corner], state=(stats, sums, starts))
        far, stats, sums = lax.optimization_barrier((far, stats, sums))
        near_far = exchange(far, "head", 1)
        parts = [(1, 1, 0), (1, 3, 0), (0, 2, 0)]
        stats, sums = run(parts, "middle", kvs=[*near, far], state=(stats, sums, starts))
        results.append(run([(0, 3, 0)], "last", kvs=[near_far], state=(stats, sums, starts)))
    return jnp.stack(results)


def solution(mesh):
    in_specs = (
        P(None, "ctx", "head"),
        P(None, ("ctx", "head"), None),
        P(None, ("ctx", "head"), None),
        P(),
    )
    out_specs = P(None, "ctx", "head")
    return jax.shard_map(body, mesh=mesh, in_specs=in_specs, out_specs=out_specs, check_vma=False)
```

```python
import functools
import math

import jax
import jax.numpy as jnp
from jax import lax
from jax.experimental import pallas as pl
from jax.experimental.pallas import tpu as pltpu
from jax.sharding import PartitionSpec as P

NEG = -1e30
STEP_BLOCKS = 8
DIGIT = 4
ORDER = (2, 3, 1)


def attention_kernel(head_size, parts, kind, *refs):
    first, last = kind == "first", kind == "last"
    queries_ref, *refs = refs
    kv_refs, refs = refs[: len(parts)], refs[len(parts) :]
    blocks = kv_refs[0].shape[0]
    step_blocks = math.gcd(blocks, STEP_BLOCKS)
    lengths_ref = None
    if first or blocks > step_blocks:
        lengths_ref, *refs = refs
    if first:
        stats_ref, sums_ref, starts_ref, turned_ref = refs
        old_stats_ref, old_sums_ref = stats_ref, sums_ref
    elif last:
        old_stats_ref, old_sums_ref, starts_ref, out_ref, result_ref, sent = refs[:6]
    else:
        old_stats_ref, old_sums_ref, starts_ref, stats_ref, sums_ref = refs
    own, head_place = lax.axis_index("ctx"), lax.axis_index("head")
    heads, _, rows = old_sums_ref.shape
    piece_rows = rows // lax.axis_size("head")
    slope = math.log2(math.e) / math.sqrt(head_size)

    query_pos = own * rows + lax.broadcasted_iota(jnp.int32, (1, rows), 1)
    first_key = jnp.int32(0)
    if lengths_ref is not None:
        starts = jnp.zeros((1, rows), jnp.int32)
        end = jnp.int32(0)
        for document in range(lengths_ref.shape[1]):
            end = end + lengths_ref[0, document]
            starts = jnp.where(query_pos >= end, end, starts)
            first_key = jnp.where(own * rows >= end, end, first_key)
    else:
        starts = starts_ref[...]
    if first:
        starts_ref[...] = starts
        for head in range(heads):
            turned_ref[head] = queries_ref[:, head * head_size : (head + 1) * head_size].T
        queries_ref = turned_ref
    in_piece = lax.broadcasted_iota(jnp.int32, (piece_rows, rows), 0)

    def step(index, count, old, emit):
        here = pl.ds(index * step_blocks, count)
        keys, values = (
            jnp.concatenate([kv_ref[here, i].reshape(-1, head_size) for kv_ref in kv_refs], axis=0) for i in range(2)
        )
        values = values.T
        key_pos = []
        for kv_ref, (flip, place, skip) in zip(kv_refs, parts):
            for i in range(count):
                block = 2 * ((own // 2) ^ (index * step_blocks + i)) + (own ^ flip) % 2
                start = block * rows + (head_place ^ place) * piece_rows + skip
                key_pos.append(start + in_piece[: kv_ref.shape[2]])
        key_pos = jnp.concatenate(key_pos, axis=0)
        valid = (key_pos >= starts) & (key_pos <= query_pos)
        scores = [
            jnp.where(valid, jnp.dot(keys, queries_ref[head], preferred_element_type=jnp.float32), NEG)
            for head in range(heads)
        ]
        for head in range(heads):
            top = jnp.max(scores[head], axis=0, keepdims=True)
            if old is not None:
                old_top, old_total, old_sums = old(head)
                top = jnp.maximum(old_top, top)
            weights = jnp.exp2((scores[head] - top) * slope)
            total = jnp.sum(weights, axis=0, keepdims=True)
            sums = jnp.dot(values, weights.astype(jnp.bfloat16), preferred_element_type=jnp.float32)
            if old is not None:
                factor = jnp.exp2((old_top - top) * slope)
                total = old_total * factor + total
                sums = old_sums * factor + sums
            emit(head, top, total, sums)

    def old_state(head):
        return old_stats_ref[head : head + 1], old_stats_ref[heads + head : heads + head + 1], old_sums_ref[head]

    def keep(head, top, total, sums):
        stats_ref[head : head + 1] = top
        stats_ref[heads + head : heads + head + 1] = total
        sums_ref[head] = sums

    def send(head):
        columns = pl.ds(head * head_size, head_size)
        return pltpu.make_async_copy(result_ref.at[:, columns], out_ref.at[:, columns], sent.at[head])

    def finish(head, top, total, sums):
        del top
        result_ref[:, head * head_size : (head + 1) * head_size] = (sums * (1.0 / total)).astype(result_ref.dtype).T
        send(head).start()

    if blocks == step_blocks:
        if first:
            step(0, blocks, None, keep)
        else:
            emit = finish if last else keep
            reach = 0
            for count in sorted({max(blocks // 4, 1), max(blocks // 2, 1), blocks}):
                pl.when((own // 2 >= reach) & (own // 2 < count))(functools.partial(step, 0, count, old_state, emit))
                reach = count
    else:
        if last:
            stats_ref, sums_ref = refs[-2:]
        if first:
            stats_ref[...] = jnp.concatenate([jnp.full((heads, rows), NEG), jnp.zeros((heads, rows))], axis=0)
            sums_ref[...] = jnp.zeros_like(sums_ref)
        else:
            stats_ref[...] = old_stats_ref[...]
            sums_ref[...] = old_sums_ref[...]

        def new_state(head):
            return stats_ref[head : head + 1], stats_ref[heads + head : heads + head + 1], sums_ref[head]

        @pl.loop(0, blocks // step_blocks)
        def _(index):
            group = (own // 2 // step_blocks) ^ index
            needed = (group <= own // 2 // step_blocks) & (group >= first_key // rows // 2 // step_blocks)
            pl.when(needed)(lambda: step(index, step_blocks, new_state, keep))

        if last:
            for head in range(heads):
                finish(head, *new_state(head))
    if last:
        for head in range(heads):
            send(head).wait()


def attend(parts, kind, lengths, queries, kvs, state, heads):
    first, last = kind == "first", kind == "last"
    blocks, head_size = kvs[0].shape[0], kvs[0].shape[3]
    rows = queries.shape[0] if first else queries.shape[2]
    stats = jax.ShapeDtypeStruct((2 * heads, rows), jnp.float32)
    sums = jax.ShapeDtypeStruct((heads, head_size, rows), jnp.float32)
    starts = jax.ShapeDtypeStruct((1, rows), jnp.int32)
    turned = jax.ShapeDtypeStruct((heads, head_size, rows), queries.dtype)
    whole = pl.BlockSpec(memory_space=pltpu.VMEM)
    operands, in_specs = [queries, *kvs], [whole] * (1 + len(kvs))
    if first or blocks > math.gcd(blocks, STEP_BLOCKS):
        operands.append(lengths)
        in_specs.append(pl.BlockSpec(memory_space=pltpu.SMEM))
    scratch = []
    if last:
        out_shape = jax.ShapeDtypeStruct((rows, heads * head_size), queries.dtype)
        out_specs = pl.BlockSpec(memory_space=pl.ANY)
        scratch = [pltpu.VMEM(out_shape.shape, out_shape.dtype), pltpu.SemaphoreType.DMA((heads,))]
        if blocks > math.gcd(blocks, STEP_BLOCKS):
            scratch += [pltpu.VMEM(stats.shape, stats.dtype), pltpu.VMEM(sums.shape, sums.dtype)]
    else:
        out_shape = (stats, sums, starts, turned) if first else (stats, sums)
        out_specs = (whole,) * len(out_shape)
    return pl.pallas_call(
        functools.partial(attention_kernel, head_size, parts, kind),
        out_shape=out_shape,
        in_specs=in_specs + [whole] * len(state),
        out_specs=out_specs,
        scratch_shapes=scratch,
        compiler_params=pltpu.CompilerParams(vmem_limit_bytes=32 * 1024 * 1024),
        cost_estimate=pl.CostEstimate(flops=1, bytes_accessed=1, transcendentals=0),
    )(*operands, *state)


def exchange(piece, axis, bits):
    return lax.ppermute(piece, axis, [(i, i ^ bits) for i in range(lax.axis_size(axis))])


def same_parity_blocks(block, axis):
    pairs = lax.axis_size(axis) // 2
    held = block[None]
    while (count := held.shape[0]) < pairs:
        digits = sorted(range(1, min(DIGIT, pairs // count)), key=lambda digit: ORDER.index(digit))
        moved = lax.optimization_barrier([exchange(held, axis, 2 * digit * count) for digit in digits])
        moved = dict(zip(digits, moved))
        held = jnp.concatenate([held] + [moved[digit] for digit in sorted(digits)])
    return held


def body(queries, key_rows, value_rows, document_lengths):
    seqs, rows, width = queries.shape
    heads = width // key_rows.shape[2]
    assert lax.axis_size("head") == 4 and lax.axis_size("ctx") % 2 == 0
    results = []
    for seq in range(seqs):
        run = functools.partial(attend, lengths=document_lengths[seq : seq + 1], heads=heads)
        own = same_parity_blocks(jnp.stack([key_rows[seq], value_rows[seq]]), "ctx")
        half = own.shape[2] // 2

        across = exchange(own, "ctx", 1)
        far = exchange(own, "head", 2)
        corner = exchange(own, ("ctx", "head"), lax.axis_size("head") + 2)
        near = [exchange(own[:, :, :half], "head", 1), exchange(own[:, :, half:], "head", 1)]
        stats, sums, starts, turned = run([(0, 0, 0)], "first", queries=queries[seq], kvs=[own], state=())
        run = functools.partial(run, queries=turned)
        stats, sums = run([(0, 1, 0), (0, 1, half)], "middle", kvs=near, state=(stats, sums, starts))

        across, stats, sums = lax.optimization_barrier((across, stats, sums))
        stats, sums = run([(1, 0, 0)], "middle", kvs=[across], state=(stats, sums, starts))
        across, far, stats, sums = lax.optimization_barrier((across, far, stats, sums))
        near = [exchange(across, "head", 1), exchange(far, "head", 1)]
        stats, sums = run([(0, 2, 0)], "middle", kvs=[far], state=(stats, sums, starts))
        corner, stats, sums = lax.optimization_barrier((corner, stats, sums))
        near_corner = exchange(corner, "head", 1)
        parts = [(1, 1, 0), (0, 3, 0), (1, 2, 0)]
        stats, sums = run(parts, "middle", kvs=[*near, corner], state=(stats, sums, starts))
        results.append(run([(1, 3, 0)], "last", kvs=[near_corner], state=(stats, sums, starts)))
    return jnp.stack(results)


def solution(mesh):
    in_specs = (
        P(None, "ctx", "head"),
        P(None, ("ctx", "head"), None),
        P(None, ("ctx", "head"), None),
        P(),
    )
    out_specs = P(None, "ctx", "head")
    return jax.shard_map(body, mesh=mesh, in_specs=in_specs, out_specs=out_specs, check_vma=False)
```

```python
import functools
import math

import jax
import jax.numpy as jnp
from jax import lax
from jax.experimental import pallas as pl
from jax.experimental.pallas import tpu as pltpu
from jax.sharding import PartitionSpec as P

NEG = -1e30
STEP_BLOCKS = 8
DIGIT = 4
ORDER = (2, 3, 1)


def attention_kernel(head_size, parts, kind, *refs):
    first, last = kind == "first", kind == "last"
    queries_ref, *refs = refs
    kv_refs, refs = refs[: len(parts)], refs[len(parts) :]
    blocks = kv_refs[0].shape[0]
    step_blocks = math.gcd(blocks, STEP_BLOCKS)
    lengths_ref = None
    if first or blocks > step_blocks:
        lengths_ref, *refs = refs
    if first:
        stats_ref, sums_ref, starts_ref, turned_ref = refs
        old_stats_ref, old_sums_ref = stats_ref, sums_ref
    elif last:
        old_stats_ref, old_sums_ref, starts_ref, out_ref, result_ref, sent = refs[:6]
    else:
        old_stats_ref, old_sums_ref, starts_ref, stats_ref, sums_ref = refs
    own, head_place = lax.axis_index("ctx"), lax.axis_index("head")
    heads, _, rows = old_sums_ref.shape
    piece_rows = rows // lax.axis_size("head")
    slope = math.log2(math.e) / math.sqrt(head_size)

    query_pos = own * rows + lax.broadcasted_iota(jnp.int32, (1, rows), 1)
    first_key = jnp.int32(0)
    if lengths_ref is not None:
        starts = jnp.zeros((1, rows), jnp.int32)
        end = jnp.int32(0)
        for document in range(lengths_ref.shape[1]):
            end = end + lengths_ref[0, document]
            starts = jnp.where(query_pos >= end, end, starts)
            first_key = jnp.where(own * rows >= end, end, first_key)
    else:
        starts = starts_ref[...]
    if first:
        starts_ref[...] = starts
        for head in range(heads):
            turned_ref[head] = queries_ref[:, head * head_size : (head + 1) * head_size].T
        queries_ref = turned_ref
    in_piece = lax.broadcasted_iota(jnp.int32, (piece_rows, rows), 0)

    def step(index, count, old, emit):
        here = pl.ds(index * step_blocks, count)
        keys, values = (
            jnp.concatenate([kv_ref[here, i].reshape(-1, head_size) for kv_ref in kv_refs], axis=0) for i in range(2)
        )
        values = values.T
        key_pos = []
        for kv_ref, (flip, place, skip) in zip(kv_refs, parts):
            for i in range(count):
                block = 2 * ((own // 2) ^ (index * step_blocks + i)) + (own ^ flip) % 2
                start = block * rows + (head_place ^ place) * piece_rows + skip
                key_pos.append(start + in_piece[: kv_ref.shape[2]])
        key_pos = jnp.concatenate(key_pos, axis=0)
        valid = (key_pos >= starts) & (key_pos <= query_pos)
        scores = [
            jnp.where(valid, jnp.dot(keys, queries_ref[head], preferred_element_type=jnp.float32), NEG)
            for head in range(heads)
        ]
        for head in range(heads):
            top = jnp.max(scores[head], axis=0, keepdims=True)
            if old is not None:
                old_top, old_total, old_sums = old(head)
                top = jnp.maximum(old_top, top)
            weights = jnp.exp2((scores[head] - top) * slope)
            total = jnp.sum(weights, axis=0, keepdims=True)
            sums = jnp.dot(values, weights.astype(jnp.bfloat16), preferred_element_type=jnp.float32)
            if old is not None:
                factor = jnp.exp2((old_top - top) * slope)
                total = old_total * factor + total
                sums = old_sums * factor + sums
            emit(head, top, total, sums)

    def old_state(head):
        return old_stats_ref[head : head + 1], old_stats_ref[heads + head : heads + head + 1], old_sums_ref[head]

    def keep(head, top, total, sums):
        stats_ref[head : head + 1] = top
        stats_ref[heads + head : heads + head + 1] = total
        sums_ref[head] = sums

    def send(head):
        columns = pl.ds(head * head_size, head_size)
        return pltpu.make_async_copy(result_ref.at[:, columns], out_ref.at[:, columns], sent.at[head])

    def finish(head, top, total, sums):
        del top
        result_ref[:, head * head_size : (head + 1) * head_size] = (sums * (1.0 / total)).astype(result_ref.dtype).T
        send(head).start()

    if blocks == step_blocks:
        if first:
            step(0, blocks, None, keep)
        else:
            emit = finish if last else keep
            reach = 0
            for count in sorted({max(blocks // 4, 1), max(blocks // 2, 1), blocks}):
                pl.when((own // 2 >= reach) & (own // 2 < count))(functools.partial(step, 0, count, old_state, emit))
                reach = count
    else:
        if last:
            stats_ref, sums_ref = refs[-2:]
        if first:
            stats_ref[...] = jnp.concatenate([jnp.full((heads, rows), NEG), jnp.zeros((heads, rows))], axis=0)
            sums_ref[...] = jnp.zeros_like(sums_ref)
        else:
            stats_ref[...] = old_stats_ref[...]
            sums_ref[...] = old_sums_ref[...]

        def new_state(head):
            return stats_ref[head : head + 1], stats_ref[heads + head : heads + head + 1], sums_ref[head]

        @pl.loop(0, blocks // step_blocks)
        def _(index):
            group = (own // 2 // step_blocks) ^ index
            needed = (group <= own // 2 // step_blocks) & (group >= first_key // rows // 2 // step_blocks)
            pl.when(needed)(lambda: step(index, step_blocks, new_state, keep))

        if last:
            for head in range(heads):
                finish(head, *new_state(head))
    if last:
        for head in range(heads):
            send(head).wait()


def attend(parts, kind, lengths, queries, kvs, state, heads):
    first, last = kind == "first", kind == "last"
    blocks, head_size = kvs[0].shape[0], kvs[0].shape[3]
    rows = queries.shape[0] if first else queries.shape[2]
    stats = jax.ShapeDtypeStruct((2 * heads, rows), jnp.float32)
    sums = jax.ShapeDtypeStruct((heads, head_size, rows), jnp.float32)
    starts = jax.ShapeDtypeStruct((1, rows), jnp.int32)
    turned = jax.ShapeDtypeStruct((heads, head_size, rows), queries.dtype)
    whole = pl.BlockSpec(memory_space=pltpu.VMEM)
    operands, in_specs = [queries, *kvs], [whole] * (1 + len(kvs))
    if first or blocks > math.gcd(blocks, STEP_BLOCKS):
        operands.append(lengths)
        in_specs.append(pl.BlockSpec(memory_space=pltpu.SMEM))
    scratch = []
    if last:
        out_shape = jax.ShapeDtypeStruct((rows, heads * head_size), queries.dtype)
        out_specs = pl.BlockSpec(memory_space=pl.ANY)
        scratch = [pltpu.VMEM(out_shape.shape, out_shape.dtype), pltpu.SemaphoreType.DMA((heads,))]
        if blocks > math.gcd(blocks, STEP_BLOCKS):
            scratch += [pltpu.VMEM(stats.shape, stats.dtype), pltpu.VMEM(sums.shape, sums.dtype)]
    else:
        out_shape = (stats, sums, starts, turned) if first else (stats, sums)
        out_specs = (whole,) * len(out_shape)
    return pl.pallas_call(
        functools.partial(attention_kernel, head_size, parts, kind),
        out_shape=out_shape,
        in_specs=in_specs + [whole] * len(state),
        out_specs=out_specs,
        scratch_shapes=scratch,
        compiler_params=pltpu.CompilerParams(vmem_limit_bytes=32 * 1024 * 1024),
        cost_estimate=pl.CostEstimate(flops=1, bytes_accessed=1, transcendentals=0),
    )(*operands, *state)


def exchange(piece, axis, bits):
    return lax.ppermute(piece, axis, [(i, i ^ bits) for i in range(lax.axis_size(axis))])


def same_parity_blocks(block, axis):
    pairs = lax.axis_size(axis) // 2
    held = block[None]
    while (count := held.shape[0]) < pairs:
        digits = sorted(range(1, min(DIGIT, pairs // count)), key=lambda digit: ORDER.index(digit))
        moved = []
        for digit in digits:
            to = [source ^ digit for source in range(DIGIT)]
            if digit == 3 and count * DIGIT == pairs:
                to = [3, 2, 0, 1]
            sources = range(lax.axis_size(axis))
            place = [i // (2 * count) % DIGIT for i in sources]
            targets = [(i, i ^ (2 * count * (place[i] ^ to[place[i]]))) for i in sources]
            moved.append(lax.ppermute(held, axis, targets))
        moved = lax.optimization_barrier(moved)
        moved = dict(zip(digits, moved))
        held = jnp.concatenate([held] + [moved[digit] for digit in sorted(digits)])
    return held


def body(queries, key_rows, value_rows, document_lengths):
    seqs, rows, width = queries.shape
    heads = width // key_rows.shape[2]
    assert lax.axis_size("head") == 4 and lax.axis_size("ctx") % 2 == 0
    results = []
    for seq in range(seqs):
        run = functools.partial(attend, lengths=document_lengths[seq : seq + 1], heads=heads)
        own = same_parity_blocks(jnp.stack([key_rows[seq], value_rows[seq]]), "ctx")
        half = own.shape[2] // 2

        across = exchange(own, "ctx", 1)
        far = exchange(own, "head", 2)
        corner = exchange(own, ("ctx", "head"), lax.axis_size("head") + 2)
        near = [exchange(own[:, :, :half], "head", 1), exchange(own[:, :, half:], "head", 1)]
        stats, sums, starts, turned = run([(0, 0, 0)], "first", queries=queries[seq], kvs=[own], state=())
        run = functools.partial(run, queries=turned)
        stats, sums = run([(0, 1, 0), (0, 1, half)], "middle", kvs=near, state=(stats, sums, starts))

        across, stats, sums = lax.optimization_barrier((across, stats, sums))
        stats, sums = run([(1, 0, 0)], "middle", kvs=[across], state=(stats, sums, starts))
        across, far, stats, sums = lax.optimization_barrier((across, far, stats, sums))
        near = [exchange(across, "head", 1), exchange(far, "head", 1)]
        stats, sums = run([(0, 2, 0)], "middle", kvs=[far], state=(stats, sums, starts))
        corner, stats, sums = lax.optimization_barrier((corner, stats, sums))
        near_corner = exchange(corner, "head", 1)
        parts = [(1, 1, 0), (0, 3, 0), (1, 2, 0)]
        stats, sums = run(parts, "middle", kvs=[*near, corner], state=(stats, sums, starts))
        results.append(run([(1, 3, 0)], "last", kvs=[near_corner], state=(stats, sums, starts)))
    return jnp.stack(results)


def solution(mesh):
    in_specs = (
        P(None, "ctx", "head"),
        P(None, ("ctx", "head"), None),
        P(None, ("ctx", "head"), None),
        P(),
    )
    out_specs = P(None, "ctx", "head")
    return jax.shard_map(body, mesh=mesh, in_specs=in_specs, out_specs=out_specs, check_vma=False)
```

```python
import functools
import math

import jax
import jax.numpy as jnp
from jax import lax
from jax.experimental import pallas as pl
from jax.experimental.pallas import tpu as pltpu
from jax.sharding import PartitionSpec as P

NEG = -1e30
STEP_BLOCKS = 8
DIGIT = 4
ORDER = (2, 3, 1)


def attention_kernel(head_size, parts, kind, *refs):
    first, last = kind == "first", kind == "last"
    queries_ref, *refs = refs
    kv_refs, refs = refs[: len(parts)], refs[len(parts) :]
    blocks = kv_refs[0].shape[0]
    step_blocks = math.gcd(blocks, STEP_BLOCKS)
    lengths_ref = None
    if first or blocks > step_blocks:
        lengths_ref, *refs = refs
    if first:
        stats_ref, sums_ref, starts_ref, turned_ref = refs
        old_stats_ref, old_sums_ref = stats_ref, sums_ref
    elif last:
        old_stats_ref, old_sums_ref, starts_ref, out_ref, result_ref, sent = refs[:6]
    else:
        old_stats_ref, old_sums_ref, starts_ref, stats_ref, sums_ref = refs
    own, head_place = lax.axis_index("ctx"), lax.axis_index("head")
    heads, _, rows = old_sums_ref.shape
    piece_rows = rows // lax.axis_size("head")
    slope = math.log2(math.e) / math.sqrt(head_size)

    query_pos = own * rows + lax.broadcasted_iota(jnp.int32, (1, rows), 1)
    first_key = jnp.int32(0)
    if lengths_ref is not None:
        starts = jnp.zeros((1, rows), jnp.int32)
        end = jnp.int32(0)
        for document in range(lengths_ref.shape[1]):
            end = end + lengths_ref[0, document]
            starts = jnp.where(query_pos >= end, end, starts)
            first_key = jnp.where(own * rows >= end, end, first_key)
    else:
        starts = starts_ref[...]
    if first:
        starts_ref[...] = starts
        for head in range(heads):
            turned_ref[head] = queries_ref[:, head * head_size : (head + 1) * head_size].T
        queries_ref = turned_ref
    in_piece = lax.broadcasted_iota(jnp.int32, (piece_rows, rows), 0)

    def step(index, count, old, emit):
        here = pl.ds(index * step_blocks, count)
        keys, values = (
            jnp.concatenate([kv_ref[here, i].reshape(-1, head_size) for kv_ref in kv_refs], axis=0) for i in range(2)
        )
        values = values.T
        key_pos = []
        for kv_ref, (flip, place, skip) in zip(kv_refs, parts):
            for i in range(count):
                block = 2 * ((own // 2) ^ (index * step_blocks + i)) + (own ^ flip) % 2
                start = block * rows + (head_place ^ place) * piece_rows + skip
                key_pos.append(start + in_piece[: kv_ref.shape[2]])
        key_pos = jnp.concatenate(key_pos, axis=0)
        valid = (key_pos >= starts) & (key_pos <= query_pos)
        scores = [
            jnp.where(valid, jnp.dot(keys, queries_ref[head], preferred_element_type=jnp.float32), NEG)
            for head in range(heads)
        ]
        for head in range(heads):
            top = jnp.max(scores[head], axis=0, keepdims=True)
            if old is not None:
                old_top, old_total, old_sums = old(head)
                top = jnp.maximum(old_top, top)
            weights = jnp.exp2((scores[head] - top) * slope)
            total = jnp.sum(weights, axis=0, keepdims=True)
            sums = jnp.dot(values, weights.astype(jnp.bfloat16), preferred_element_type=jnp.float32)
            if old is not None:
                factor = jnp.exp2((old_top - top) * slope)
                total = old_total * factor + total
                sums = old_sums * factor + sums
            emit(head, top, total, sums)

    def old_state(head):
        return old_stats_ref[head : head + 1], old_stats_ref[heads + head : heads + head + 1], old_sums_ref[head]

    def keep(head, top, total, sums):
        stats_ref[head : head + 1] = top
        stats_ref[heads + head : heads + head + 1] = total
        sums_ref[head] = sums

    def send(head):
        columns = pl.ds(head * head_size, head_size)
        return pltpu.make_async_copy(result_ref.at[:, columns], out_ref.at[:, columns], sent.at[head])

    def finish(head, top, total, sums):
        del top
        result_ref[:, head * head_size : (head + 1) * head_size] = (sums * (1.0 / total)).astype(result_ref.dtype).T
        send(head).start()

    if blocks == step_blocks:
        if first:
            step(0, blocks, None, keep)
        else:
            emit = finish if last else keep
            reach = 0
            for count in sorted({max(blocks // 4, 1), max(blocks // 2, 1), blocks}):
                pl.when((own // 2 >= reach) & (own // 2 < count))(functools.partial(step, 0, count, old_state, emit))
                reach = count
    else:
        if last:
            stats_ref, sums_ref = refs[-2:]
        if first:
            stats_ref[...] = jnp.concatenate([jnp.full((heads, rows), NEG), jnp.zeros((heads, rows))], axis=0)
            sums_ref[...] = jnp.zeros_like(sums_ref)
        else:
            stats_ref[...] = old_stats_ref[...]
            sums_ref[...] = old_sums_ref[...]

        def new_state(head):
            return stats_ref[head : head + 1], stats_ref[heads + head : heads + head + 1], sums_ref[head]

        @pl.loop(0, blocks // step_blocks)
        def _(index):
            group = (own // 2 // step_blocks) ^ index
            needed = (group <= own // 2 // step_blocks) & (group >= first_key // rows // 2 // step_blocks)
            pl.when(needed)(lambda: step(index, step_blocks, new_state, keep))

        if last:
            for head in range(heads):
                finish(head, *new_state(head))
    if last:
        for head in range(heads):
            send(head).wait()


def attend(parts, kind, lengths, queries, kvs, state, heads):
    first, last = kind == "first", kind == "last"
    blocks, head_size = kvs[0].shape[0], kvs[0].shape[3]
    rows = queries.shape[0] if first else queries.shape[2]
    stats = jax.ShapeDtypeStruct((2 * heads, rows), jnp.float32)
    sums = jax.ShapeDtypeStruct((heads, head_size, rows), jnp.float32)
    starts = jax.ShapeDtypeStruct((1, rows), jnp.int32)
    turned = jax.ShapeDtypeStruct((heads, head_size, rows), queries.dtype)
    whole = pl.BlockSpec(memory_space=pltpu.VMEM)
    operands, in_specs = [queries, *kvs], [whole] * (1 + len(kvs))
    if first or blocks > math.gcd(blocks, STEP_BLOCKS):
        operands.append(lengths)
        in_specs.append(pl.BlockSpec(memory_space=pltpu.SMEM))
    scratch = []
    if last:
        out_shape = jax.ShapeDtypeStruct((rows, heads * head_size), queries.dtype)
        out_specs = pl.BlockSpec(memory_space=pl.ANY)
        scratch = [pltpu.VMEM(out_shape.shape, out_shape.dtype), pltpu.SemaphoreType.DMA((heads,))]
        if blocks > math.gcd(blocks, STEP_BLOCKS):
            scratch += [pltpu.VMEM(stats.shape, stats.dtype), pltpu.VMEM(sums.shape, sums.dtype)]
    else:
        out_shape = (stats, sums, starts, turned) if first else (stats, sums)
        out_specs = (whole,) * len(out_shape)
    return pl.pallas_call(
        functools.partial(attention_kernel, head_size, parts, kind),
        out_shape=out_shape,
        in_specs=in_specs + [whole] * len(state),
        out_specs=out_specs,
        scratch_shapes=scratch,
        compiler_params=pltpu.CompilerParams(vmem_limit_bytes=32 * 1024 * 1024),
        cost_estimate=pl.CostEstimate(flops=1, bytes_accessed=1, transcendentals=0),
    )(*operands, *state)


def exchange(piece, axis, bits):
    return lax.ppermute(piece, axis, [(i, i ^ bits) for i in range(lax.axis_size(axis))])


def same_parity_blocks(block, axis):
    pairs = lax.axis_size(axis) // 2
    held = block[None]
    while (count := held.shape[0]) < pairs:
        digits = sorted(range(1, min(DIGIT, pairs // count)), key=lambda digit: ORDER.index(digit))
        moved = []
        for digit in digits:
            to = [source ^ digit for source in range(DIGIT)]
            if digit == 3 and count * DIGIT == pairs:
                to = [3, 2, 0, 1]
            sources = range(lax.axis_size(axis))
            place = [i // (2 * count) % DIGIT for i in sources]
            targets = [(i, i ^ (2 * count * (place[i] ^ to[place[i]]))) for i in sources]
            moved.append(lax.ppermute(held, axis, targets))
        moved = lax.optimization_barrier(moved)
        moved = dict(zip(digits, moved))
        held = jnp.concatenate([held] + [moved[digit] for digit in sorted(digits)])
    return held


def body(queries, key_rows, value_rows, document_lengths):
    seqs, rows, width = queries.shape
    heads = width // key_rows.shape[2]
    assert lax.axis_size("head") == 4 and lax.axis_size("ctx") % 2 == 0
    results = []
    for seq in range(seqs):
        run = functools.partial(attend, lengths=document_lengths[seq : seq + 1], heads=heads)
        own = same_parity_blocks(jnp.stack([key_rows[seq], value_rows[seq]]), "ctx")
        half = own.shape[2] // 2

        across = exchange(own, "ctx", 1)
        far = exchange(own, "head", 2)
        corner = exchange(own, ("ctx", "head"), lax.axis_size("head") + 2)
        stats, sums, starts, turned = run([(0, 0, 0)], "first", queries=queries[seq], kvs=[own], state=())
        run = functools.partial(run, queries=turned)

        across, stats, sums, held = lax.optimization_barrier((across, stats, sums, own))
        near = [exchange(piece[:, :, rows], "head", 1) for piece in (held, across) for rows in (slice(half), slice(half, None))]
        stats, sums = run([(1, 0, 0)], "middle", kvs=[across], state=(stats, sums, starts))
        parts = [(0, 1, 0), (0, 1, half), (1, 1, 0), (1, 1, half)]
        stats, sums = run(parts, "middle", kvs=near, state=(stats, sums, starts))
        far, stats, sums = lax.optimization_barrier((far, stats, sums))
        near_far = exchange(far, "head", 1)
        stats, sums = run([(0, 2, 0)], "middle", kvs=[far], state=(stats, sums, starts))
        corner, stats, sums = lax.optimization_barrier((corner, stats, sums))
        near_corner = exchange(corner, "head", 1)
        stats, sums = run([(0, 3, 0), (1, 2, 0)], "middle", kvs=[near_far, corner], state=(stats, sums, starts))
        results.append(run([(1, 3, 0)], "last", kvs=[near_corner], state=(stats, sums, starts)))
    return jnp.stack(results)


def solution(mesh):
    in_specs = (
        P(None, "ctx", "head"),
        P(None, ("ctx", "head"), None),
        P(None, ("ctx", "head"), None),
        P(),
    )
    out_specs = P(None, "ctx", "head")
    return jax.shard_map(body, mesh=mesh, in_specs=in_specs, out_specs=out_specs, check_vma=False)
```

```python
import functools
import math

import jax
import jax.numpy as jnp
from jax import lax
from jax.experimental import pallas as pl
from jax.experimental.pallas import tpu as pltpu
from jax.sharding import PartitionSpec as P

NEG = -1e30
STEP_BLOCKS = 8
DIGIT = 4
ORDER = (2, 3, 1)


def attention_kernel(head_size, parts, kind, *refs):
    first, last = kind == "first", kind == "last"
    queries_ref, *refs = refs
    kv_refs, refs = refs[: len(parts)], refs[len(parts) :]
    blocks = kv_refs[0].shape[0]
    step_blocks = math.gcd(blocks, STEP_BLOCKS)
    lengths_ref = None
    if first or blocks > step_blocks:
        lengths_ref, *refs = refs
    if first:
        stats_ref, sums_ref, starts_ref, turned_ref = refs
        old_stats_ref, old_sums_ref = stats_ref, sums_ref
    elif last:
        old_stats_ref, old_sums_ref, starts_ref, out_ref, result_ref, sent = refs[:6]
    else:
        old_stats_ref, old_sums_ref, starts_ref, stats_ref, sums_ref = refs
    own, head_place = lax.axis_index("ctx"), lax.axis_index("head")
    heads, _, rows = old_sums_ref.shape
    piece_rows = rows // lax.axis_size("head")
    slope = math.log2(math.e) / math.sqrt(head_size)

    query_pos = own * rows + lax.broadcasted_iota(jnp.int32, (1, rows), 1)
    first_key = jnp.int32(0)
    if lengths_ref is not None:
        starts = jnp.zeros((1, rows), jnp.int32)
        end = jnp.int32(0)
        for document in range(lengths_ref.shape[1]):
            end = end + lengths_ref[0, document]
            starts = jnp.where(query_pos >= end, end, starts)
            first_key = jnp.where(own * rows >= end, end, first_key)
    else:
        starts = starts_ref[...]
    if first:
        starts_ref[...] = starts
        for head in range(heads):
            turned_ref[head] = queries_ref[:, head * head_size : (head + 1) * head_size].T
        queries_ref = turned_ref
    in_piece = lax.broadcasted_iota(jnp.int32, (piece_rows, rows), 0)

    def step(index, count, old, emit):
        here = pl.ds(index * step_blocks, count)
        keys, values = (
            jnp.concatenate([kv_ref[here, i].reshape(-1, head_size) for kv_ref in kv_refs], axis=0) for i in range(2)
        )
        values = values.T
        key_pos = []
        for kv_ref, (flip, place, skip) in zip(kv_refs, parts):
            for i in range(count):
                block = 2 * ((own // 2) ^ (index * step_blocks + i)) + (own ^ flip) % 2
                start = block * rows + (head_place ^ place) * piece_rows + skip
                key_pos.append(start + in_piece[: kv_ref.shape[2]])
        key_pos = jnp.concatenate(key_pos, axis=0)
        valid = (key_pos >= starts) & (key_pos <= query_pos)
        scores = [
            jnp.where(valid, jnp.dot(keys, queries_ref[head], preferred_element_type=jnp.float32), NEG)
            for head in range(heads)
        ]
        for head in range(heads):
            top = jnp.max(scores[head], axis=0, keepdims=True)
            if old is not None:
                old_top, old_total, old_sums = old(head)
                top = jnp.maximum(old_top, top)
            weights = jnp.exp2((scores[head] - top) * slope)
            total = jnp.sum(weights, axis=0, keepdims=True)
            sums = jnp.dot(values, weights.astype(jnp.bfloat16), preferred_element_type=jnp.float32)
            if old is not None:
                factor = jnp.exp2((old_top - top) * slope)
                total = old_total * factor + total
                sums = old_sums * factor + sums
            emit(head, top, total, sums)

    def old_state(head):
        return old_stats_ref[head : head + 1], old_stats_ref[heads + head : heads + head + 1], old_sums_ref[head]

    def keep(head, top, total, sums):
        stats_ref[head : head + 1] = top
        stats_ref[heads + head : heads + head + 1] = total
        sums_ref[head] = sums

    def send(head):
        columns = pl.ds(head * head_size, head_size)
        return pltpu.make_async_copy(result_ref.at[:, columns], out_ref.at[:, columns], sent.at[head])

    def finish(head, top, total, sums):
        del top
        result_ref[:, head * head_size : (head + 1) * head_size] = (sums * (1.0 / total)).astype(result_ref.dtype).T
        send(head).start()

    if blocks == step_blocks:
        if first:
            step(0, blocks, None, keep)
        else:
            emit = finish if last else keep
            reach = 0
            for count in sorted({max(blocks // 4, 1), max(blocks // 2, 1), blocks}):
                pl.when((own // 2 >= reach) & (own // 2 < count))(functools.partial(step, 0, count, old_state, emit))
                reach = count
    else:
        if last:
            stats_ref, sums_ref = refs[-2:]
        if first:
            stats_ref[...] = jnp.concatenate([jnp.full((heads, rows), NEG), jnp.zeros((heads, rows))], axis=0)
            sums_ref[...] = jnp.zeros_like(sums_ref)
        else:
            stats_ref[...] = old_stats_ref[...]
            sums_ref[...] = old_sums_ref[...]

        def new_state(head):
            return stats_ref[head : head + 1], stats_ref[heads + head : heads + head + 1], sums_ref[head]

        @pl.loop(0, blocks // step_blocks)
        def _(index):
            group = (own // 2 // step_blocks) ^ index
            needed = (group <= own // 2 // step_blocks) & (group >= first_key // rows // 2 // step_blocks)
            pl.when(needed)(lambda: step(index, step_blocks, new_state, keep))

        if last:
            for head in range(heads):
                finish(head, *new_state(head))
    if last:
        for head in range(heads):
            send(head).wait()


def attend(parts, kind, lengths, queries, kvs, state, heads):
    first, last = kind == "first", kind == "last"
    blocks, head_size = kvs[0].shape[0], kvs[0].shape[3]
    rows = queries.shape[0] if first else queries.shape[2]
    stats = jax.ShapeDtypeStruct((2 * heads, rows), jnp.float32)
    sums = jax.ShapeDtypeStruct((heads, head_size, rows), jnp.float32)
    starts = jax.ShapeDtypeStruct((1, rows), jnp.int32)
    turned = jax.ShapeDtypeStruct((heads, head_size, rows), queries.dtype)
    whole = pl.BlockSpec(memory_space=pltpu.VMEM)
    operands, in_specs = [queries, *kvs], [whole] * (1 + len(kvs))
    if first or blocks > math.gcd(blocks, STEP_BLOCKS):
        operands.append(lengths)
        in_specs.append(pl.BlockSpec(memory_space=pltpu.SMEM))
    scratch = []
    if last:
        out_shape = jax.ShapeDtypeStruct((rows, heads * head_size), queries.dtype)
        out_specs = pl.BlockSpec(memory_space=pl.ANY)
        scratch = [pltpu.VMEM(out_shape.shape, out_shape.dtype), pltpu.SemaphoreType.DMA((heads,))]
        if blocks > math.gcd(blocks, STEP_BLOCKS):
            scratch += [pltpu.VMEM(stats.shape, stats.dtype), pltpu.VMEM(sums.shape, sums.dtype)]
    else:
        out_shape = (stats, sums, starts, turned) if first else (stats, sums)
        out_specs = (whole,) * len(out_shape)
    return pl.pallas_call(
        functools.partial(attention_kernel, head_size, parts, kind),
        out_shape=out_shape,
        in_specs=in_specs + [whole] * len(state),
        out_specs=out_specs,
        scratch_shapes=scratch,
        compiler_params=pltpu.CompilerParams(vmem_limit_bytes=32 * 1024 * 1024),
        cost_estimate=pl.CostEstimate(flops=1, bytes_accessed=1, transcendentals=0),
    )(*operands, *state)


def exchange(piece, axis, bits):
    return lax.ppermute(piece, axis, [(i, i ^ bits) for i in range(lax.axis_size(axis))])


def same_parity_blocks(block, axis):
    pairs = lax.axis_size(axis) // 2
    held = block[None]
    while (count := held.shape[0]) < pairs:
        digits = sorted(range(1, min(DIGIT, pairs // count)), key=lambda digit: ORDER.index(digit))
        moved = []
        for digit in digits:
            to = [source ^ digit for source in range(DIGIT)]
            if digit == 3 and count * DIGIT == pairs:
                to = [3, 2, 0, 1]
            sources = range(lax.axis_size(axis))
            place = [i // (2 * count) % DIGIT for i in sources]
            targets = [(i, i ^ (2 * count * (place[i] ^ to[place[i]]))) for i in sources]
            moved.append(lax.ppermute(held, axis, targets))
        moved = lax.optimization_barrier(moved)
        moved = dict(zip(digits, moved))
        held = jnp.concatenate([held] + [moved[digit] for digit in sorted(digits)])
    return held


def body(queries, key_rows, value_rows, document_lengths):
    seqs, rows, width = queries.shape
    heads = width // key_rows.shape[2]
    assert lax.axis_size("head") == 4 and lax.axis_size("ctx") % 2 == 0
    results = []
    for seq in range(seqs):
        run = functools.partial(attend, lengths=document_lengths[seq : seq + 1], heads=heads)
        own = same_parity_blocks(jnp.stack([key_rows[seq], value_rows[seq]]), "ctx")
        half = own.shape[2] // 2

        across = exchange(own, "ctx", 1)
        corner = exchange(own, ("ctx", "head"), lax.axis_size("head") + 2)
        far = exchange(own, "head", 2)
        near = [exchange(own[:, :, :half], "head", 1), exchange(own[:, :, half:], "head", 1)]
        stats, sums, starts, turned = run([(0, 0, 0)], "first", queries=queries[seq], kvs=[own], state=())
        run = functools.partial(run, queries=turned)
        stats, sums = run([(0, 1, 0), (0, 1, half)], "middle", kvs=near, state=(stats, sums, starts))

        across, stats, sums = lax.optimization_barrier((across, stats, sums))
        stats, sums = run([(1, 0, 0)], "middle", kvs=[across], state=(stats, sums, starts))
        across, corner, stats, sums = lax.optimization_barrier((across, corner, stats, sums))
        near = [exchange(across, "head", 1), exchange(corner, "head", 1)]
        stats, sums = run([(1, 2, 0)], "middle", kvs=[corner], state=(stats, sums, starts))
        far, stats, sums = lax.optimization_barrier((far, stats, sums))
        near_far = exchange(far, "head", 1)
        parts = [(1, 1, 0), (1, 3, 0), (0, 2, 0)]
        stats, sums = run(parts, "middle", kvs=[*near, far], state=(stats, sums, starts))
        results.append(run([(0, 3, 0)], "last", kvs=[near_far], state=(stats, sums, starts)))
    return jnp.stack(results)


def solution(mesh):
    in_specs = (
        P(None, "ctx", "head"),
        P(None, ("ctx", "head"), None),
        P(None, ("ctx", "head"), None),
        P(),
    )
    out_specs = P(None, "ctx", "head")
    return jax.shard_map(body, mesh=mesh, in_specs=in_specs, out_specs=out_specs, check_vma=False)
```

```python
import functools
import math

import jax
import jax.numpy as jnp
from jax import lax
from jax.experimental import pallas as pl
from jax.experimental.pallas import tpu as pltpu
from jax.sharding import PartitionSpec as P

NEG = -1e30
STEP_BLOCKS = 8
DIGIT = 4
ORDER = (2, 3, 1)


def attention_kernel(head_size, parts, kind, *refs):
    first, last = kind == "first", kind == "last"
    queries_ref, *refs = refs
    kv_refs, refs = refs[: len(parts)], refs[len(parts) :]
    blocks = kv_refs[0].shape[0]
    step_blocks = math.gcd(blocks, STEP_BLOCKS)
    lengths_ref = None
    if first or blocks > step_blocks:
        lengths_ref, *refs = refs
    if first:
        stats_ref, sums_ref, starts_ref, turned_ref = refs
        old_stats_ref, old_sums_ref = stats_ref, sums_ref
    elif last:
        old_stats_ref, old_sums_ref, starts_ref, out_ref, result_ref, sent = refs[:6]
    else:
        old_stats_ref, old_sums_ref, starts_ref, stats_ref, sums_ref = refs
    own, head_place = lax.axis_index("ctx"), lax.axis_index("head")
    heads, _, rows = old_sums_ref.shape
    piece_rows = rows // lax.axis_size("head")
    slope = math.log2(math.e) / math.sqrt(head_size)

    query_pos = own * rows + lax.broadcasted_iota(jnp.int32, (1, rows), 1)
    first_key = jnp.int32(0)
    if lengths_ref is not None:
        starts = jnp.zeros((1, rows), jnp.int32)
        end = jnp.int32(0)
        for document in range(lengths_ref.shape[1]):
            end = end + lengths_ref[0, document]
            starts = jnp.where(query_pos >= end, end, starts)
            first_key = jnp.where(own * rows >= end, end, first_key)
    else:
        starts = starts_ref[...]
    if first:
        starts_ref[...] = starts
        for head in range(heads):
            turned_ref[head] = queries_ref[:, head * head_size : (head + 1) * head_size].T
        queries_ref = turned_ref
    in_piece = lax.broadcasted_iota(jnp.int32, (piece_rows, rows), 0)

    def step(index, count, old, emit):
        here = pl.ds(index * step_blocks, count)
        keys, values = (
            jnp.concatenate([kv_ref[here, i].reshape(-1, head_size) for kv_ref in kv_refs], axis=0) for i in range(2)
        )
        values = values.T
        key_pos = []
        for kv_ref, (flip, place, skip) in zip(kv_refs, parts):
            for i in range(count):
                block = 2 * ((own // 2) ^ (index * step_blocks + i)) + (own ^ flip) % 2
                start = block * rows + (head_place ^ place) * piece_rows + skip
                key_pos.append(start + in_piece[: kv_ref.shape[2]])
        key_pos = jnp.concatenate(key_pos, axis=0)
        valid = (key_pos >= starts) & (key_pos <= query_pos)
        scores = [
            jnp.where(valid, jnp.dot(keys, queries_ref[head], preferred_element_type=jnp.float32), NEG)
            for head in range(heads)
        ]
        for head in range(heads):
            top = jnp.max(scores[head], axis=0, keepdims=True)
            if old is not None:
                old_top, old_total, old_sums = old(head)
                top = jnp.maximum(old_top, top)
            weights = jnp.exp2((scores[head] - top) * slope)
            total = jnp.sum(weights, axis=0, keepdims=True)
            sums = jnp.dot(values, weights.astype(jnp.bfloat16), preferred_element_type=jnp.float32)
            if old is not None:
                factor = jnp.exp2((old_top - top) * slope)
                total = old_total * factor + total
                sums = old_sums * factor + sums
            emit(head, top, total, sums)

    def old_state(head):
        return old_stats_ref[head : head + 1], old_stats_ref[heads + head : heads + head + 1], old_sums_ref[head]

    def keep(head, top, total, sums):
        stats_ref[head : head + 1] = top
        stats_ref[heads + head : heads + head + 1] = total
        sums_ref[head] = sums

    def send(head):
        columns = pl.ds(head * head_size, head_size)
        return pltpu.make_async_copy(result_ref.at[:, columns], out_ref.at[:, columns], sent.at[head])

    def finish(head, top, total, sums):
        del top
        result_ref[:, head * head_size : (head + 1) * head_size] = (sums * (1.0 / total)).astype(result_ref.dtype).T
        send(head).start()

    if blocks == step_blocks:
        if first:
            step(0, blocks, None, keep)
        else:
            emit = finish if last else keep
            reach = 0
            for count in sorted({max(blocks // 4, 1), max(blocks // 2, 1), blocks}):
                pl.when((own // 2 >= reach) & (own // 2 < count))(functools.partial(step, 0, count, old_state, emit))
                reach = count
    else:
        if last:
            stats_ref, sums_ref = refs[-2:]
        if first:
            stats_ref[...] = jnp.concatenate([jnp.full((heads, rows), NEG), jnp.zeros((heads, rows))], axis=0)
            sums_ref[...] = jnp.zeros_like(sums_ref)
        else:
            stats_ref[...] = old_stats_ref[...]
            sums_ref[...] = old_sums_ref[...]

        def new_state(head):
            return stats_ref[head : head + 1], stats_ref[heads + head : heads + head + 1], sums_ref[head]

        @pl.loop(0, blocks // step_blocks)
        def _(index):
            group = (own // 2 // step_blocks) ^ index
            needed = (group <= own // 2 // step_blocks) & (group >= first_key // rows // 2 // step_blocks)
            pl.when(needed)(lambda: step(index, step_blocks, new_state, keep))

        if last:
            for head in range(heads):
                finish(head, *new_state(head))
    if last:
        for head in range(heads):
            send(head).wait()


def attend(parts, kind, lengths, queries, kvs, state, heads):
    first, last = kind == "first", kind == "last"
    blocks, head_size = kvs[0].shape[0], kvs[0].shape[3]
    rows = queries.shape[0] if first else queries.shape[2]
    stats = jax.ShapeDtypeStruct((2 * heads, rows), jnp.float32)
    sums = jax.ShapeDtypeStruct((heads, head_size, rows), jnp.float32)
    starts = jax.ShapeDtypeStruct((1, rows), jnp.int32)
    turned = jax.ShapeDtypeStruct((heads, head_size, rows), queries.dtype)
    whole = pl.BlockSpec(memory_space=pltpu.VMEM)
    operands, in_specs = [queries, *kvs], [whole] * (1 + len(kvs))
    if first or blocks > math.gcd(blocks, STEP_BLOCKS):
        operands.append(lengths)
        in_specs.append(pl.BlockSpec(memory_space=pltpu.SMEM))
    scratch = []
    if last:
        out_shape = jax.ShapeDtypeStruct((rows, heads * head_size), queries.dtype)
        out_specs = pl.BlockSpec(memory_space=pl.ANY)
        scratch = [pltpu.VMEM(out_shape.shape, out_shape.dtype), pltpu.SemaphoreType.DMA((heads,))]
        if blocks > math.gcd(blocks, STEP_BLOCKS):
            scratch += [pltpu.VMEM(stats.shape, stats.dtype), pltpu.VMEM(sums.shape, sums.dtype)]
    else:
        out_shape = (stats, sums, starts, turned) if first else (stats, sums)
        out_specs = (whole,) * len(out_shape)
    return pl.pallas_call(
        functools.partial(attention_kernel, head_size, parts, kind),
        out_shape=out_shape,
        in_specs=in_specs + [whole] * len(state),
        out_specs=out_specs,
        scratch_shapes=scratch,
        compiler_params=pltpu.CompilerParams(vmem_limit_bytes=32 * 1024 * 1024),
        cost_estimate=pl.CostEstimate(flops=1, bytes_accessed=1, transcendentals=0),
    )(*operands, *state)


def exchange(piece, axis, bits):
    return lax.ppermute(piece, axis, [(i, i ^ bits) for i in range(lax.axis_size(axis))])


def same_parity_blocks(block, axis):
    pairs = lax.axis_size(axis) // 2
    held = block[None]
    while (count := held.shape[0]) < pairs:
        digits = sorted(range(1, min(DIGIT, pairs // count)), key=lambda digit: ORDER.index(digit))
        moved = []
        for digit in digits:
            to = [source ^ digit for source in range(DIGIT)]
            if digit == 3 and count * DIGIT == pairs:
                to = [3, 2, 0, 1]
            sources = range(lax.axis_size(axis))
            place = [i // (2 * count) % DIGIT for i in sources]
            targets = [(i, i ^ (2 * count * (place[i] ^ to[place[i]]))) for i in sources]
            moved.append(lax.ppermute(held, axis, targets))
        moved = lax.optimization_barrier(moved)
        moved = dict(zip(digits, moved))
        held = jnp.concatenate([held] + [moved[digit] for digit in sorted(digits)])
    return held


def body(queries, key_rows, value_rows, document_lengths):
    seqs, rows, width = queries.shape
    heads = width // key_rows.shape[2]
    assert lax.axis_size("head") == 4 and lax.axis_size("ctx") % 2 == 0
    results = []
    for seq in range(seqs):
        run = functools.partial(attend, lengths=document_lengths[seq : seq + 1], heads=heads)
        own = same_parity_blocks(jnp.stack([key_rows[seq], value_rows[seq]]), "ctx")
        half = own.shape[2] // 2

        corner = exchange(own, ("ctx", "head"), lax.axis_size("head") + 2)
        across = exchange(own, "ctx", 1)
        far = exchange(own, "head", 2)
        near = [exchange(own[:, :, :half], "head", 1), exchange(own[:, :, half:], "head", 1)]
        stats, sums, starts, turned = run([(0, 0, 0)], "first", queries=queries[seq], kvs=[own], state=())
        run = functools.partial(run, queries=turned)
        stats, sums = run([(0, 1, 0), (0, 1, half)], "middle", kvs=near, state=(stats, sums, starts))

        across, stats, sums = lax.optimization_barrier((across, stats, sums))
        stats, sums = run([(1, 0, 0)], "middle", kvs=[across], state=(stats, sums, starts))
        corner, across, stats, sums = lax.optimization_barrier((corner, across, stats, sums))
        near = [exchange(across, "head", 1), exchange(corner, "head", 1)]
        stats, sums = run([(1, 2, 0)], "middle", kvs=[corner], state=(stats, sums, starts))
        far, stats, sums = lax.optimization_barrier((far, stats, sums))
        near_far = exchange(far, "head", 1)
        parts = [(1, 1, 0), (1, 3, 0), (0, 2, 0)]
        stats, sums = run(parts, "middle", kvs=[*near, far], state=(stats, sums, starts))
        results.append(run([(0, 3, 0)], "last", kvs=[near_far], state=(stats, sums, starts)))
    return jnp.stack(results)


def solution(mesh):
    in_specs = (
        P(None, "ctx", "head"),
        P(None, ("ctx", "head"), None),
        P(None, ("ctx", "head"), None),
        P(),
    )
    out_specs = P(None, "ctx", "head")
    return jax.shard_map(body, mesh=mesh, in_specs=in_specs, out_specs=out_specs, check_vma=False)
```
